32 devices in a mesh: pages: 8 (over z, x), mp: 4 (over y, core).
Axes of the slice: x: 2, y: 2, z: 4, core: 2. Of those that a mesh axis runs over, the one named last changes fastest.
Arguments:
- queries: bfloat16 [256, 8192], P('pages', 'mp'), may hold values from -9 to 9
- cached_keys: bfloat16 [128, 128, 8, 128], P('pages', None, 'mp'), may hold values from -8 to 8
- cached_values: bfloat16 [128, 128, 8, 128], P('pages', None, 'mp'), may hold values from -4 to 4
- out_weight: bfloat16 [8192, 8192], P('mp', 'pages'), may hold values from -0.0625 to 0.0625
- select: int32 [2, 24], replicated, may hold values from 0 to 127, as said below
- page_table: int32 [128], replicated, may hold values from 0 to 127, as said below
- block_page: int32 [2], replicated, may hold values from 0 to 127, as said below
Outputs:
- mixed: bfloat16 [256, 8192], P('mp', 'pages')
The draws below stay inside these ranges and needn't reach their ends.
Inputs may be any that keep to these rules, and one draw needn't show every extreme that they name: A permutation: each logical page has its own cache row, held by index page_table[p] // 16 of pages. `select`: each row holds 24 distinct pages: the block's own page block_page[b] and pages lying wholly before the block. They lie on exactly 4 owners, 6 on each. No owner holds selected pages of more than min(2, 4) blocks, and some owner holds that many. `block_page`: Distinct.
All inputs are finite; a program needn't handle non-finite values.
Results may differ from the reference program's by a relative error of at most 0.0063.
Values may be sent and summed in bfloat16 or wider, within the bound.
No kernel may reach another device: no remote copies, remote signals or barrier semaphores. Data moves between devices by JAX's collectives and lax.ppermute only.
A program may use at most 64 MiB of HBM per device.

```python
import jax
import jax.numpy as jnp
from jax import lax

D = 8192
QUERY_HEADS = 64
KEY_VALUE_HEADS = 8
HEAD_SIZE = 128
PAGE_TOKENS = 128
PAGES_PER_INDEX = 16
PICKED_PAGES = 6
OWNERS_SEL = 4
QBLOCKS = 2
CACHE_PAGES = 128
N_PAGES = 8


def page_layout(key):
    owners = N_PAGES
    early = PAGES_PER_INDEX * 7 // 8
    late = PAGES_PER_INDEX - early
    perm_early = jax.random.permutation(jax.random.fold_in(key, 11), owners * early).astype(jnp.int32)
    slot_early = perm_early // early * PAGES_PER_INDEX + perm_early % early
    perm_late = jax.random.permutation(jax.random.fold_in(key, 12), owners * late).astype(jnp.int32)
    slot_late = perm_late // late * PAGES_PER_INDEX + early + perm_late % late
    table = jnp.concatenate([slot_early, slot_late]).astype(jnp.int32)
    inverse = jnp.argsort(table, stable=True).astype(jnp.int32)
    span = min(QBLOCKS + 2, owners)
    half_owners = owners // 2
    base = jax.random.permutation(jax.random.fold_in(key, 13), half_owners)[:span // 2].astype(jnp.int32)
    pool = jnp.stack([base, base + half_owners], axis=1).reshape(-1).astype(jnp.int32)
    position = (jnp.arange(QBLOCKS, dtype=jnp.int32)[:, None] + jnp.arange(OWNERS_SEL, dtype=jnp.int32)[None, :]) % span
    owner_ids = pool[position]
    own_late = jax.random.randint(jax.random.fold_in(key, 14), (QBLOCKS,), 0, late, dtype=jnp.int32)
    block_page = inverse[owner_ids[:, 0] * PAGES_PER_INDEX + early + own_late]
    scores = jax.random.randint(jax.random.fold_in(key, 15), (QBLOCKS, OWNERS_SEL, early), 0, 1 << 20, dtype=jnp.int32) * early + jnp.arange(early, dtype=jnp.int32)
    picks = jnp.argsort(scores, axis=-1, stable=True)[..., :PICKED_PAGES].astype(jnp.int32)
    early_pages = inverse[owner_ids[..., None] * PAGES_PER_INDEX + picks]
    chosen = jnp.concatenate([block_page[:, None], early_pages[:, 0, 1:], early_pages[:, 1:].reshape(QBLOCKS, -1)], axis=1)
    width = OWNERS_SEL * PICKED_PAGES
    mixing = jax.random.randint(jax.random.fold_in(key, 16), (QBLOCKS, width), 0, 1 << 20, dtype=jnp.int32) * width + jnp.arange(width, dtype=jnp.int32)
    shuffle = jnp.argsort(mixing, axis=-1, stable=True)
    chosen = jnp.take_along_axis(chosen, shuffle, axis=1)
    return (table, chosen.astype(jnp.int32), block_page.astype(jnp.int32))


def draw_page_table(key, part):
    return page_layout(key)[0]


def draw_select(key, part):
    return page_layout(key)[1]


def draw_block_page(key, part):
    return page_layout(key)[2]


def draw_queries(key, part):
    count = QBLOCKS * PAGE_TOKENS
    base = jnp.clip(jax.random.normal(jax.random.fold_in(key, 1), (count, QUERY_HEADS, HEAD_SIZE), jnp.float32), -4.0, 4.0)
    return base.reshape(count, QUERY_HEADS * HEAD_SIZE).astype(jnp.bfloat16)


def draw_cached_keys(key, part):
    array_shape = (PAGES_PER_INDEX * N_PAGES, PAGE_TOKENS, KEY_VALUE_HEADS, HEAD_SIZE)
    base = jnp.clip(jax.random.normal(jax.random.fold_in(key, 5), array_shape, jnp.float32), -4.0, 4.0)
    return base.astype(jnp.bfloat16)


def shard_levels(rng, extent, cuts, smallest, largest):
    def one(dim, shards_of):
        heights = jax.random.uniform(jax.random.fold_in(jax.random.fold_in(rng, 6), dim), (shards_of,), jnp.float32, smallest / len(cuts), largest / len(cuts))
        return jnp.repeat(jnp.exp(heights), extent[dim] // shards_of).reshape((-1,) + (1,) * (len(extent) - dim - 1))

    factor_of = one(*cuts[0])
    for cut in cuts[1:]:
        factor_of = factor_of * one(*cut)
    return factor_of


def noise(rng, dims, deviation, bound, shards=(), kind=jnp.bfloat16):
    entries = deviation * jax.random.normal(rng, dims, jnp.float32)
    if shards:
        entries = entries * shard_levels(rng, dims, shards, -0.22, 0.18)
    return jnp.clip(entries, -bound, bound).astype(kind)


def setup_inputs(seed: int = 0) -> dict:
    key_of = jax.random.split(jax.random.key(seed), 8)
    queries = draw_queries(jax.random.fold_in(key_of[7], 71), 0)
    cached_keys = draw_cached_keys(jax.random.fold_in(key_of[7], 71), 0)
    cached_values = noise(key_of[2], (CACHE_PAGES, PAGE_TOKENS, KEY_VALUE_HEADS, HEAD_SIZE), 1.0, 4.0, ((0, 8), (2, 4)))
    out_weight = noise(key_of[3], (QUERY_HEADS * HEAD_SIZE, D), (QUERY_HEADS * HEAD_SIZE) ** -0.5, 0.0625, ((0, 4), (1, 8)))
    select = draw_select(jax.random.fold_in(key_of[7], 71), 0)
    page_table = draw_page_table(jax.random.fold_in(key_of[7], 71), 0)
    block_page = draw_block_page(jax.random.fold_in(key_of[7], 71), 0)
    return dict(queries=queries, cached_keys=cached_keys, cached_values=cached_values, out_weight=out_weight, select=select, page_table=page_table, block_page=block_page)


FLOOR = -1.0e30


def group_attend(row_list, key_rows, value_rows, key_pos, query_pos):
    repeat_heads = QUERY_HEADS // KEY_VALUE_HEADS
    query_block = row_list.astype(jnp.float32).reshape(PAGE_TOKENS, KEY_VALUE_HEADS, repeat_heads, HEAD_SIZE)
    scores = jnp.einsum("rgeh,kgh->rgek", query_block, key_rows.astype(jnp.float32), precision=lax.Precision.HIGHEST) * (HEAD_SIZE ** -0.5)
    allowed = key_pos[None, :] <= query_pos[:, None]
    scores = jnp.where(allowed[:, None, None, :], scores, FLOOR)
    peak = jnp.max(scores, axis=-1)
    weights = jnp.exp(scores - peak[..., None])
    total = jnp.sum(weights, axis=-1)
    rounded = lax.optimization_barrier(weights.astype(jnp.bfloat16)).astype(jnp.float32)
    output = jnp.einsum("rgek,kgh->rgeh", rounded, value_rows.astype(jnp.float32), precision=lax.Precision.HIGHEST)
    return output.reshape(PAGE_TOKENS, QUERY_HEADS, HEAD_SIZE), peak.reshape(PAGE_TOKENS, QUERY_HEADS), total.reshape(PAGE_TOKENS, QUERY_HEADS)


def reference(queries, cached_keys, cached_values, out_weight, select, page_table, block_page):
    offsets = jnp.arange(PAGE_TOKENS, dtype=jnp.int32)
    blocks = []
    for block in range(QBLOCKS):
        row_list = queries[block * PAGE_TOKENS:(block + 1) * PAGE_TOKENS]
        chosen = select[block]
        owners = page_table[chosen] // PAGES_PER_INDEX
        grouped = chosen[jnp.argsort(owners, stable=True)].reshape(OWNERS_SEL, PICKED_PAGES)
        query_pos = block_page[block] * PAGE_TOKENS + offsets
        results = []
        for group in range(OWNERS_SEL):
            pages = grouped[group]
            slot_list = page_table[pages]
            key_rows = cached_keys[slot_list].reshape(PICKED_PAGES * PAGE_TOKENS, KEY_VALUE_HEADS, HEAD_SIZE)
            value_rows = cached_values[slot_list].reshape(PICKED_PAGES * PAGE_TOKENS, KEY_VALUE_HEADS, HEAD_SIZE)
            key_pos = (pages[:, None] * PAGE_TOKENS + offsets[None, :]).reshape(-1).astype(jnp.int32)
            results.append(group_attend(row_list, key_rows, value_rows, key_pos, query_pos))
        row_max = results[0][1]
        for result in results[1:]:
            row_max = jnp.maximum(row_max, result[1])
        row_total = jnp.zeros((PAGE_TOKENS, QUERY_HEADS), jnp.float32)
        for result in results:
            row_total = row_total + result[2] * jnp.exp(result[1] - row_max)
        merged = jnp.zeros((PAGE_TOKENS, QUERY_HEADS, HEAD_SIZE), jnp.float32)
        for output, peak, total in results:
            share = output * (jnp.exp(peak - row_max) / row_total)[..., None]
            merged = merged + lax.optimization_barrier(share.astype(jnp.bfloat16)).astype(jnp.float32)
        blocks.append(merged.astype(jnp.bfloat16).reshape(PAGE_TOKENS, QUERY_HEADS * HEAD_SIZE))
    attention = jnp.concatenate(blocks, axis=0)
    return jnp.dot(attention, out_weight, preferred_element_type=jnp.float32).astype(jnp.bfloat16)
```

```python
import functools
import math

import jax
import jax.numpy as jnp
from jax import lax
from jax.experimental import pallas as pl
from jax.experimental.pallas import tpu as pltpu
from jax.sharding import PartitionSpec as P

PICKED_PAGES = 6
FLOOR = -1e30
LANES = 128
HEADS_PER_TILE = 2

VMEM = pltpu.VMEM
SMEM = pltpu.SMEM
BF16 = jnp.bfloat16
F32 = jnp.float32


def in_vmem():
    return pl.BlockSpec(memory_space=VMEM)


def in_smem():
    return pl.BlockSpec(memory_space=SMEM)


def params(mib):
    return pltpu.CompilerParams(vmem_limit_bytes=mib * 2**20)


class Plan:
    def __init__(self, n, ways, rows, blocks, page):
        self.n, self.rows, self.blocks, self.page = n, rows, blocks, page
        self.group = n // blocks
        self.halves = blocks == 2 and n == 8 and ways == 4 and rows * self.group == page
        self.cross = n * 3 // 4
        self.chunks = self.group if self.halves else 1

    def block(self, me, lb):
        return (me // self.group) ^ lb if self.halves else lb

    def offsets(self, me, lb, shape):
        row = lax.broadcasted_iota(jnp.int32, shape, 0) % self.page
        if not self.halves:
            return row
        mine = (me ^ (lb * self.cross)) % self.group
        return ((row // self.rows) ^ mine) * self.rows + row % self.rows


def fetch_kernel(plan, pages_dev, select, table, stands, keys, values, k_out, v_out, info, k_buf, v_buf, sems):
    me = lax.axis_index("pages")
    blocks, picked = k_buf.shape[:2]
    span = k_buf.shape[2]
    heads = k_out.shape[1]
    page = span // heads
    low = me * pages_dev
    for lb in range(blocks):
        block = plan.block(me, lb)
        stand = stands[block]
        info[lb, 1] = 0

        def step(i, carry, lb=lb, block=block, stand=stand):
            others, all_ = carry
            logical = select[block, i]
            row = table[logical] - low
            mine = (row >= 0) & (row < pages_dev)
            own = logical == stand
            slot = jnp.where(own, 0, jnp.clip(picked - 1 - others, 0, picked - 1))

            @pl.when(mine)
            def _():
                pltpu.make_async_copy(keys.at[row], k_buf.at[lb, slot], sems.at[lb, slot, 0]).start()
                pltpu.make_async_copy(values.at[row], v_buf.at[lb, slot], sems.at[lb, slot, 1]).start()

                @pl.when(slot == 0)
                def _():
                    info[lb, 1] = logical

            one = mine.astype(jnp.int32)
            return others + jnp.where(own, 0, one), all_ + one

        _, count = lax.fori_loop(0, select.shape[1], step, (jnp.int32(0), jnp.int32(0)))
        info[lb, 0] = count

    row = lax.broadcasted_iota(jnp.int32, (span, span), 0)
    column = lax.broadcasted_iota(jnp.int32, (span, span), 1)
    apart = (column == (row % page) * heads + row // page).astype(F32).astype(BF16)
    for lb in range(blocks):

        @pl.when(info[lb, 0] > 0)
        def _(lb=lb):
            for g in range(heads):
                v_out[lb, g, :, LANES:] = jnp.ones((picked * page, LANES), BF16)
            for slot in range(picked):
                pltpu.make_async_copy(keys.at[0], k_buf.at[lb, slot], sems.at[lb, slot, 0]).wait()
                pltpu.make_async_copy(values.at[0], v_buf.at[lb, slot], sems.at[lb, slot, 1]).wait()
                both = jnp.concatenate([k_buf[lb, slot], v_buf[lb, slot]], axis=1)
                split = jnp.dot(apart, both, preferred_element_type=F32).astype(BF16)
                for g in range(heads):
                    here = slice(slot * page, (slot + 1) * page)
                    k_out[lb, g, here, :] = split[g * page : (g + 1) * page, :LANES]
                    v_out[lb, g, here, :LANES] = split[g * page : (g + 1) * page, LANES:]


def fetch(plan, select, table, stands, keys, values):
    pages_dev, page, heads, size = keys.shape
    blocks, picked = select.shape[0], PICKED_PAGES
    span = page * heads
    return pl.pallas_call(
        functools.partial(fetch_kernel, plan, pages_dev),
        out_shape=(
            jax.ShapeDtypeStruct((blocks, heads, picked * page, size), BF16),
            jax.ShapeDtypeStruct((blocks, heads, picked * page, size + LANES), BF16),
            jax.ShapeDtypeStruct((blocks, 2), jnp.int32),
        ),
        in_specs=[in_smem(), in_smem(), in_smem()] + [pl.BlockSpec(memory_space=pl.ANY)] * 2,
        out_specs=(in_vmem(), in_vmem(), in_smem()),
        scratch_shapes=[
            VMEM((blocks, picked, span, size), BF16),
            VMEM((blocks, picked, span, size), BF16),
            pltpu.SemaphoreType.DMA((blocks, picked, 2)),
        ],
        compiler_params=params(16),
        cost_estimate=pl.CostEstimate(flops=4 * 10**9, bytes_accessed=8 * 2**20, transcendentals=0),
    )(select, table, stands, keys.reshape(pages_dev, span, size), values.reshape(pages_dev, span, size))


def pack_stats(lse, heads):
    lane = lax.broadcasted_iota(jnp.int32, lse.shape, 1)
    high = lse.astype(BF16).astype(F32)
    rest = lse - high
    middle = rest.astype(BF16).astype(F32)
    low = rest - middle
    packed = jnp.where(lane < heads, high, 0.0)
    packed = packed + jnp.where((lane >= heads) & (lane < 2 * heads), pltpu.roll(middle, heads, 1), 0.0)
    packed = packed + jnp.where((lane >= 2 * heads) & (lane < 3 * heads), pltpu.roll(low, 2 * heads, 1), 0.0)
    return packed.astype(BF16)


def unpack_stats(packed, heads):
    wide = packed.astype(F32)
    return wide + pltpu.roll(wide, LANES - heads, 1) + pltpu.roll(wide, LANES - 2 * heads, 1)


def attend_kernel(plan, heads, info, stands, *refs):
    me = lax.axis_index("pages")
    blocks, chunks, page = plan.blocks, plan.chunks, plan.page
    queries = refs[: blocks * chunks]
    k_ref, v_ref = refs[blocks * chunks : blocks * chunks + 2]
    outs = refs[blocks * chunks + 2 :]
    kv_heads, size = k_ref.shape[1], k_ref.shape[3]
    repeat = heads // kv_heads
    width = heads * size
    part = page // chunks
    tile = math.gcd(repeat, HEADS_PER_TILE)
    scale = size**-0.5 * math.log2(math.e)
    lane = lax.broadcasted_iota(jnp.int32, (page, LANES), 1)
    for lb in range(blocks):
        block = plan.block(me, lb)
        mine = queries[lb * chunks : (lb + 1) * chunks]

        def put(c, columns, value, lb=lb):
            outs[c][lb * part : (lb + 1) * part, columns] = value

        @pl.when(info[lb, 0] > 0)
        def _(lb=lb, block=block, mine=mine, put=put):
            shape = (tile * page, page)
            key_pos = info[lb, 1] * page + lax.broadcasted_iota(jnp.int32, shape, 1)
            query_pos = stands[block] * page + plan.offsets(me, lb, shape)
            allowed = key_pos <= query_pos
            stats = jnp.zeros((page, LANES), F32)
            for g in range(kv_heads):
                for t in range(0, repeat, tile):
                    first = g * repeat + t
                    q = jnp.concatenate(
                        [m[:, h * size : (h + 1) * size] for h in range(first, first + tile) for m in mine], axis=0
                    )
                    scores = scale * lax.dot_general(
                        q, k_ref[lb, g], (((1,), (1,)), ((), ())), preferred_element_type=F32
                    )
                    scores = jnp.concatenate(
                        [jnp.where(allowed, scores[:, :page], FLOOR), scores[:, page:]], axis=1
                    )
                    peak = jnp.max(scores, axis=1, keepdims=True)
                    weights = jnp.exp2(scores - peak).astype(BF16)
                    both = jnp.dot(weights, v_ref[lb, g], preferred_element_type=F32)
                    total = both[:, size:]
                    out = (both[:, :size] / total).astype(BF16)
                    lse = peak + jnp.log2(total)
                    for i in range(tile):
                        h = first + i
                        stats = jnp.where(lane == h, lse[i * page : (i + 1) * page], stats)
                        for c in range(chunks):
                            put(c, slice(h * size, (h + 1) * size), out[i * page + c * part : i * page + (c + 1) * part])
            packed = pack_stats(stats, heads)
            for c in range(chunks):
                put(c, slice(width, width + LANES), packed[c * part : (c + 1) * part])

        @pl.when(info[lb, 0] == 0)
        def _(put=put):
            for c in range(chunks):
                put(c, slice(0, width), jnp.zeros((part, width), BF16))
                put(c, slice(width, width + LANES), pack_stats(jnp.full((part, LANES), FLOOR, F32), heads))


def attend(plan, heads, info, stands, queries, keys, values):
    part = plan.page // plan.chunks
    shape = jax.ShapeDtypeStruct((plan.blocks * part, queries[0].shape[1] + LANES), BF16)
    return pl.pallas_call(
        functools.partial(attend_kernel, plan, heads),
        out_shape=(shape,) * plan.chunks,
        in_specs=[in_smem(), in_smem()] + [in_vmem()] * (len(queries) + 2),
        out_specs=(in_vmem(),) * plan.chunks,
        compiler_params=params(32),
    )(info, stands, *queries, keys, values)


def merged(parts, stats, heads, size):
    top = functools.reduce(jnp.maximum, stats)
    shares = [jnp.exp2(s - top) for s in stats]
    total = functools.reduce(jnp.add, shares)
    shares = [s / total for s in shares]

    def head(h):
        return functools.reduce(
            jnp.add, [p(h).astype(F32) * s[:, h : h + 1] for p, s in zip(parts, shares, strict=True)]
        )

    return head, top + jnp.log2(total)


def merge_kernel(heads, *refs):
    sources, out = refs[:-1], refs[-1]
    width = out.shape[1] - LANES
    size = width // heads
    head, lse = merged(
        [lambda h, r=r: r[:, h * size : (h + 1) * size] for r in sources],
        [unpack_stats(r[:, width:], heads) for r in sources],
        heads,
        size,
    )
    for h in range(heads):
        out[:, h * size : (h + 1) * size] = head(h).astype(BF16)
    out[:, width:] = pack_stats(lse, heads)


def merge(heads, *sources):
    return pl.pallas_call(
        functools.partial(merge_kernel, heads),
        out_shape=jax.ShapeDtypeStruct(sources[0].shape, BF16),
        in_specs=[in_vmem()] * len(sources),
        out_specs=in_vmem(),
        compiler_params=params(8),
    )(*sources)


def finish_kernel(heads, near, far, out):
    rows, width = out.shape
    size = width // heads
    part = rows // 2
    for i in range(2):
        here, there = slice(i * part, (i + 1) * part), slice((1 - i) * part, (2 - i) * part)
        head, _ = merged(
            [
                lambda h: near[here, h * size : (h + 1) * size],
                lambda h: far[there, h * size : (h + 1) * size],
            ],
            [unpack_stats(near[here, width:], heads), unpack_stats(far[there, width:], heads)],
            heads,
            size,
        )
        for h in range(heads):
            out[here, h * size : (h + 1) * size] = head(h).astype(BF16)


def finish(heads, near, far):
    return pl.pallas_call(
        functools.partial(finish_kernel, heads),
        out_shape=jax.ShapeDtypeStruct((near.shape[0], near.shape[1] - LANES), BF16),
        in_specs=[in_vmem()] * 2,
        out_specs=in_vmem(),
        compiler_params=params(8),
    )(near, far)


def project_kernel(plan, ways, *refs):
    sources, weight, outs, rows_ref = refs[: plan.group], refs[plan.group], refs[plan.group + 1 : -1], refs[-1]
    me, column = lax.axis_index("pages"), lax.axis_index("mp")
    rows = plan.rows
    holders = plan.n // ways
    for k in range(plan.group):
        for half in range(2):
            device = me ^ k ^ (half * plan.cross)
            place = ((device // holders) ^ column) * holders + device % holders
            rows_ref[pl.ds(pl.multiple_of(place * rows, rows), rows), :] = sources[k][half * rows : (half + 1) * rows, :]
    part = holders * rows
    product = jnp.dot(rows_ref[...], weight[...], preferred_element_type=F32)
    keep, send = outs
    for i, w in enumerate(range(0, ways, 2)):
        keep[i * part : (i + 1) * part, :] = product[w * part : (w + 1) * part]
        send[i * part : (i + 1) * part, :] = product[(w + 1) * part : (w + 2) * part].astype(BF16)


def project(plan, ways, sources, weight):
    total = plan.n * plan.rows
    columns = weight.shape[1]
    return pl.pallas_call(
        functools.partial(project_kernel, plan, ways),
        out_shape=(
            jax.ShapeDtypeStruct((total // 2, columns), F32),
            jax.ShapeDtypeStruct((total // 2, columns), BF16),
        ),
        in_specs=[in_vmem()] * (plan.group + 1),
        out_specs=(in_vmem(), in_vmem()),
        scratch_shapes=[VMEM((total, weight.shape[0]), BF16)],
        compiler_params=params(24),
    )(*sources, weight)


def swap(x, axis, distance):
    n = lax.axis_size(axis)
    return lax.ppermute(x, axis, [(i, i ^ distance) for i in range(n)])


def by_halves(plan, heads, queries, weight, stands, pages):
    keys, values, info = pages
    far = swap(queries, "pages", plan.cross)
    own = [queries] + [swap(queries, "pages", k) for k in range(1, plan.group)]
    other = [far] + [swap(far, "pages", k) for k in range(1, plan.group)]
    outs = attend(plan, heads, info, stands, own + other, keys, values)
    near = merge(heads, outs[0], *(swap(outs[k], "pages", k) for k in range(1, plan.group)))
    rows = finish(heads, near, swap(near, "pages", plan.cross))
    every = [rows] + [swap(rows, "pages", k) for k in range(1, plan.group)]
    keep, send = project(plan, lax.axis_size("mp"), every, weight)
    total = keep + swap(send, "mp", 1).astype(F32)
    part = total.shape[0] // 2
    return (total[:part] + swap(total[part:].astype(BF16), "mp", 2).astype(F32)).astype(BF16)


def by_gathers(plan, heads, queries, weight, stands, pages):
    keys, values, info = pages
    width = queries.shape[1]
    size = width // heads
    gathered = lax.all_gather(queries, "pages", axis=0, tiled=True)
    rows = gathered.shape[0]
    mine = [gathered[i * plan.page : (i + 1) * plan.page] for i in range(plan.blocks)]
    (out,) = attend(plan, heads, info, stands, mine, keys, values)
    packed = out[:, width : width + 3 * heads].astype(F32)
    lse = packed[:, :heads] + packed[:, heads : 2 * heads] + packed[:, 2 * heads :]
    every = lax.all_gather(lse, "pages")
    top = jnp.max(every, axis=0)
    share = jnp.exp2(lse - top) / jnp.sum(jnp.exp2(every - top), axis=0)
    part = (out[:, :width].reshape(rows, heads, size).astype(F32) * share[..., None]).reshape(1, rows, width)
    received = lax.all_to_all(part.astype(BF16), "pages", split_axis=1, concat_axis=0, tiled=True)
    mixed = jnp.sum(received, axis=0, dtype=F32).astype(BF16)
    terms = jnp.dot(lax.all_gather(mixed, "pages", axis=0, tiled=True), weight, preferred_element_type=F32)
    return lax.psum_scatter(terms, "mp", scatter_dimension=0, tiled=True).astype(BF16)


def per_device(queries, cached_keys, cached_values, out_weight, select, page_table, block_page):
    n, ways = lax.axis_size("pages"), lax.axis_size("mp")
    plan = Plan(n, ways, queries.shape[0], select.shape[0], cached_keys.shape[1])
    heads = queries.shape[1] // cached_keys.shape[3]
    pages = fetch(plan, select, page_table, block_page, cached_keys, cached_values)
    way = by_halves if plan.halves else by_gathers
    return way(plan, heads, queries, out_weight, block_page, pages)


def solution(mesh):
    placed = (
        P("pages", "mp"),
        P("pages", None, "mp", None),
        P("pages", None, "mp", None),
        P("mp", "pages"),
        P(),
        P(),
        P(),
    )
    return jax.shard_map(
        per_device, mesh=mesh, in_specs=placed, out_specs=P("mp", "pages"), check_vma=False
    )
```

```python
import functools
import math

import jax
import jax.numpy as jnp
from jax import lax
from jax.experimental import pallas as pl
from jax.experimental.pallas import tpu as pltpu
from jax.sharding import PartitionSpec as P

PICKED_PAGES = 6
FLOOR = -1e30
LANES = 128
HEADS_PER_TILE = 2

VMEM = pltpu.VMEM
SMEM = pltpu.SMEM
BF16 = jnp.bfloat16
F32 = jnp.float32


def in_vmem():
    return pl.BlockSpec(memory_space=VMEM)


def in_smem():
    return pl.BlockSpec(memory_space=SMEM)


def params(mib):
    return pltpu.CompilerParams(vmem_limit_bytes=mib * 2**20)


class Plan:
    def __init__(self, n, ways, rows, blocks, page):
        self.n, self.rows, self.blocks, self.page = n, rows, blocks, page
        self.group = n // blocks
        self.halves = blocks == 2 and n == 8 and ways == 4 and rows * self.group == page
        self.cross = n * 3 // 4
        self.chunks = self.group if self.halves else 1

    def block(self, me, lb):
        return (me // self.group) ^ lb if self.halves else lb

    def offsets(self, me, lb, shape):
        row = lax.broadcasted_iota(jnp.int32, shape, 0) % self.page
        if not self.halves:
            return row
        mine = (me ^ (lb * self.cross)) % self.group
        return ((row // self.rows) ^ mine) * self.rows + row % self.rows


def fetch_kernel(plan, pages_dev, select_hbm, table_hbm, stands_hbm, keys, values, k_out, v_out, info, select, table, stands, rows, k_buf, v_buf, sems, int_sems):
    me = lax.axis_index("pages")
    blocks, picked = k_buf.shape[:2]
    span = k_buf.shape[2]
    heads = k_out.shape[1]
    page = span // heads
    low = me * pages_dev
    loads = [
        pltpu.make_async_copy(a, b, int_sems.at[i])
        for i, (a, b) in enumerate(((select_hbm, select), (table_hbm, table), (stands_hbm, stands)))
    ]
    for load in loads:
        load.start()
    row = lax.broadcasted_iota(jnp.int32, (span, span), 0)
    column = lax.broadcasted_iota(jnp.int32, (span, span), 1)
    apart = (column == (row % page) * heads + row // page).astype(F32).astype(BF16)
    for load in loads:
        load.wait()
    for lb in range(blocks):
        block = plan.block(me, lb)
        stand = stands[block]
        info[lb, 1] = plan.n * pages_dev
        info[lb, 2] = stand
        others = jnp.int32(0)
        count = jnp.int32(0)
        for i in range(select.shape[1]):
            logical = select[block, i]
            local = table[logical] - low
            mine = (local >= 0) & (local < pages_dev)
            own = logical == stand
            slot = jnp.where(own, 0, jnp.maximum(picked - 1 - others, 0))
            slot = jnp.where(mine, slot, picked)
            rows[lb, slot] = local
            rows[blocks + lb, slot] = logical
            one = mine.astype(jnp.int32)
            others = others + jnp.where(own, 0, one)
            count = count + one
        info[lb, 0] = count
        info[lb, 1] = rows[blocks + lb, 0]

        @pl.when(count > 0)
        def _(lb=lb):
            for slot in range(picked):
                local = jnp.clip(rows[lb, slot], 0, pages_dev - 1)
                pltpu.make_async_copy(keys.at[local], k_buf.at[lb, slot], sems.at[lb, slot, 0]).start()
                pltpu.make_async_copy(values.at[local], v_buf.at[lb, slot], sems.at[lb, slot, 1]).start()

    for lb in range(blocks):

        @pl.when(info[lb, 0] > 0)
        def _(lb=lb):
            for g in range(heads):
                v_out[lb, g, :, LANES:] = jnp.ones((picked * page, LANES), BF16)
            for slot in range(picked):
                pltpu.make_async_copy(keys.at[0], k_buf.at[lb, slot], sems.at[lb, slot, 0]).wait()
                pltpu.make_async_copy(values.at[0], v_buf.at[lb, slot], sems.at[lb, slot, 1]).wait()
            for slot in range(picked):
                both = jnp.concatenate([k_buf[lb, slot], v_buf[lb, slot]], axis=1)
                split = jnp.dot(apart, both, preferred_element_type=F32).astype(BF16)
                for g in range(heads):
                    here = slice(slot * page, (slot + 1) * page)
                    k_out[lb, g, here, :] = split[g * page : (g + 1) * page, :LANES]
                    v_out[lb, g, here, :LANES] = split[g * page : (g + 1) * page, LANES:]


def fetch(plan, select, table, stands, keys, values):
    pages_dev, page, heads, size = keys.shape
    blocks, picked = select.shape[0], PICKED_PAGES
    span = page * heads
    return pl.pallas_call(
        functools.partial(fetch_kernel, plan, pages_dev),
        out_shape=(
            jax.ShapeDtypeStruct((blocks, heads, picked * page, size), BF16),
            jax.ShapeDtypeStruct((blocks, heads, picked * page, size + LANES), BF16),
            jax.ShapeDtypeStruct((blocks, 3), jnp.int32),
        ),
        in_specs=[pl.BlockSpec(memory_space=pltpu.HBM)] * 5,
        out_specs=(in_vmem(), in_vmem(), in_smem()),
        scratch_shapes=[
            SMEM(select.shape, jnp.int32),
            SMEM(table.shape, jnp.int32),
            SMEM(stands.shape, jnp.int32),
            SMEM((2 * blocks, picked + 1), jnp.int32),
            VMEM((blocks, picked, span, size), BF16),
            VMEM((blocks, picked, span, size), BF16),
            pltpu.SemaphoreType.DMA((blocks, picked, 2)),
            pltpu.SemaphoreType.DMA((3,)),
        ],
        compiler_params=params(16),
        cost_estimate=pl.CostEstimate(flops=2 * 10**9, bytes_accessed=8 * 2**20, transcendentals=0),
    )(*(pltpu.with_memory_space_constraint(x, pltpu.HBM) for x in (select, table, stands, keys.reshape(pages_dev, span, size), values.reshape(pages_dev, span, size))))


def pack_stats(lse, heads):
    lane = lax.broadcasted_iota(jnp.int32, lse.shape, 1)
    high = lse.astype(BF16).astype(F32)
    rest = lse - high
    middle = rest.astype(BF16).astype(F32)
    low = rest - middle
    packed = jnp.where(lane < heads, high, 0.0)
    packed = packed + jnp.where((lane >= heads) & (lane < 2 * heads), pltpu.roll(middle, heads, 1), 0.0)
    packed = packed + jnp.where((lane >= 2 * heads) & (lane < 3 * heads), pltpu.roll(low, 2 * heads, 1), 0.0)
    return packed.astype(BF16)


def unpack_stats(packed, heads):
    wide = packed.astype(F32)
    return wide + pltpu.roll(wide, LANES - heads, 1) + pltpu.roll(wide, LANES - 2 * heads, 1)


def attend_kernel(plan, heads, lb, info, *refs):
    me = lax.axis_index("pages")
    chunks, page = plan.chunks, plan.page
    queries, (k_ref, v_ref), outs = refs[:chunks], refs[chunks : chunks + 2], refs[chunks + 2 :]
    kv_heads, size = k_ref.shape[1], k_ref.shape[3]
    repeat = heads // kv_heads
    width = heads * size
    part = page // chunks
    tile = math.gcd(repeat, HEADS_PER_TILE)
    scale = size**-0.5 * math.log2(math.e)
    lane = lax.broadcasted_iota(jnp.int32, (page, LANES), 1)

    @pl.when(info[lb, 0] > 0)
    def _():
        shape = (tile * page, page)
        key_pos = info[lb, 1] * page + lax.broadcasted_iota(jnp.int32, shape, 1)
        query_pos = info[lb, 2] * page + plan.offsets(me, lb, shape)
        allowed = key_pos <= query_pos
        stats = jnp.zeros((page, LANES), F32)
        for g in range(kv_heads):
            for t in range(0, repeat, tile):
                first = g * repeat + t
                q = jnp.concatenate(
                    [m[:, h * size : (h + 1) * size] for h in range(first, first + tile) for m in queries], axis=0
                )
                scores = scale * lax.dot_general(
                    q, k_ref[lb, g], (((1,), (1,)), ((), ())), preferred_element_type=F32
                )
                scores = jnp.concatenate([jnp.where(allowed, scores[:, :page], FLOOR), scores[:, page:]], axis=1)
                peak = jnp.max(scores, axis=1, keepdims=True)
                weights = jnp.exp2(scores - peak).astype(BF16)
                both = jnp.dot(weights, v_ref[lb, g], preferred_element_type=F32)
                total = both[:, size:]
                out = (both[:, :size] / total).astype(BF16)
                lse = peak + jnp.log2(total)
                for i in range(tile):
                    h = first + i
                    stats = jnp.where(lane == h, lse[i * page : (i + 1) * page], stats)
                    for c in range(chunks):
                        outs[c][:, h * size : (h + 1) * size] = out[i * page + c * part : i * page + (c + 1) * part]
        packed = pack_stats(stats, heads)
        for c in range(chunks):
            outs[c][:, width:] = packed[c * part : (c + 1) * part]

    @pl.when(info[lb, 0] == 0)
    def _():
        for c in range(chunks):
            outs[c][:, :width] = jnp.zeros((part, width), BF16)
            outs[c][:, width:] = pack_stats(jnp.full((part, LANES), FLOOR, F32), heads)


def attend(plan, heads, lb, pages, queries):
    keys, values, info = pages
    part = plan.page // plan.chunks
    shape = jax.ShapeDtypeStruct((part, queries[0].shape[1] + LANES), BF16)
    return pl.pallas_call(
        functools.partial(attend_kernel, plan, heads, lb),
        out_shape=(shape,) * plan.chunks,
        in_specs=[in_smem()] + [in_vmem()] * (len(queries) + 2),
        out_specs=(in_vmem(),) * plan.chunks,
        compiler_params=params(32),
        cost_estimate=pl.CostEstimate(flops=2 * 10**9, bytes_accessed=4 * 2**20, transcendentals=10**6),
    )(info, *queries, keys, values)


def merged(parts, stats, heads, size):
    top = functools.reduce(jnp.maximum, stats)
    shares = [jnp.exp2(s - top) for s in stats]
    total = functools.reduce(jnp.add, shares)
    shares = [s / total for s in shares]

    def head(h):
        return functools.reduce(
            jnp.add, [p(h).astype(F32) * s[:, h : h + 1] for p, s in zip(parts, shares, strict=True)]
        )

    return head, top + jnp.log2(total)


def merge_kernel(heads, *refs):
    sources, out = refs[:-1], refs[-1]
    width = out.shape[1] - LANES
    size = width // heads
    head, lse = merged(
        [lambda h, r=r: r[:, h * size : (h + 1) * size] for r in sources],
        [unpack_stats(r[:, width:], heads) for r in sources],
        heads,
        size,
    )
    for h in range(heads):
        out[:, h * size : (h + 1) * size] = head(h).astype(BF16)
    out[:, width:] = pack_stats(lse, heads)


def merge(heads, *sources):
    return pl.pallas_call(
        functools.partial(merge_kernel, heads),
        out_shape=jax.ShapeDtypeStruct(sources[0].shape, BF16),
        in_specs=[in_vmem()] * len(sources),
        out_specs=in_vmem(),
        compiler_params=params(8),
    )(*sources)


def finish_kernel(heads, near, far, out):
    width = out.shape[1]
    size = width // heads
    head, _ = merged(
        [lambda h, r=r: r[:, h * size : (h + 1) * size] for r in (near, far)],
        [unpack_stats(r[:, width:], heads) for r in (near, far)],
        heads,
        size,
    )
    for h in range(heads):
        out[:, h * size : (h + 1) * size] = head(h).astype(BF16)


def finish(heads, near, far):
    return pl.pallas_call(
        functools.partial(finish_kernel, heads),
        out_shape=jax.ShapeDtypeStruct((near.shape[0], near.shape[1] - LANES), BF16),
        in_specs=[in_vmem()] * 2,
        out_specs=in_vmem(),
        compiler_params=params(8),
    )(near, far)


def project_kernel(plan, ways, *refs):
    sources, weight, outs, rows_ref = refs[: plan.n], refs[plan.n], refs[plan.n + 1 : -1], refs[-1]
    me, column = lax.axis_index("pages"), lax.axis_index("mp")
    rows = plan.rows
    holders = plan.n // ways
    for k in range(plan.group):
        for half in range(2):
            device = me ^ k ^ (half * plan.cross)
            place = ((device // holders) ^ column) * holders + device % holders
            rows_ref[pl.ds(pl.multiple_of(place * rows, rows), rows), :] = sources[half * plan.group + k][...]
    part = holders * rows
    product = jnp.dot(rows_ref[...], weight[...], preferred_element_type=F32)
    keep, send = outs
    for i, w in enumerate(range(0, ways, 2)):
        keep[i * part : (i + 1) * part, :] = product[w * part : (w + 1) * part]
        send[i * part : (i + 1) * part, :] = product[(w + 1) * part : (w + 2) * part].astype(BF16)


def project(plan, ways, sources, weight):
    total = plan.n * plan.rows
    columns = weight.shape[1]
    return pl.pallas_call(
        functools.partial(project_kernel, plan, ways),
        out_shape=(
            jax.ShapeDtypeStruct((total // 2, columns), F32),
            jax.ShapeDtypeStruct((total // 2, columns), BF16),
        ),
        in_specs=[in_vmem()] * (plan.n + 1),
        out_specs=(in_vmem(), in_vmem()),
        scratch_shapes=[VMEM((total, weight.shape[0]), BF16)],
        compiler_params=params(24),
    )(*sources, weight)


def swap(x, axis, distance):
    n = lax.axis_size(axis)
    return lax.ppermute(x, axis, [(i, i ^ distance) for i in range(n)])


def spread(x, plan):
    return [x] + [swap(x, "pages", k) for k in range(1, plan.group)]


def by_halves(plan, heads, queries, weight, pages):
    far = swap(queries, "pages", plan.cross)
    chunks = [spread(queries, plan), spread(far, plan)]
    near = []
    for lb in range(plan.blocks):
        outs = attend(plan, heads, lb, pages, chunks[lb])
        near.append(merge(heads, outs[0], *(swap(outs[k], "pages", k) for k in range(1, plan.group))))
    across = [swap(x, "pages", plan.cross) for x in near]
    others = spread(finish(heads, near[1], across[0]), plan)
    mine = spread(finish(heads, near[0], across[1]), plan)
    keep, send = project(plan, lax.axis_size("mp"), mine + others, weight)
    total = keep + swap(send, "mp", 1).astype(F32)
    part = total.shape[0] // 2
    return (total[:part] + swap(total[part:].astype(BF16), "mp", 2).astype(F32)).astype(BF16)


def by_gathers(plan, heads, queries, weight, pages):
    width = queries.shape[1]
    size = width // heads
    gathered = lax.all_gather(queries, "pages", axis=0, tiled=True)
    rows = gathered.shape[0]
    outs = [
        attend(plan, heads, lb, pages, [gathered[lb * plan.page : (lb + 1) * plan.page]])[0]
        for lb in range(plan.blocks)
    ]
    out = jnp.concatenate(outs, axis=0)
    packed = out[:, width : width + 3 * heads].astype(F32)
    lse = packed[:, :heads] + packed[:, heads : 2 * heads] + packed[:, 2 * heads :]
    every = lax.all_gather(lse, "pages")
    top = jnp.max(every, axis=0)
    share = jnp.exp2(lse - top) / jnp.sum(jnp.exp2(every - top), axis=0)
    part = (out[:, :width].reshape(rows, heads, size).astype(F32) * share[..., None]).reshape(1, rows, width)
    received = lax.all_to_all(part.astype(BF16), "pages", split_axis=1, concat_axis=0, tiled=True)
    mixed = jnp.sum(received, axis=0, dtype=F32).astype(BF16)
    terms = jnp.dot(lax.all_gather(mixed, "pages", axis=0, tiled=True), weight, preferred_element_type=F32)
    return lax.psum_scatter(terms, "mp", scatter_dimension=0, tiled=True).astype(BF16)


def per_device(queries, cached_keys, cached_values, out_weight, select, page_table, block_page):
    n, ways = lax.axis_size("pages"), lax.axis_size("mp")
    plan = Plan(n, ways, queries.shape[0], select.shape[0], cached_keys.shape[1])
    heads = queries.shape[1] // cached_keys.shape[3]
    pages = fetch(plan, select, page_table, block_page, cached_keys, cached_values)
    way = by_halves if plan.halves else by_gathers
    return way(plan, heads, queries, out_weight, pages)


def solution(mesh):
    placed = (
        P("pages", "mp"),
        P("pages", None, "mp", None),
        P("pages", None, "mp", None),
        P("mp", "pages"),
        P(),
        P(),
        P(),
    )
    return jax.shard_map(
        per_device, mesh=mesh, in_specs=placed, out_specs=P("mp", "pages"), check_vma=False
    )
```

```python
import functools
import math

import jax
import jax.numpy as jnp
from jax import lax
from jax.experimental import pallas as pl
from jax.experimental.pallas import tpu as pltpu
from jax.sharding import PartitionSpec as P

PICKED_PAGES = 6
FLOOR = -1e30
LANES = 128
HEADS_PER_TILE = 2

VMEM = pltpu.VMEM
SMEM = pltpu.SMEM
BF16 = jnp.bfloat16
F32 = jnp.float32


def in_vmem():
    return pl.BlockSpec(memory_space=VMEM)


def in_smem():
    return pl.BlockSpec(memory_space=SMEM)


def params(mib):
    return pltpu.CompilerParams(vmem_limit_bytes=mib * 2**20)


class Plan:
    def __init__(self, n, ways, rows, blocks, page):
        self.n, self.rows, self.blocks, self.page = n, rows, blocks, page
        self.group = n // blocks
        self.halves = blocks == 2 and n == 8 and ways == 4 and rows * self.group == page
        self.cross = n * 3 // 4
        self.chunks = self.group if self.halves else 1

    def block(self, me, lb):
        return (me // self.group) ^ lb if self.halves else lb

    def offsets(self, me, lb, shape):
        row = lax.broadcasted_iota(jnp.int32, shape, 0) % self.page
        if not self.halves:
            return row
        mine = (me ^ (lb * self.cross)) % self.group
        return ((row // self.rows) ^ mine) * self.rows + row % self.rows


def fetch_kernel(plan, pages_dev, *refs):
    select_hbm, table_hbm, stands_hbm, queries, keys, values, k_out, v_out, info, q_out = refs[:10]
    select, table, stands, rows, k_buf, v_buf, sems, int_sems = refs[10:]
    me = lax.axis_index("pages")
    blocks, picked = k_buf.shape[:2]
    span = k_buf.shape[2]
    heads = k_out.shape[1]
    page = span // heads
    low = me * pages_dev
    loads = [
        pltpu.make_async_copy(a, b, int_sems.at[i])
        for i, (a, b) in enumerate(((select_hbm, select), (table_hbm, table), (stands_hbm, stands), (queries, q_out)))
    ]
    for load in loads:
        load.start()
    row = lax.broadcasted_iota(jnp.int32, (span, span), 0)
    column = lax.broadcasted_iota(jnp.int32, (span, span), 1)
    apart = (column == (row % page) * heads + row // page).astype(F32).astype(BF16)
    for load in loads[:3]:
        load.wait()
    for lb in range(blocks):
        block = plan.block(me, lb)
        stand = stands[block]
        info[lb, 1] = plan.n * pages_dev
        info[lb, 2] = stand
        others = jnp.int32(0)
        count = jnp.int32(0)
        for i in range(select.shape[1]):
            logical = select[block, i]
            local = table[logical] - low
            mine = (local >= 0) & (local < pages_dev)
            own = logical == stand
            slot = jnp.where(own, 0, jnp.maximum(picked - 1 - others, 0))
            slot = jnp.where(mine, slot, picked)
            rows[lb, slot] = local
            rows[blocks + lb, slot] = logical
            one = mine.astype(jnp.int32)
            others = others + jnp.where(own, 0, one)
            count = count + one
        info[lb, 0] = count
        info[lb, 1] = rows[blocks + lb, 0]

        @pl.when(count > 0)
        def _(lb=lb):
            for slot in range(picked):
                local = jnp.clip(rows[lb, slot], 0, pages_dev - 1)
                pltpu.make_async_copy(keys.at[local], k_buf.at[lb, slot], sems.at[lb, slot, 0]).start()
                pltpu.make_async_copy(values.at[local], v_buf.at[lb, slot], sems.at[lb, slot, 1]).start()

    for lb in range(blocks):

        @pl.when(info[lb, 0] > 0)
        def _(lb=lb):
            for g in range(heads):
                v_out[lb, g, :, LANES:] = jnp.ones((picked * page, LANES), BF16)
            for slot in range(picked):
                pltpu.make_async_copy(keys.at[0], k_buf.at[lb, slot], sems.at[lb, slot, 0]).wait()
                pltpu.make_async_copy(values.at[0], v_buf.at[lb, slot], sems.at[lb, slot, 1]).wait()
            for slot in range(picked):
                both = jnp.concatenate([k_buf[lb, slot], v_buf[lb, slot]], axis=1)
                split = jnp.dot(apart, both, preferred_element_type=F32).astype(BF16)
                for g in range(heads):
                    here = slice(slot * page, (slot + 1) * page)
                    k_out[lb, g, here, :] = split[g * page : (g + 1) * page, :LANES]
                    v_out[lb, g, here, :LANES] = split[g * page : (g + 1) * page, LANES:]
    loads[3].wait()


def fetch(plan, select, table, stands, queries, keys, values):
    pages_dev, page, heads, size = keys.shape
    blocks, picked = select.shape[0], PICKED_PAGES
    span = page * heads
    flat = (pages_dev, span, size)
    operands = (select, table, stands, queries, keys.reshape(flat), values.reshape(flat))
    return pl.pallas_call(
        functools.partial(fetch_kernel, plan, pages_dev),
        out_shape=(
            jax.ShapeDtypeStruct((blocks, heads, picked * page, size), BF16),
            jax.ShapeDtypeStruct((blocks, heads, picked * page, size + LANES), BF16),
            jax.ShapeDtypeStruct((blocks, 3), jnp.int32),
            jax.ShapeDtypeStruct(queries.shape, queries.dtype),
        ),
        in_specs=[pl.BlockSpec(memory_space=pltpu.HBM)] * len(operands),
        out_specs=(in_vmem(), in_vmem(), in_smem(), in_vmem()),
        scratch_shapes=[
            SMEM(select.shape, jnp.int32),
            SMEM(table.shape, jnp.int32),
            SMEM(stands.shape, jnp.int32),
            SMEM((2 * blocks, picked + 1), jnp.int32),
            VMEM((blocks, picked, span, size), BF16),
            VMEM((blocks, picked, span, size), BF16),
            pltpu.SemaphoreType.DMA((blocks, picked, 2)),
            pltpu.SemaphoreType.DMA((4,)),
        ],
        compiler_params=params(16),
        cost_estimate=pl.CostEstimate(flops=2 * 10**9, bytes_accessed=8 * 2**20, transcendentals=0),
    )(*(pltpu.with_memory_space_constraint(x, pltpu.HBM) for x in operands))


def pack_stats(lse, heads):
    lane = lax.broadcasted_iota(jnp.int32, lse.shape, 1)
    high = lse.astype(BF16).astype(F32)
    rest = lse - high
    middle = rest.astype(BF16).astype(F32)
    low = rest - middle
    packed = jnp.where(lane < heads, high, 0.0)
    packed = packed + jnp.where((lane >= heads) & (lane < 2 * heads), pltpu.roll(middle, heads, 1), 0.0)
    packed = packed + jnp.where((lane >= 2 * heads) & (lane < 3 * heads), pltpu.roll(low, 2 * heads, 1), 0.0)
    return packed.astype(BF16)


def unpack_stats(packed, heads):
    wide = packed.astype(F32)
    return wide + pltpu.roll(wide, LANES - heads, 1) + pltpu.roll(wide, LANES - 2 * heads, 1)


def attend_kernel(plan, heads, lb, info, *refs):
    me = lax.axis_index("pages")
    chunks, page = plan.chunks, plan.page
    queries, (k_ref, v_ref), outs = refs[:chunks], refs[chunks : chunks + 2], refs[chunks + 2 :]
    kv_heads, size = k_ref.shape[1], k_ref.shape[3]
    repeat = heads // kv_heads
    width = heads * size
    part = page // chunks
    tile = math.gcd(repeat, HEADS_PER_TILE)
    scale = size**-0.5 * math.log2(math.e)
    lane = lax.broadcasted_iota(jnp.int32, (page, LANES), 1)

    @pl.when(info[lb, 0] > 0)
    def _():
        shape = (tile * page, page)
        key_pos = info[lb, 1] * page + lax.broadcasted_iota(jnp.int32, shape, 1)
        query_pos = info[lb, 2] * page + plan.offsets(me, lb, shape)
        allowed = key_pos <= query_pos
        stats = jnp.zeros((page, LANES), F32)
        def product(first):
            q = jnp.concatenate(
                [m[:, h * size : (h + 1) * size] for h in range(first, first + tile) for m in queries], axis=0
            )
            return lax.dot_general(q, k_ref[lb, first // repeat], (((1,), (1,)), ((), ())), preferred_element_type=F32)

        ahead = product(0)
        for first in range(0, heads, tile):
            scores = scale * ahead
            if first + tile < heads:
                ahead = product(first + tile)
            scores = jnp.concatenate([jnp.where(allowed, scores[:, :page], FLOOR), scores[:, page:]], axis=1)
            peak = jnp.max(scores, axis=1, keepdims=True)
            weights = jnp.exp2(scores - peak).astype(BF16)
            both = jnp.dot(weights, v_ref[lb, first // repeat], preferred_element_type=F32)
            total = both[:, size:]
            out = (both[:, :size] / total).astype(BF16)
            lse = peak + jnp.log2(total)
            for i in range(tile):
                h = first + i
                stats = jnp.where(lane == h, lse[i * page : (i + 1) * page], stats)
                for c in range(chunks):
                    outs[c][:, h * size : (h + 1) * size] = out[i * page + c * part : i * page + (c + 1) * part]
        packed = pack_stats(stats, heads)
        for c in range(chunks):
            outs[c][:, width:] = packed[c * part : (c + 1) * part]

    @pl.when(info[lb, 0] == 0)
    def _():
        for c in range(chunks):
            outs[c][:, :width] = jnp.zeros((part, width), BF16)
            outs[c][:, width:] = pack_stats(jnp.full((part, LANES), FLOOR, F32), heads)


def attend(plan, heads, lb, pages, queries):
    keys, values, info, _ = pages
    part = plan.page // plan.chunks
    shape = jax.ShapeDtypeStruct((part, queries[0].shape[1] + LANES), BF16)
    return pl.pallas_call(
        functools.partial(attend_kernel, plan, heads, lb),
        out_shape=(shape,) * plan.chunks,
        in_specs=[in_smem()] + [in_vmem()] * (len(queries) + 2),
        out_specs=(in_vmem(),) * plan.chunks,
        compiler_params=params(32),
        cost_estimate=pl.CostEstimate(flops=2 * 10**9, bytes_accessed=4 * 2**20, transcendentals=10**6),
    )(info, *queries, keys, values)


def merged(parts, stats):
    top = functools.reduce(jnp.maximum, stats)
    shares = [jnp.exp2(s - top) for s in stats]
    total = functools.reduce(jnp.add, shares)
    shares = [s / total for s in shares]

    def head(h):
        return functools.reduce(
            jnp.add, [p(h).astype(F32) * s[:, h : h + 1] for p, s in zip(parts, shares, strict=True)]
        )

    return head, top + jnp.log2(total)


def merge_kernel(heads, *refs):
    sources, out = refs[:-1], refs[-1]
    width = out.shape[1] - LANES
    size = width // heads
    head, lse = merged([heads_of(r, size) for r in sources], [unpack_stats(r[:, width:], heads) for r in sources])
    for h in range(heads):
        out[:, h * size : (h + 1) * size] = head(h).astype(BF16)
    out[:, width:] = pack_stats(lse, heads)


def merge(heads, *sources):
    return pl.pallas_call(
        functools.partial(merge_kernel, heads),
        out_shape=jax.ShapeDtypeStruct(sources[0].shape, BF16),
        in_specs=[in_vmem()] * len(sources),
        out_specs=in_vmem(),
        compiler_params=params(8),
    )(*sources)


def heads_of(ref, size):
    return lambda h: ref[:, h * size : (h + 1) * size]


def finish_kernel(heads, near, far, out):
    width = out.shape[1]
    size = width // heads
    head, _ = merged([heads_of(r, size) for r in (near, far)], [unpack_stats(r[:, width:], heads) for r in (near, far)])
    for h in range(heads):
        out[:, h * size : (h + 1) * size] = head(h).astype(BF16)


def finish(heads, near, far):
    return pl.pallas_call(
        functools.partial(finish_kernel, heads),
        out_shape=jax.ShapeDtypeStruct((near.shape[0], near.shape[1] - LANES), BF16),
        in_specs=[in_vmem()] * 2,
        out_specs=in_vmem(),
        compiler_params=params(8),
    )(near, far)


def merge_finish_kernel(heads, *refs):
    merge_kernel(heads, *refs[:-3], refs[-2])
    finish_kernel(heads, refs[-2], refs[-3], refs[-1])


def merge_finish(heads, far, *sources):
    rows, wide = far.shape
    return pl.pallas_call(
        functools.partial(merge_finish_kernel, heads),
        out_shape=(jax.ShapeDtypeStruct((rows, wide), BF16), jax.ShapeDtypeStruct((rows, wide - LANES), BF16)),
        in_specs=[in_vmem()] * (len(sources) + 1),
        out_specs=(in_vmem(),) * 2,
        compiler_params=params(8),
    )(*sources, far)


def project_kernel(plan, lb, *refs):
    sources, weight, (keep, send, rows_ref) = refs[: plan.group], refs[plan.group], refs[plan.group + 1 :]
    me, column = lax.axis_index("pages"), lax.axis_index("mp")
    rows = plan.rows
    holders = plan.group // 2
    for i, k in enumerate((*others(plan), 0)):
        device = me ^ k ^ (lb * plan.cross)
        place = ((device // holders % 2) ^ (column % 2)) * holders + device % holders
        rows_ref[pl.ds(pl.multiple_of(place * rows, rows), rows), :] = sources[i][...]
    product = jnp.dot(rows_ref[...], weight[...], preferred_element_type=F32)
    part = holders * rows
    keep[...] = product[:part]
    send[...] = product[part:].astype(BF16)


def project(plan, lb, sources, weight):
    columns = weight.shape[1]
    part = plan.page // 2
    return pl.pallas_call(
        functools.partial(project_kernel, plan, lb),
        out_shape=(jax.ShapeDtypeStruct((part, columns), F32), jax.ShapeDtypeStruct((part, columns), BF16)),
        in_specs=[in_vmem()] * (plan.group + 1),
        out_specs=(in_vmem(), in_vmem()),
        scratch_shapes=[VMEM((plan.page, weight.shape[0]), BF16)],
        compiler_params=params(24),
    )(*(sources[k] for k in (*others(plan), 0)), weight)


def swap(x, axis, distance):
    n = lax.axis_size(axis)
    return lax.ppermute(x, axis, [(i, i ^ distance) for i in range(n)])


def others(plan):
    return range(plan.group - 1, 0, -1)


def spread(x, plan):
    return {0: x} | {k: swap(x, "pages", k) for k in others(plan)}


def by_halves(plan, heads, queries, weight, pages):
    far = swap(queries, "pages", plan.cross)
    received = []
    for lb, rows in enumerate((pages[3], far)):
        chunks = spread(rows, plan)
        outs = attend(plan, heads, lb, pages, [chunks[k] for k in range(plan.group)])
        received.append([swap(outs[k], "pages", k) for k in others(plan)] + [outs[0]])
    near = merge(heads, *received[0])
    near_far, far_rows = merge_finish(heads, swap(near, "pages", plan.cross), *received[1])
    across = swap(near_far, "pages", plan.cross)
    sums = [None, None]
    for lb in (1, 0):
        rows = far_rows if lb else finish(heads, near, across)
        keep, send = project(plan, lb, spread(rows, plan), weight)
        sums[lb] = keep + swap(send, "mp", 1).astype(F32)
    stays = plan.block(lax.axis_index("pages"), 0) == lax.axis_index("mp") // 2
    mine = jnp.where(stays, sums[0], sums[1])
    away = jnp.where(stays, sums[1], sums[0]).astype(BF16)
    return (mine + swap(away, "mp", 2).astype(F32)).astype(BF16)


def by_gathers(plan, heads, queries, weight, pages):
    width = queries.shape[1]
    size = width // heads
    gathered = lax.all_gather(queries, "pages", axis=0, tiled=True)
    rows = gathered.shape[0]
    outs = [
        attend(plan, heads, lb, pages, [gathered[lb * plan.page : (lb + 1) * plan.page]])[0]
        for lb in range(plan.blocks)
    ]
    out = jnp.concatenate(outs, axis=0)
    packed = out[:, width : width + 3 * heads].astype(F32)
    lse = packed[:, :heads] + packed[:, heads : 2 * heads] + packed[:, 2 * heads :]
    every = lax.all_gather(lse, "pages")
    top = jnp.max(every, axis=0)
    share = jnp.exp2(lse - top) / jnp.sum(jnp.exp2(every - top), axis=0)
    part = (out[:, :width].reshape(rows, heads, size).astype(F32) * share[..., None]).reshape(1, rows, width)
    received = lax.all_to_all(part.astype(BF16), "pages", split_axis=1, concat_axis=0, tiled=True)
    mixed = jnp.sum(received, axis=0, dtype=F32).astype(BF16)
    terms = jnp.dot(lax.all_gather(mixed, "pages", axis=0, tiled=True), weight, preferred_element_type=F32)
    return lax.psum_scatter(terms, "mp", scatter_dimension=0, tiled=True).astype(BF16)


def per_device(queries, cached_keys, cached_values, out_weight, select, page_table, block_page):
    n, ways = lax.axis_size("pages"), lax.axis_size("mp")
    plan = Plan(n, ways, queries.shape[0], select.shape[0], cached_keys.shape[1])
    heads = queries.shape[1] // cached_keys.shape[3]
    pages = fetch(plan, select, page_table, block_page, queries, cached_keys, cached_values)
    way = by_halves if plan.halves else by_gathers
    return way(plan, heads, queries, out_weight, pages)


def solution(mesh):
    placed = (
        P("pages", "mp"),
        P("pages", None, "mp", None),
        P("pages", None, "mp", None),
        P("mp", "pages"),
        P(),
        P(),
        P(),
    )
    return jax.shard_map(
        per_device, mesh=mesh, in_specs=placed, out_specs=P("mp", "pages"), check_vma=False
    )
```

```python
import functools
import math

import jax
import jax.numpy as jnp
from jax import lax
from jax.experimental import pallas as pl
from jax.experimental.pallas import tpu as pltpu
from jax.sharding import PartitionSpec as P

PICKED_PAGES = 6
FLOOR = -1e30
LANES = 128
HEADS_PER_TILE = 2

VMEM = pltpu.VMEM
SMEM = pltpu.SMEM
BF16 = jnp.bfloat16
F32 = jnp.float32


def in_vmem():
    return pl.BlockSpec(memory_space=VMEM)


def in_smem():
    return pl.BlockSpec(memory_space=SMEM)


def params(mib):
    return pltpu.CompilerParams(vmem_limit_bytes=mib * 2**20)


class Plan:
    def __init__(self, n, ways, rows, blocks, page):
        self.n, self.rows, self.blocks, self.page = n, rows, blocks, page
        self.group = n // blocks
        self.halves = blocks == 2 and n == 8 and ways == 4 and rows * self.group == page
        self.cross = n * 3 // 4
        self.chunks = self.group if self.halves else 1

    def block(self, me, lb):
        return (me // self.group) ^ lb if self.halves else lb

    def offsets(self, me, lb, shape):
        row = lax.broadcasted_iota(jnp.int32, shape, 0) % self.page
        if not self.halves:
            return row
        mine = (me ^ (lb * self.cross)) % self.group
        return ((row // self.rows) ^ mine) * self.rows + row % self.rows


def fetch_kernel(plan, pages_dev, select_hbm, table_hbm, stands_hbm, keys, values, k_out, v_out, info, select, table, stands, rows, k_buf, v_buf, sems, int_sems):
    me = lax.axis_index("pages")
    blocks, picked = k_buf.shape[:2]
    span = k_buf.shape[2]
    heads = k_out.shape[1]
    page = span // heads
    low = me * pages_dev
    loads = [
        pltpu.make_async_copy(a, b, int_sems.at[i])
        for i, (a, b) in enumerate(((select_hbm, select), (table_hbm, table), (stands_hbm, stands)))
    ]
    for load in loads:
        load.start()
    row = lax.broadcasted_iota(jnp.int32, (span, span), 0)
    column = lax.broadcasted_iota(jnp.int32, (span, span), 1)
    apart = (column == (row % page) * heads + row // page).astype(F32).astype(BF16)
    for load in loads:
        load.wait()
    for lb in range(blocks):
        block = plan.block(me, lb)
        stand = stands[block]
        info[lb, 1] = plan.n * pages_dev
        info[lb, 2] = stand
        others = jnp.int32(0)
        count = jnp.int32(0)
        for i in range(select.shape[1]):
            logical = select[block, i]
            local = table[logical] - low
            mine = (local >= 0) & (local < pages_dev)
            own = logical == stand
            slot = jnp.where(own, 0, jnp.maximum(picked - 1 - others, 0))
            slot = jnp.where(mine, slot, picked)
            rows[lb, slot] = local
            rows[blocks + lb, slot] = logical
            one = mine.astype(jnp.int32)
            others = others + jnp.where(own, 0, one)
            count = count + one
        info[lb, 0] = count
        info[lb, 1] = rows[blocks + lb, 0]

        @pl.when(count > 0)
        def _(lb=lb):
            for slot in range(picked):
                local = jnp.clip(rows[lb, slot], 0, pages_dev - 1)
                pltpu.make_async_copy(keys.at[local], k_buf.at[lb, slot], sems.at[lb, slot, 0]).start()
                pltpu.make_async_copy(values.at[local], v_buf.at[lb, slot], sems.at[lb, slot, 1]).start()

    for lb in range(blocks):

        @pl.when(info[lb, 0] > 0)
        def _(lb=lb):
            for g in range(heads):
                v_out[lb, g, :, LANES:] = jnp.ones((picked * page, LANES), BF16)
            for slot in range(picked):
                pltpu.make_async_copy(keys.at[0], k_buf.at[lb, slot], sems.at[lb, slot, 0]).wait()
                pltpu.make_async_copy(values.at[0], v_buf.at[lb, slot], sems.at[lb, slot, 1]).wait()
            for slot in range(picked):
                both = jnp.concatenate([k_buf[lb, slot], v_buf[lb, slot]], axis=1)
                split = jnp.dot(apart, both, preferred_element_type=F32).astype(BF16)
                for g in range(heads):
                    here = slice(slot * page, (slot + 1) * page)
                    k_out[lb, g, here, :] = split[g * page : (g + 1) * page, :LANES]
                    v_out[lb, g, here, :LANES] = split[g * page : (g + 1) * page, LANES:]


def fetch(plan, select, table, stands, keys, values):
    pages_dev, page, heads, size = keys.shape
    blocks, picked = select.shape[0], PICKED_PAGES
    span = page * heads
    return pl.pallas_call(
        functools.partial(fetch_kernel, plan, pages_dev),
        out_shape=(
            jax.ShapeDtypeStruct((blocks, heads, picked * page, size), BF16),
            jax.ShapeDtypeStruct((blocks, heads, picked * page, size + LANES), BF16),
            jax.ShapeDtypeStruct((blocks, 3), jnp.int32),
        ),
        in_specs=[pl.BlockSpec(memory_space=pltpu.HBM)] * 5,
        out_specs=(in_vmem(), in_vmem(), in_smem()),
        scratch_shapes=[
            SMEM(select.shape, jnp.int32),
            SMEM(table.shape, jnp.int32),
            SMEM(stands.shape, jnp.int32),
            SMEM((2 * blocks, picked + 1), jnp.int32),
            VMEM((blocks, picked, span, size), BF16),
            VMEM((blocks, picked, span, size), BF16),
            pltpu.SemaphoreType.DMA((blocks, picked, 2)),
            pltpu.SemaphoreType.DMA((3,)),
        ],
        compiler_params=params(16),
        cost_estimate=pl.CostEstimate(flops=2 * 10**9, bytes_accessed=8 * 2**20, transcendentals=0),
    )(*(pltpu.with_memory_space_constraint(x, pltpu.HBM) for x in (select, table, stands, keys.reshape(pages_dev, span, size), values.reshape(pages_dev, span, size))))


def pack_stats(lse, heads):
    lane = lax.broadcasted_iota(jnp.int32, lse.shape, 1)
    high = lse.astype(BF16).astype(F32)
    rest = lse - high
    middle = rest.astype(BF16).astype(F32)
    low = rest - middle
    packed = jnp.where(lane < heads, high, 0.0)
    packed = packed + jnp.where((lane >= heads) & (lane < 2 * heads), pltpu.roll(middle, heads, 1), 0.0)
    packed = packed + jnp.where((lane >= 2 * heads) & (lane < 3 * heads), pltpu.roll(low, 2 * heads, 1), 0.0)
    return packed.astype(BF16)


def unpack_stats(packed, heads):
    wide = packed.astype(F32)
    return wide + pltpu.roll(wide, LANES - heads, 1) + pltpu.roll(wide, LANES - 2 * heads, 1)


def attend_kernel(plan, heads, lb, info, *refs):
    me = lax.axis_index("pages")
    chunks, page = plan.chunks, plan.page
    queries, (k_ref, v_ref), outs = refs[:chunks], refs[chunks : chunks + 2], refs[chunks + 2 :]
    kv_heads, size = k_ref.shape[1], k_ref.shape[3]
    repeat = heads // kv_heads
    width = heads * size
    part = page // chunks
    tile = math.gcd(repeat, HEADS_PER_TILE)
    scale = size**-0.5 * math.log2(math.e)
    lane = lax.broadcasted_iota(jnp.int32, (page, LANES), 1)

    @pl.when(info[lb, 0] > 0)
    def _():
        shape = (tile * page, page)
        key_pos = info[lb, 1] * page + lax.broadcasted_iota(jnp.int32, shape, 1)
        query_pos = info[lb, 2] * page + plan.offsets(me, lb, shape)
        allowed = key_pos <= query_pos
        stats = jnp.zeros((page, LANES), F32)
        def product(first):
            q = jnp.concatenate(
                [m[:, h * size : (h + 1) * size] for h in range(first, first + tile) for m in queries], axis=0
            )
            return lax.dot_general(q, k_ref[lb, first // repeat], (((1,), (1,)), ((), ())), preferred_element_type=F32)

        ahead = product(0)
        for first in range(0, heads, tile):
            scores = scale * ahead
            if first + tile < heads:
                ahead = product(first + tile)
            scores = jnp.concatenate([jnp.where(allowed, scores[:, :page], FLOOR), scores[:, page:]], axis=1)
            peak = jnp.max(scores, axis=1, keepdims=True)
            weights = jnp.exp2(scores - peak).astype(BF16)
            both = jnp.dot(weights, v_ref[lb, first // repeat], preferred_element_type=F32)
            total = both[:, size:]
            out = (both[:, :size] / total).astype(BF16)
            lse = peak + jnp.log2(total)
            for i in range(tile):
                h = first + i
                stats = jnp.where(lane == h, lse[i * page : (i + 1) * page], stats)
                for c in range(chunks):
                    outs[c][:, h * size : (h + 1) * size] = out[i * page + c * part : i * page + (c + 1) * part]
        packed = pack_stats(stats, heads)
        for c in range(chunks):
            outs[c][:, width:] = packed[c * part : (c + 1) * part]

    @pl.when(info[lb, 0] == 0)
    def _():
        for c in range(chunks):
            outs[c][:, :width] = jnp.zeros((part, width), BF16)
            outs[c][:, width:] = pack_stats(jnp.full((part, LANES), FLOOR, F32), heads)


def attend(plan, heads, lb, pages, queries):
    keys, values, info = pages
    part = plan.page // plan.chunks
    shape = jax.ShapeDtypeStruct((part, queries[0].shape[1] + LANES), BF16)
    return pl.pallas_call(
        functools.partial(attend_kernel, plan, heads, lb),
        out_shape=(shape,) * plan.chunks,
        in_specs=[in_smem()] + [in_vmem()] * (len(queries) + 2),
        out_specs=(in_vmem(),) * plan.chunks,
        compiler_params=params(32),
        cost_estimate=pl.CostEstimate(flops=2 * 10**9, bytes_accessed=4 * 2**20, transcendentals=10**6),
    )(info, *queries, keys, values)


def merged(parts, stats):
    top = functools.reduce(jnp.maximum, stats)
    shares = [jnp.exp2(s - top) for s in stats]
    total = functools.reduce(jnp.add, shares)
    shares = [s / total for s in shares]

    def head(h):
        return functools.reduce(
            jnp.add, [p(h).astype(F32) * s[:, h : h + 1] for p, s in zip(parts, shares, strict=True)]
        )

    return head, top + jnp.log2(total)


def merge_kernel(heads, *refs):
    sources, out = refs[:-1], refs[-1]
    width = out.shape[1] - LANES
    size = width // heads
    head, lse = merged([heads_of(r, size) for r in sources], [unpack_stats(r[:, width:], heads) for r in sources])
    for h in range(heads):
        out[:, h * size : (h + 1) * size] = head(h).astype(BF16)
    out[:, width:] = pack_stats(lse, heads)


def merge(heads, *sources):
    return pl.pallas_call(
        functools.partial(merge_kernel, heads),
        out_shape=jax.ShapeDtypeStruct(sources[0].shape, BF16),
        in_specs=[in_vmem()] * len(sources),
        out_specs=in_vmem(),
        compiler_params=params(8),
    )(*sources)


def heads_of(ref, size):
    return lambda h: ref[:, h * size : (h + 1) * size]


def finish_kernel(heads, near, far, out):
    width = out.shape[1]
    size = width // heads
    head, _ = merged([heads_of(r, size) for r in (near, far)], [unpack_stats(r[:, width:], heads) for r in (near, far)])
    for h in range(heads):
        out[:, h * size : (h + 1) * size] = head(h).astype(BF16)


def finish(heads, near, far):
    return pl.pallas_call(
        functools.partial(finish_kernel, heads),
        out_shape=jax.ShapeDtypeStruct((near.shape[0], near.shape[1] - LANES), BF16),
        in_specs=[in_vmem()] * 2,
        out_specs=in_vmem(),
        compiler_params=params(8),
    )(near, far)


def project_kernel(plan, lb, *refs):
    sources, weight, (keep, send, rows_ref) = refs[: plan.group], refs[plan.group], refs[plan.group + 1 :]
    me, column = lax.axis_index("pages"), lax.axis_index("mp")
    rows = plan.rows
    holders = plan.group // 2
    for k in range(plan.group):
        device = me ^ k ^ (lb * plan.cross)
        place = ((device // holders % 2) ^ (column % 2)) * holders + device % holders
        rows_ref[pl.ds(pl.multiple_of(place * rows, rows), rows), :] = sources[k][...]
    product = jnp.dot(rows_ref[...], weight[...], preferred_element_type=F32)
    part = holders * rows
    keep[...] = product[:part]
    send[...] = product[part:].astype(BF16)


def project(plan, lb, sources, weight):
    columns = weight.shape[1]
    part = plan.page // 2
    return pl.pallas_call(
        functools.partial(project_kernel, plan, lb),
        out_shape=(jax.ShapeDtypeStruct((part, columns), F32), jax.ShapeDtypeStruct((part, columns), BF16)),
        in_specs=[in_vmem()] * (plan.group + 1),
        out_specs=(in_vmem(), in_vmem()),
        scratch_shapes=[VMEM((plan.page, weight.shape[0]), BF16)],
        compiler_params=params(24),
    )(*(sources[k] for k in range(plan.group)), weight)


def swap(x, axis, distance):
    n = lax.axis_size(axis)
    return lax.ppermute(x, axis, [(i, i ^ distance) for i in range(n)])


def others(plan):
    return range(1, plan.group)


def spread(x, plan):
    return {0: x} | {k: swap(x, "pages", k) for k in others(plan)}


def by_halves(plan, heads, queries, weight, pages):
    far = swap(queries, "pages", plan.cross)
    near = []
    for lb, rows in enumerate((queries, far)):
        chunks = spread(rows, plan)
        outs = attend(plan, heads, lb, pages, [chunks[k] for k in range(plan.group)])
        near.append(merge(heads, outs[0], *(swap(outs[k], "pages", k) for k in others(plan))))
    across = [swap(x, "pages", plan.cross) for x in near]
    sums = [None, None]
    for lb in (1, 0):
        rows = finish(heads, near[lb], across[1 - lb])
        keep, send = project(plan, lb, spread(rows, plan), weight)
        sums[lb] = keep + swap(send, "mp", 1).astype(F32)
    stays = plan.block(lax.axis_index("pages"), 0) == lax.axis_index("mp") // 2
    mine = jnp.where(stays, sums[0], sums[1])
    away = jnp.where(stays, sums[1], sums[0]).astype(BF16)
    return (mine + swap(away, "mp", 2).astype(F32)).astype(BF16)


def by_gathers(plan, heads, queries, weight, pages):
    width = queries.shape[1]
    size = width // heads
    gathered = lax.all_gather(queries, "pages", axis=0, tiled=True)
    rows = gathered.shape[0]
    outs = [
        attend(plan, heads, lb, pages, [gathered[lb * plan.page : (lb + 1) * plan.page]])[0]
        for lb in range(plan.blocks)
    ]
    out = jnp.concatenate(outs, axis=0)
    packed = out[:, width : width + 3 * heads].astype(F32)
    lse = packed[:, :heads] + packed[:, heads : 2 * heads] + packed[:, 2 * heads :]
    every = lax.all_gather(lse, "pages")
    top = jnp.max(every, axis=0)
    share = jnp.exp2(lse - top) / jnp.sum(jnp.exp2(every - top), axis=0)
    part = (out[:, :width].reshape(rows, heads, size).astype(F32) * share[..., None]).reshape(1, rows, width)
    received = lax.all_to_all(part.astype(BF16), "pages", split_axis=1, concat_axis=0, tiled=True)
    mixed = jnp.sum(received, axis=0, dtype=F32).astype(BF16)
    terms = jnp.dot(lax.all_gather(mixed, "pages", axis=0, tiled=True), weight, preferred_element_type=F32)
    return lax.psum_scatter(terms, "mp", scatter_dimension=0, tiled=True).astype(BF16)


def per_device(queries, cached_keys, cached_values, out_weight, select, page_table, block_page):
    n, ways = lax.axis_size("pages"), lax.axis_size("mp")
    plan = Plan(n, ways, queries.shape[0], select.shape[0], cached_keys.shape[1])
    heads = queries.shape[1] // cached_keys.shape[3]
    pages = fetch(plan, select, page_table, block_page, cached_keys, cached_values)
    way = by_halves if plan.halves else by_gathers
    return way(plan, heads, queries, out_weight, pages)


def solution(mesh):
    placed = (
        P("pages", "mp"),
        P("pages", None, "mp", None),
        P("pages", None, "mp", None),
        P("mp", "pages"),
        P(),
        P(),
        P(),
    )
    return jax.shard_map(
        per_device, mesh=mesh, in_specs=placed, out_specs=P("mp", "pages"), check_vma=False
    )
```

```python
import functools
import math

import jax
import jax.numpy as jnp
from jax import lax
from jax.experimental import pallas as pl
from jax.experimental.pallas import tpu as pltpu
from jax.sharding import PartitionSpec as P

PICKED_PAGES = 6
FLOOR = -1e30
LANES = 128
HEADS_PER_TILE = 2

VMEM = pltpu.VMEM
SMEM = pltpu.SMEM
BF16 = jnp.bfloat16
F32 = jnp.float32


def in_vmem():
    return pl.BlockSpec(memory_space=VMEM)


def in_smem():
    return pl.BlockSpec(memory_space=SMEM)


def params(mib):
    return pltpu.CompilerParams(vmem_limit_bytes=mib * 2**20)


class Plan:
    def __init__(self, n, ways, rows, blocks, page):
        self.n, self.ways, self.rows, self.blocks, self.page = n, ways, rows, blocks, page
        self.group = n // blocks
        self.halves = blocks == 2 and n == 8 and ways == 4 and rows * self.group == page
        self.cross = n * 3 // 4

    def block(self, me, lb):
        return (me // self.group) ^ lb if self.halves else lb

    def holder(self, me, column, lb, chunk):
        turned = chunk // 2 + chunk % 2 * 2
        return me ^ (lb * self.cross) ^ jnp.where(column % 2 == 0, turned, chunk)

    def offsets(self, me, lb, shape):
        row = lax.broadcasted_iota(jnp.int32, shape, 0) % self.page
        if not self.halves:
            return row
        holder = self.holder(me, lax.axis_index("mp"), lb, row // self.rows)
        return holder % self.group * self.rows + row % self.rows

    def swap(self, x, turn):
        pairs = [
            (p * self.ways + m, (p ^ (1 + (m + turn) % 2)) * self.ways + m)
            for p in range(self.n)
            for m in range(self.ways)
        ]
        return lax.ppermute(x, ("pages", "mp"), pairs)


def fetch_kernel(plan, pages_dev, *refs):
    select_hbm, table_hbm, stands_hbm, queries, keys, values, k_out, v_out, info, q_out = refs[:10]
    select, table, stands, rows, k_buf, v_buf, sems, int_sems = refs[10:]
    me = lax.axis_index("pages")
    blocks, heads = k_out.shape[:2]
    span = k_buf.shape[1]
    page = span // heads
    picked = k_out.shape[2] // page
    low = me * pages_dev
    loads = [
        pltpu.make_async_copy(a, b, int_sems.at[i])
        for i, (a, b) in enumerate(((select_hbm, select), (table_hbm, table), (stands_hbm, stands), (queries, q_out.at[: queries.shape[0]])))
    ]
    whole = [
        pltpu.make_async_copy(a, b, sems.at[i]) for i, (a, b) in enumerate(((keys, k_buf), (values, v_buf)))
    ]
    for load in loads + whole:
        load.start()
    row = lax.broadcasted_iota(jnp.int32, (span, span), 0)
    column = lax.broadcasted_iota(jnp.int32, (span, span), 1)
    apart = (column == (row % page) * heads + row // page).astype(F32).astype(BF16)
    for load in loads[:3]:
        load.wait()
    for lb in range(blocks):
        block = plan.block(me, lb)
        stand = stands[block]
        info[lb, 1] = plan.n * pages_dev
        info[lb, 2] = stand
        others = jnp.int32(0)
        count = jnp.int32(0)
        for i in range(select.shape[1]):
            logical = select[block, i]
            local = table[logical] - low
            mine = (local >= 0) & (local < pages_dev)
            own = logical == stand
            slot = jnp.where(own, 0, jnp.maximum(picked - 1 - others, 0))
            slot = jnp.where(mine, slot, picked)
            rows[lb, slot] = local
            rows[blocks + lb, slot] = logical
            one = mine.astype(jnp.int32)
            others = others + jnp.where(own, 0, one)
            count = count + one
        info[lb, 0] = count
        info[lb, 1] = rows[blocks + lb, 0]

    for load in whole:
        load.wait()
    for lb in range(blocks):

        @pl.when(info[lb, 0] > 0)
        def _(lb=lb):
            for g in range(heads):
                v_out[lb, g, :, LANES:] = jnp.ones((picked * page, LANES), BF16)
            for slot in range(picked):
                local = jnp.clip(rows[lb, slot], 0, pages_dev - 1)
                both = jnp.concatenate([k_buf[local], v_buf[local]], axis=1)
                split = jnp.dot(apart, both, preferred_element_type=F32).astype(BF16)
                for g in range(heads):
                    here = slice(slot * page, (slot + 1) * page)
                    k_out[lb, g, here, :] = split[g * page : (g + 1) * page, :LANES]
                    v_out[lb, g, here, :LANES] = split[g * page : (g + 1) * page, LANES:]
    loads[3].wait()


def fetch(plan, select, table, stands, queries, keys, values):
    pages_dev, page, heads, size = keys.shape
    blocks, picked = select.shape[0], PICKED_PAGES
    span = page * heads
    flat = (pages_dev, span, size)
    operands = (select, table, stands, queries, keys.reshape(flat), values.reshape(flat))
    return pl.pallas_call(
        functools.partial(fetch_kernel, plan, pages_dev),
        out_shape=(
            jax.ShapeDtypeStruct((blocks, heads, picked * page, size), BF16),
            jax.ShapeDtypeStruct((blocks, heads, picked * page, size + LANES), BF16),
            jax.ShapeDtypeStruct((blocks, 3), jnp.int32),
            jax.ShapeDtypeStruct((2 * queries.shape[0], queries.shape[1]), queries.dtype),
        ),
        in_specs=[pl.BlockSpec(memory_space=pltpu.HBM)] * len(operands),
        out_specs=(in_vmem(), in_vmem(), in_smem(), in_vmem()),
        scratch_shapes=[
            SMEM(select.shape, jnp.int32),
            SMEM(table.shape, jnp.int32),
            SMEM(stands.shape, jnp.int32),
            SMEM((2 * blocks, picked + 1), jnp.int32),
            VMEM((pages_dev, span, size), BF16),
            VMEM((pages_dev, span, size), BF16),
            pltpu.SemaphoreType.DMA((2,)),
            pltpu.SemaphoreType.DMA((4,)),
        ],
        compiler_params=params(16),
        cost_estimate=pl.CostEstimate(flops=2 * 10**9, bytes_accessed=8 * 2**20, transcendentals=0),
    )(*(pltpu.with_memory_space_constraint(x, pltpu.HBM) for x in operands))


def pack_stats(lse, heads):
    lane = lax.broadcasted_iota(jnp.int32, lse.shape, 1)
    high = lse.astype(BF16).astype(F32)
    rest = lse - high
    middle = rest.astype(BF16).astype(F32)
    low = rest - middle
    packed = jnp.where(lane < heads, high, 0.0)
    packed = packed + jnp.where((lane >= heads) & (lane < 2 * heads), pltpu.roll(middle, heads, 1), 0.0)
    packed = packed + jnp.where((lane >= 2 * heads) & (lane < 3 * heads), pltpu.roll(low, 2 * heads, 1), 0.0)
    return packed.astype(BF16)


def unpack_stats(packed, heads):
    wide = packed.astype(F32)
    return wide + pltpu.roll(wide, LANES - heads, 1) + pltpu.roll(wide, LANES - 2 * heads, 1)


def attend_kernel(plan, heads, lb, info, *refs):
    me = lax.axis_index("pages")
    chunks, page = len(refs) // 2 - 1, plan.page
    queries, (k_ref, v_ref), outs = refs[:chunks], refs[chunks : chunks + 2], refs[chunks + 2 :]
    kv_heads, size = k_ref.shape[1], k_ref.shape[3]
    repeat = heads // kv_heads
    width = heads * size
    part = page // chunks
    tile = math.gcd(repeat, HEADS_PER_TILE)
    scale = size**-0.5 * math.log2(math.e)
    lane = lax.broadcasted_iota(jnp.int32, (page, LANES), 1)

    @pl.when(info[lb, 0] > 0)
    def _():
        shape = (tile * page, page)
        key_pos = info[lb, 1] * page + lax.broadcasted_iota(jnp.int32, shape, 1)
        query_pos = info[lb, 2] * page + plan.offsets(me, lb, shape)
        allowed = key_pos <= query_pos
        stats = jnp.zeros((page, LANES), F32)
        def product(first):
            q = jnp.concatenate(
                [m[:, h * size : (h + 1) * size] for h in range(first, first + tile) for m in queries], axis=0
            )
            return lax.dot_general(q, k_ref[lb, first // repeat], (((1,), (1,)), ((), ())), preferred_element_type=F32)

        ahead = product(0)
        for first in range(0, heads, tile):
            scores = scale * ahead
            if first + tile < heads:
                ahead = product(first + tile)
            scores = jnp.concatenate([jnp.where(allowed, scores[:, :page], FLOOR), scores[:, page:]], axis=1)
            peak = jnp.max(scores, axis=1, keepdims=True)
            weights = jnp.exp2(scores - peak).astype(BF16)
            both = jnp.dot(weights, v_ref[lb, first // repeat], preferred_element_type=F32)
            total = both[:, size:]
            out = (both[:, :size] / total).astype(BF16)
            lse = peak + jnp.log2(total)
            for i in range(tile):
                h = first + i
                stats = jnp.where(lane == h, lse[i * page : (i + 1) * page], stats)
                for c in range(chunks):
                    outs[c][:, h * size : (h + 1) * size] = out[i * page + c * part : i * page + (c + 1) * part]
        packed = pack_stats(stats, heads)
        for c in range(chunks):
            outs[c][:, width:] = packed[c * part : (c + 1) * part]

    @pl.when(info[lb, 0] == 0)
    def _():
        for c in range(chunks):
            outs[c][:, :width] = jnp.zeros((part, width), BF16)
            outs[c][:, width:] = pack_stats(jnp.full((part, LANES), FLOOR, F32), heads)


def attend(plan, heads, lb, pages, queries):
    keys, values, info, _ = pages
    part = plan.page // len(queries)
    shape = jax.ShapeDtypeStruct((part, queries[0].shape[1] + LANES), BF16)
    return pl.pallas_call(
        functools.partial(attend_kernel, plan, heads, lb),
        out_shape=(shape,) * len(queries),
        in_specs=[in_smem()] + [in_vmem()] * (len(queries) + 2),
        out_specs=(in_vmem(),) * len(queries),
        compiler_params=params(32),
        cost_estimate=pl.CostEstimate(flops=2 * 10**9, bytes_accessed=4 * 2**20, transcendentals=10**6),
    )(info, *queries, keys, values)


def merged(parts, stats):
    top = functools.reduce(jnp.maximum, stats)
    shares = [jnp.exp2(s - top) for s in stats]
    total = functools.reduce(jnp.add, shares)
    shares = [s / total for s in shares]

    def head(h):
        return functools.reduce(
            jnp.add, [p(h).astype(F32) * s[:, h : h + 1] for p, s in zip(parts, shares, strict=True)]
        )

    return head, top + jnp.log2(total)


def heads_of(ref, size):
    return lambda h: ref[:, h * size : (h + 1) * size]


def merge_kernel(heads, first, second, *outs):
    width = first.shape[1] - LANES
    size = width // heads
    part = outs[0].shape[0]
    sources = (first, second)
    head, lse = merged([heads_of(r, size) for r in sources], [unpack_stats(r[:, width:], heads) for r in sources])
    for h in range(heads):
        block = head(h).astype(BF16)
        for i, out in enumerate(outs):
            out[:, h * size : (h + 1) * size] = block[i * part : (i + 1) * part]
    packed = pack_stats(lse, heads)
    for i, out in enumerate(outs):
        out[:, width:] = packed[i * part : (i + 1) * part]


def merge(heads, first, second, parts):
    rows, wide = first.shape
    return pl.pallas_call(
        functools.partial(merge_kernel, heads),
        out_shape=(jax.ShapeDtypeStruct((rows // parts, wide), BF16),) * parts,
        in_specs=[in_vmem()] * 2,
        out_specs=(in_vmem(),) * parts,
        compiler_params=params(8),
    )(first, second)


def finish_kernel(heads, near, far, out):
    width = out.shape[1]
    size = width // heads
    head, _ = merged([heads_of(r, size) for r in (near, far)], [unpack_stats(r[:, width:], heads) for r in (near, far)])
    for h in range(heads):
        out[:, h * size : (h + 1) * size] = head(h).astype(BF16)


def finish(heads, near, far):
    return pl.pallas_call(
        functools.partial(finish_kernel, heads),
        out_shape=jax.ShapeDtypeStruct((near.shape[0], near.shape[1] - LANES), BF16),
        in_specs=[in_vmem()] * 2,
        out_specs=in_vmem(),
        compiler_params=params(8),
    )(near, far)


def project_kernel(plan, lb, *refs):
    sources, (weight, keep, send, rows_ref) = refs[:-4], refs[-4:]
    me, column = lax.axis_index("pages"), lax.axis_index("mp")
    rows = plan.rows
    holders = plan.group // 2
    for chunk in range(plan.group):
        device = plan.holder(me, column, lb, chunk)
        place = ((device // holders % 2) ^ (column % 2)) * holders + device % holders
        here = slice(chunk % 2 * rows, (chunk % 2 + 1) * rows)
        rows_ref[pl.ds(pl.multiple_of(place * rows, rows), rows), :] = sources[chunk // 2][here, :]
    product = jnp.dot(rows_ref[...], weight[...], preferred_element_type=F32)
    part = holders * rows
    keep[...] = product[:part]
    send[...] = product[part:].astype(BF16)


def project(plan, lb, sources, weight):
    columns = weight.shape[1]
    part = plan.page // 2
    return pl.pallas_call(
        functools.partial(project_kernel, plan, lb),
        out_shape=(jax.ShapeDtypeStruct((part, columns), F32), jax.ShapeDtypeStruct((part, columns), BF16)),
        in_specs=[in_vmem()] * (len(sources) + 1),
        out_specs=(in_vmem(), in_vmem()),
        scratch_shapes=[VMEM((plan.page, weight.shape[0]), BF16)],
        compiler_params=params(24),
    )(*sources, weight)


def swap(x, axis, distance):
    n = lax.axis_size(axis)
    return lax.ppermute(x, axis, [(i, i ^ distance) for i in range(n)])


def spread(x, plan, pair=None):
    arrived = plan.swap(x, 1)
    if pair is None:
        pair = jnp.concatenate([x, arrived], axis=0)
    else:
        pair = lax.dynamic_update_slice(pair, arrived, (x.shape[0], 0))
    return [pair, plan.swap(pair, 0)]


def gathered(plan, heads, outs):
    keep, send = outs
    stay, go = merge(heads, keep, plan.swap(send, 0), 2)
    return merge(heads, stay, plan.swap(go, 1), 1)[0]


def by_halves(plan, heads, queries, weight, pages):
    far = swap(queries, "pages", plan.cross)
    near = [
        gathered(plan, heads, attend(plan, heads, lb, pages, spread(x, plan, pair)))
        for lb, (x, pair) in enumerate(((queries, pages[3]), (far, None)))
    ]
    across = [swap(x, "pages", plan.cross) for x in near]
    sums = [None, None]
    for lb in (1, 0):
        rows = finish(heads, near[lb], across[1 - lb])
        keep, send = project(plan, lb, spread(rows, plan), weight)
        sums[lb] = keep + swap(send, "mp", 1).astype(F32)
    stays = plan.block(lax.axis_index("pages"), 0) == lax.axis_index("mp") // 2
    mine = jnp.where(stays, sums[0], sums[1])
    away = jnp.where(stays, sums[1], sums[0]).astype(BF16)
    return (mine + swap(away, "mp", 2).astype(F32)).astype(BF16)


def by_gathers(plan, heads, queries, weight, pages):
    width = queries.shape[1]
    size = width // heads
    every = lax.all_gather(queries, "pages", axis=0, tiled=True)
    rows = every.shape[0]
    outs = [
        attend(plan, heads, lb, pages, [every[lb * plan.page : (lb + 1) * plan.page]])[0]
        for lb in range(plan.blocks)
    ]
    out = jnp.concatenate(outs, axis=0)
    packed = out[:, width : width + 3 * heads].astype(F32)
    lse = packed[:, :heads] + packed[:, heads : 2 * heads] + packed[:, 2 * heads :]
    stats = lax.all_gather(lse, "pages")
    top = jnp.max(stats, axis=0)
    share = jnp.exp2(lse - top) / jnp.sum(jnp.exp2(stats - top), axis=0)
    part = (out[:, :width].reshape(rows, heads, size).astype(F32) * share[..., None]).reshape(1, rows, width)
    received = lax.all_to_all(part.astype(BF16), "pages", split_axis=1, concat_axis=0, tiled=True)
    mixed = jnp.sum(received, axis=0, dtype=F32).astype(BF16)
    terms = jnp.dot(lax.all_gather(mixed, "pages", axis=0, tiled=True), weight, preferred_element_type=F32)
    return lax.psum_scatter(terms, "mp", scatter_dimension=0, tiled=True).astype(BF16)


def per_device(queries, cached_keys, cached_values, out_weight, select, page_table, block_page):
    n, ways = lax.axis_size("pages"), lax.axis_size("mp")
    plan = Plan(n, ways, queries.shape[0], select.shape[0], cached_keys.shape[1])
    heads = queries.shape[1] // cached_keys.shape[3]
    pages = fetch(plan, select, page_table, block_page, queries, cached_keys, cached_values)
    way = by_halves if plan.halves else by_gathers
    return way(plan, heads, queries, out_weight, pages)


def solution(mesh):
    placed = (
        P("pages", "mp"),
        P("pages", None, "mp", None),
        P("pages", None, "mp", None),
        P("mp", "pages"),
        P(),
        P(),
        P(),
    )
    return jax.shard_map(
        per_device, mesh=mesh, in_specs=placed, out_specs=P("mp", "pages"), check_vma=False
    )
```

```python
import functools
import math

import jax
import jax.numpy as jnp
from jax import lax
from jax.experimental import pallas as pl
from jax.experimental.pallas import tpu as pltpu
from jax.sharding import PartitionSpec as P

PICKED_PAGES = 6
FLOOR = -1e30
LANES = 128
HEADS_PER_TILE = 2

VMEM = pltpu.VMEM
SMEM = pltpu.SMEM
BF16 = jnp.bfloat16
F32 = jnp.float32


def in_vmem():
    return pl.BlockSpec(memory_space=VMEM)


def in_smem():
    return pl.BlockSpec(memory_space=SMEM)


def params(mib):
    return pltpu.CompilerParams(vmem_limit_bytes=mib * 2**20)


class Plan:
    def __init__(self, n, ways, rows, blocks, page):
        self.n, self.ways, self.rows, self.blocks, self.page = n, ways, rows, blocks, page
        self.group = n // blocks
        self.halves = blocks == 2 and n == 8 and ways == 4 and rows * self.group == page
        self.cross = n * 3 // 4
        self.chunks = self.group if self.halves else 1

    def block(self, me, lb):
        return (me // self.group) ^ lb if self.halves else lb

    def holder(self, me, column, lb, chunk):
        turned = chunk // 2 + chunk % 2 * 2
        return me ^ (lb * self.cross) ^ jnp.where(column % 2 == 0, chunk, turned)

    def offsets(self, me, lb, shape):
        row = lax.broadcasted_iota(jnp.int32, shape, 0) % self.page
        if not self.halves:
            return row
        holder = self.holder(me, lax.axis_index("mp"), lb, row // self.rows)
        return holder % self.group * self.rows + row % self.rows

    def swap(self, x, chunk):
        pairs = []
        for p in range(self.n):
            for m in range(self.ways):
                turned = chunk // 2 + chunk % 2 * 2
                pairs.append((p * self.ways + m, (p ^ (turned if m % 2 else chunk)) * self.ways + m))
        return lax.ppermute(x, ("pages", "mp"), pairs)


def fetch_kernel(plan, pages_dev, select_hbm, table_hbm, stands_hbm, keys, values, k_out, v_out, info, select, table, stands, rows, k_buf, v_buf, sems, int_sems):
    me = lax.axis_index("pages")
    blocks, heads = k_out.shape[:2]
    span = k_buf.shape[1]
    page = span // heads
    picked = k_out.shape[2] // page
    low = me * pages_dev
    loads = [
        pltpu.make_async_copy(a, b, int_sems.at[i])
        for i, (a, b) in enumerate(((select_hbm, select), (table_hbm, table), (stands_hbm, stands)))
    ]
    whole = [
        pltpu.make_async_copy(a, b, sems.at[i]) for i, (a, b) in enumerate(((keys, k_buf), (values, v_buf)))
    ]
    for load in loads + whole:
        load.start()
    row = lax.broadcasted_iota(jnp.int32, (span, span), 0)
    column = lax.broadcasted_iota(jnp.int32, (span, span), 1)
    apart = (column == (row % page) * heads + row // page).astype(F32).astype(BF16)
    for load in loads:
        load.wait()
    for lb in range(blocks):
        block = plan.block(me, lb)
        stand = stands[block]
        info[lb, 1] = plan.n * pages_dev
        info[lb, 2] = stand
        others = jnp.int32(0)
        count = jnp.int32(0)
        for i in range(select.shape[1]):
            logical = select[block, i]
            local = table[logical] - low
            mine = (local >= 0) & (local < pages_dev)
            own = logical == stand
            slot = jnp.where(own, 0, jnp.maximum(picked - 1 - others, 0))
            slot = jnp.where(mine, slot, picked)
            rows[lb, slot] = local
            rows[blocks + lb, slot] = logical
            one = mine.astype(jnp.int32)
            others = others + jnp.where(own, 0, one)
            count = count + one
        info[lb, 0] = count
        info[lb, 1] = rows[blocks + lb, 0]

    for load in whole:
        load.wait()
    for lb in range(blocks):

        @pl.when(info[lb, 0] > 0)
        def _(lb=lb):
            for g in range(heads):
                v_out[lb, g, :, LANES:] = jnp.ones((picked * page, LANES), BF16)
            for slot in range(picked):
                local = jnp.clip(rows[lb, slot], 0, pages_dev - 1)
                both = jnp.concatenate([k_buf[local], v_buf[local]], axis=1)
                split = jnp.dot(apart, both, preferred_element_type=F32).astype(BF16)
                for g in range(heads):
                    here = slice(slot * page, (slot + 1) * page)
                    k_out[lb, g, here, :] = split[g * page : (g + 1) * page, :LANES]
                    v_out[lb, g, here, :LANES] = split[g * page : (g + 1) * page, LANES:]


def fetch(plan, select, table, stands, keys, values):
    pages_dev, page, heads, size = keys.shape
    blocks, picked = select.shape[0], PICKED_PAGES
    span = page * heads
    return pl.pallas_call(
        functools.partial(fetch_kernel, plan, pages_dev),
        out_shape=(
            jax.ShapeDtypeStruct((blocks, heads, picked * page, size), BF16),
            jax.ShapeDtypeStruct((blocks, heads, picked * page, size + LANES), BF16),
            jax.ShapeDtypeStruct((blocks, 3), jnp.int32),
        ),
        in_specs=[pl.BlockSpec(memory_space=pltpu.HBM)] * 5,
        out_specs=(in_vmem(), in_vmem(), in_smem()),
        scratch_shapes=[
            SMEM(select.shape, jnp.int32),
            SMEM(table.shape, jnp.int32),
            SMEM(stands.shape, jnp.int32),
            SMEM((2 * blocks, picked + 1), jnp.int32),
            VMEM((pages_dev, span, size), BF16),
            VMEM((pages_dev, span, size), BF16),
            pltpu.SemaphoreType.DMA((2,)),
            pltpu.SemaphoreType.DMA((3,)),
        ],
        compiler_params=params(16),
        cost_estimate=pl.CostEstimate(flops=2 * 10**9, bytes_accessed=8 * 2**20, transcendentals=0),
    )(*(pltpu.with_memory_space_constraint(x, pltpu.HBM) for x in (select, table, stands, keys.reshape(pages_dev, span, size), values.reshape(pages_dev, span, size))))


def pack_stats(lse, heads):
    lane = lax.broadcasted_iota(jnp.int32, lse.shape, 1)
    high = lse.astype(BF16).astype(F32)
    rest = lse - high
    middle = rest.astype(BF16).astype(F32)
    low = rest - middle
    packed = jnp.where(lane < heads, high, 0.0)
    packed = packed + jnp.where((lane >= heads) & (lane < 2 * heads), pltpu.roll(middle, heads, 1), 0.0)
    packed = packed + jnp.where((lane >= 2 * heads) & (lane < 3 * heads), pltpu.roll(low, 2 * heads, 1), 0.0)
    return packed.astype(BF16)


def unpack_stats(packed, heads):
    wide = packed.astype(F32)
    return wide + pltpu.roll(wide, LANES - heads, 1) + pltpu.roll(wide, LANES - 2 * heads, 1)


def attend_kernel(plan, heads, lb, info, *refs):
    me = lax.axis_index("pages")
    chunks, page = plan.chunks, plan.page
    queries, (k_ref, v_ref), outs = refs[:chunks], refs[chunks : chunks + 2], refs[chunks + 2 :]
    kv_heads, size = k_ref.shape[1], k_ref.shape[3]
    repeat = heads // kv_heads
    width = heads * size
    part = page // chunks
    tile = math.gcd(repeat, HEADS_PER_TILE)
    scale = size**-0.5 * math.log2(math.e)
    lane = lax.broadcasted_iota(jnp.int32, (page, LANES), 1)

    @pl.when(info[lb, 0] > 0)
    def _():
        shape = (tile * page, page)
        key_pos = info[lb, 1] * page + lax.broadcasted_iota(jnp.int32, shape, 1)
        query_pos = info[lb, 2] * page + plan.offsets(me, lb, shape)
        allowed = key_pos <= query_pos
        stats = jnp.zeros((page, LANES), F32)
        def product(first):
            q = jnp.concatenate(
                [m[:, h * size : (h + 1) * size] for h in range(first, first + tile) for m in queries], axis=0
            )
            return lax.dot_general(q, k_ref[lb, first // repeat], (((1,), (1,)), ((), ())), preferred_element_type=F32)

        ahead = product(0)
        for first in range(0, heads, tile):
            scores = scale * ahead
            if first + tile < heads:
                ahead = product(first + tile)
            scores = jnp.concatenate([jnp.where(allowed, scores[:, :page], FLOOR), scores[:, page:]], axis=1)
            peak = jnp.max(scores, axis=1, keepdims=True)
            weights = jnp.exp2(scores - peak).astype(BF16)
            both = jnp.dot(weights, v_ref[lb, first // repeat], preferred_element_type=F32)
            total = both[:, size:]
            out = (both[:, :size] / total).astype(BF16)
            lse = peak + jnp.log2(total)
            for i in range(tile):
                h = first + i
                stats = jnp.where(lane == h, lse[i * page : (i + 1) * page], stats)
                for c in range(chunks):
                    outs[c][:, h * size : (h + 1) * size] = out[i * page + c * part : i * page + (c + 1) * part]
        packed = pack_stats(stats, heads)
        for c in range(chunks):
            outs[c][:, width:] = packed[c * part : (c + 1) * part]

    @pl.when(info[lb, 0] == 0)
    def _():
        for c in range(chunks):
            outs[c][:, :width] = jnp.zeros((part, width), BF16)
            outs[c][:, width:] = pack_stats(jnp.full((part, LANES), FLOOR, F32), heads)


def attend(plan, heads, lb, pages, queries):
    keys, values, info = pages
    part = plan.page // plan.chunks
    shape = jax.ShapeDtypeStruct((part, queries[0].shape[1] + LANES), BF16)
    return pl.pallas_call(
        functools.partial(attend_kernel, plan, heads, lb),
        out_shape=(shape,) * plan.chunks,
        in_specs=[in_smem()] + [in_vmem()] * (len(queries) + 2),
        out_specs=(in_vmem(),) * plan.chunks,
        compiler_params=params(32),
        cost_estimate=pl.CostEstimate(flops=2 * 10**9, bytes_accessed=4 * 2**20, transcendentals=10**6),
    )(info, *queries, keys, values)


def merged(parts, stats):
    top = functools.reduce(jnp.maximum, stats)
    shares = [jnp.exp2(s - top) for s in stats]
    total = functools.reduce(jnp.add, shares)
    shares = [s / total for s in shares]

    def head(h):
        return functools.reduce(
            jnp.add, [p(h).astype(F32) * s[:, h : h + 1] for p, s in zip(parts, shares, strict=True)]
        )

    return head, top + jnp.log2(total)


def merge_kernel(heads, *refs):
    sources, out = refs[:-1], refs[-1]
    width = out.shape[1] - LANES
    size = width // heads
    head, lse = merged([heads_of(r, size) for r in sources], [unpack_stats(r[:, width:], heads) for r in sources])
    for h in range(heads):
        out[:, h * size : (h + 1) * size] = head(h).astype(BF16)
    out[:, width:] = pack_stats(lse, heads)


def merge(heads, *sources):
    return pl.pallas_call(
        functools.partial(merge_kernel, heads),
        out_shape=jax.ShapeDtypeStruct(sources[0].shape, BF16),
        in_specs=[in_vmem()] * len(sources),
        out_specs=in_vmem(),
        compiler_params=params(8),
    )(*sources)


def heads_of(ref, size):
    return lambda h: ref[:, h * size : (h + 1) * size]


def finish_kernel(heads, near, far, out):
    width = out.shape[1]
    size = width // heads
    head, _ = merged([heads_of(r, size) for r in (near, far)], [unpack_stats(r[:, width:], heads) for r in (near, far)])
    for h in range(heads):
        out[:, h * size : (h + 1) * size] = head(h).astype(BF16)


def finish(heads, near, far):
    return pl.pallas_call(
        functools.partial(finish_kernel, heads),
        out_shape=jax.ShapeDtypeStruct((near.shape[0], near.shape[1] - LANES), BF16),
        in_specs=[in_vmem()] * 2,
        out_specs=in_vmem(),
        compiler_params=params(8),
    )(near, far)


def project_kernel(plan, lb, *refs):
    sources, weight, (keep, send, rows_ref) = refs[: plan.group], refs[plan.group], refs[plan.group + 1 :]
    me, column = lax.axis_index("pages"), lax.axis_index("mp")
    rows = plan.rows
    holders = plan.group // 2
    for k in range(plan.group):
        device = plan.holder(me, column, lb, k)
        place = ((device // holders % 2) ^ (column % 2)) * holders + device % holders
        rows_ref[pl.ds(pl.multiple_of(place * rows, rows), rows), :] = sources[k][...]
    product = jnp.dot(rows_ref[...], weight[...], preferred_element_type=F32)
    part = holders * rows
    keep[...] = product[:part]
    send[...] = product[part:].astype(BF16)


def project(plan, lb, sources, weight):
    columns = weight.shape[1]
    part = plan.page // 2
    return pl.pallas_call(
        functools.partial(project_kernel, plan, lb),
        out_shape=(jax.ShapeDtypeStruct((part, columns), F32), jax.ShapeDtypeStruct((part, columns), BF16)),
        in_specs=[in_vmem()] * (plan.group + 1),
        out_specs=(in_vmem(), in_vmem()),
        scratch_shapes=[VMEM((plan.page, weight.shape[0]), BF16)],
        compiler_params=params(24),
    )(*(sources[k] for k in range(plan.group)), weight)


def swap(x, axis, distance):
    n = lax.axis_size(axis)
    return lax.ppermute(x, axis, [(i, i ^ distance) for i in range(n)])


def others(plan):
    return range(1, plan.group)


def spread(x, plan):
    return {0: x} | {k: plan.swap(x, k) for k in others(plan)}


def by_halves(plan, heads, queries, weight, pages):
    far = swap(queries, "pages", plan.cross)
    near = []
    for lb, rows in enumerate((queries, far)):
        chunks = spread(rows, plan)
        outs = attend(plan, heads, lb, pages, [chunks[k] for k in range(plan.group)])
        near.append(merge(heads, outs[0], *(plan.swap(outs[k], k) for k in others(plan))))
    across = [swap(x, "pages", plan.cross) for x in near]
    sums = [None, None]
    for lb in (1, 0):
        rows = finish(heads, near[lb], across[1 - lb])
        keep, send = project(plan, lb, spread(rows, plan), weight)
        sums[lb] = keep + swap(send, "mp", 1).astype(F32)
    stays = plan.block(lax.axis_index("pages"), 0) == lax.axis_index("mp") // 2
    mine = jnp.where(stays, sums[0], sums[1])
    away = jnp.where(stays, sums[1], sums[0]).astype(BF16)
    return (mine + swap(away, "mp", 2).astype(F32)).astype(BF16)


def by_gathers(plan, heads, queries, weight, pages):
    width = queries.shape[1]
    size = width // heads
    gathered = lax.all_gather(queries, "pages", axis=0, tiled=True)
    rows = gathered.shape[0]
    outs = [
        attend(plan, heads, lb, pages, [gathered[lb * plan.page : (lb + 1) * plan.page]])[0]
        for lb in range(plan.blocks)
    ]
    out = jnp.concatenate(outs, axis=0)
    packed = out[:, width : width + 3 * heads].astype(F32)
    lse = packed[:, :heads] + packed[:, heads : 2 * heads] + packed[:, 2 * heads :]
    every = lax.all_gather(lse, "pages")
    top = jnp.max(every, axis=0)
    share = jnp.exp2(lse - top) / jnp.sum(jnp.exp2(every - top), axis=0)
    part = (out[:, :width].reshape(rows, heads, size).astype(F32) * share[..., None]).reshape(1, rows, width)
    received = lax.all_to_all(part.astype(BF16), "pages", split_axis=1, concat_axis=0, tiled=True)
    mixed = jnp.sum(received, axis=0, dtype=F32).astype(BF16)
    terms = jnp.dot(lax.all_gather(mixed, "pages", axis=0, tiled=True), weight, preferred_element_type=F32)
    return lax.psum_scatter(terms, "mp", scatter_dimension=0, tiled=True).astype(BF16)


def per_device(queries, cached_keys, cached_values, out_weight, select, page_table, block_page):
    n, ways = lax.axis_size("pages"), lax.axis_size("mp")
    plan = Plan(n, ways, queries.shape[0], select.shape[0], cached_keys.shape[1])
    heads = queries.shape[1] // cached_keys.shape[3]
    pages = fetch(plan, select, page_table, block_page, cached_keys, cached_values)
    way = by_halves if plan.halves else by_gathers
    return way(plan, heads, queries, out_weight, pages)


def solution(mesh):
    placed = (
        P("pages", "mp"),
        P("pages", None, "mp", None),
        P("pages", None, "mp", None),
        P("mp", "pages"),
        P(),
        P(),
        P(),
    )
    return jax.shard_map(
        per_device, mesh=mesh, in_specs=placed, out_specs=P("mp", "pages"), check_vma=False
    )
```

```python
import functools
import math

import jax
import jax.numpy as jnp
from jax import lax
from jax.experimental import pallas as pl
from jax.experimental.pallas import tpu as pltpu
from jax.sharding import PartitionSpec as P

PICKED_PAGES = 6
FLOOR = -1e30
LANES = 128
HEADS_PER_TILE = 2

VMEM = pltpu.VMEM
SMEM = pltpu.SMEM
BF16 = jnp.bfloat16
F32 = jnp.float32


def in_vmem():
    return pl.BlockSpec(memory_space=VMEM)


def in_smem():
    return pl.BlockSpec(memory_space=SMEM)


def params(mib):
    return pltpu.CompilerParams(vmem_limit_bytes=mib * 2**20)


class Plan:
    def __init__(self, n, ways, rows, blocks, page):
        self.n, self.rows, self.blocks, self.page = n, rows, blocks, page
        self.group = n // blocks
        self.halves = blocks == 2 and n == 8 and ways == 4 and rows * self.group == page
        self.cross = n * 3 // 4
        self.chunks = self.group if self.halves else 1

    def block(self, me, lb):
        return (me // self.group) ^ lb if self.halves else lb

    def offsets(self, me, lb, shape):
        row = lax.broadcasted_iota(jnp.int32, shape, 0) % self.page
        if not self.halves:
            return row
        mine = (me ^ (lb * self.cross)) % self.group
        return ((row // self.rows) ^ mine) * self.rows + row % self.rows


def fetch_kernel(plan, pages_dev, select_hbm, table_hbm, stands_hbm, keys, values, k_out, v_out, info, select, table, stands, rows, k_buf, v_buf, sems, int_sems):
    me = lax.axis_index("pages")
    blocks, heads = k_out.shape[:2]
    span = k_buf.shape[1]
    page = span // heads
    picked = k_out.shape[2] // page
    low = me * pages_dev
    loads = [
        pltpu.make_async_copy(a, b, int_sems.at[i])
        for i, (a, b) in enumerate(((select_hbm, select), (table_hbm, table), (stands_hbm, stands)))
    ]
    whole = [
        pltpu.make_async_copy(a, b, sems.at[i]) for i, (a, b) in enumerate(((keys, k_buf), (values, v_buf)))
    ]
    for load in loads + whole:
        load.start()
    row = lax.broadcasted_iota(jnp.int32, (span, span), 0)
    column = lax.broadcasted_iota(jnp.int32, (span, span), 1)
    apart = (column == (row % page) * heads + row // page).astype(F32).astype(BF16)
    for load in loads:
        load.wait()
    for lb in range(blocks):
        block = plan.block(me, lb)
        stand = stands[block]
        info[lb, 1] = plan.n * pages_dev
        info[lb, 2] = stand
        others = jnp.int32(0)
        count = jnp.int32(0)
        for i in range(select.shape[1]):
            logical = select[block, i]
            local = table[logical] - low
            mine = (local >= 0) & (local < pages_dev)
            own = logical == stand
            slot = jnp.where(own, 0, jnp.maximum(picked - 1 - others, 0))
            slot = jnp.where(mine, slot, picked)
            rows[lb, slot] = local
            rows[blocks + lb, slot] = logical
            one = mine.astype(jnp.int32)
            others = others + jnp.where(own, 0, one)
            count = count + one
        info[lb, 0] = count
        info[lb, 1] = rows[blocks + lb, 0]

    for load in whole:
        load.wait()
    for lb in range(blocks):

        @pl.when(info[lb, 0] > 0)
        def _(lb=lb):
            for g in range(heads):
                v_out[lb, g, :, LANES:] = jnp.ones((picked * page, LANES), BF16)
            for slot in range(picked):
                local = jnp.clip(rows[lb, slot], 0, pages_dev - 1)
                both = jnp.concatenate([k_buf[local], v_buf[local]], axis=1)
                split = jnp.dot(apart, both, preferred_element_type=F32).astype(BF16)
                for g in range(heads):
                    here = slice(slot * page, (slot + 1) * page)
                    k_out[lb, g, here, :] = split[g * page : (g + 1) * page, :LANES]
                    v_out[lb, g, here, :LANES] = split[g * page : (g + 1) * page, LANES:]


def fetch(plan, select, table, stands, keys, values):
    pages_dev, page, heads, size = keys.shape
    blocks, picked = select.shape[0], PICKED_PAGES
    span = page * heads
    return pl.pallas_call(
        functools.partial(fetch_kernel, plan, pages_dev),
        out_shape=(
            jax.ShapeDtypeStruct((blocks, heads, picked * page, size), BF16),
            jax.ShapeDtypeStruct((blocks, heads, picked * page, size + LANES), BF16),
            jax.ShapeDtypeStruct((blocks, 3), jnp.int32),
        ),
        in_specs=[pl.BlockSpec(memory_space=pltpu.HBM)] * 5,
        out_specs=(in_vmem(), in_vmem(), in_smem()),
        scratch_shapes=[
            SMEM(select.shape, jnp.int32),
            SMEM(table.shape, jnp.int32),
            SMEM(stands.shape, jnp.int32),
            SMEM((2 * blocks, picked + 1), jnp.int32),
            VMEM((pages_dev, span, size), BF16),
            VMEM((pages_dev, span, size), BF16),
            pltpu.SemaphoreType.DMA((2,)),
            pltpu.SemaphoreType.DMA((3,)),
        ],
        compiler_params=params(16),
        cost_estimate=pl.CostEstimate(flops=2 * 10**9, bytes_accessed=8 * 2**20, transcendentals=0),
    )(*(pltpu.with_memory_space_constraint(x, pltpu.HBM) for x in (select, table, stands, keys.reshape(pages_dev, span, size), values.reshape(pages_dev, span, size))))


def pack_stats(lse, heads):
    lane = lax.broadcasted_iota(jnp.int32, lse.shape, 1)
    high = lse.astype(BF16).astype(F32)
    rest = lse - high
    middle = rest.astype(BF16).astype(F32)
    low = rest - middle
    packed = jnp.where(lane < heads, high, 0.0)
    packed = packed + jnp.where((lane >= heads) & (lane < 2 * heads), pltpu.roll(middle, heads, 1), 0.0)
    packed = packed + jnp.where((lane >= 2 * heads) & (lane < 3 * heads), pltpu.roll(low, 2 * heads, 1), 0.0)
    return packed.astype(BF16)


def unpack_stats(packed, heads):
    wide = packed.astype(F32)
    return wide + pltpu.roll(wide, LANES - heads, 1) + pltpu.roll(wide, LANES - 2 * heads, 1)


def attend_kernel(plan, heads, lb, info, *refs):
    me = lax.axis_index("pages")
    chunks, page = plan.chunks, plan.page
    queries, (k_ref, v_ref), outs = refs[:chunks], refs[chunks : chunks + 2], refs[chunks + 2 :]
    kv_heads, size = k_ref.shape[1], k_ref.shape[3]
    repeat = heads // kv_heads
    width = heads * size
    part = page // chunks
    tile = math.gcd(repeat, HEADS_PER_TILE)
    scale = size**-0.5 * math.log2(math.e)
    lane = lax.broadcasted_iota(jnp.int32, (page, LANES), 1)

    @pl.when(info[lb, 0] > 0)
    def _():
        shape = (tile * page, page)
        key_pos = info[lb, 1] * page + lax.broadcasted_iota(jnp.int32, shape, 1)
        query_pos = info[lb, 2] * page + plan.offsets(me, lb, shape)
        allowed = key_pos <= query_pos
        stats = jnp.zeros((page, LANES), F32)
        def product(first):
            q = jnp.concatenate(
                [m[:, h * size : (h + 1) * size] for h in range(first, first + tile) for m in queries], axis=0
            )
            return lax.dot_general(q, k_ref[lb, first // repeat], (((1,), (1,)), ((), ())), preferred_element_type=F32)

        ahead = product(0)
        for first in range(0, heads, tile):
            scores = scale * ahead
            if first + tile < heads:
                ahead = product(first + tile)
            scores = jnp.concatenate([jnp.where(allowed, scores[:, :page], FLOOR), scores[:, page:]], axis=1)
            peak = jnp.max(scores, axis=1, keepdims=True)
            weights = jnp.exp2(scores - peak).astype(BF16)
            both = jnp.dot(weights, v_ref[lb, first // repeat], preferred_element_type=F32)
            total = both[:, size:]
            out = (both[:, :size] / total).astype(BF16)
            lse = peak + jnp.log2(total)
            for i in range(tile):
                h = first + i
                stats = jnp.where(lane == h, lse[i * page : (i + 1) * page], stats)
                for c in range(chunks):
                    outs[c][:, h * size : (h + 1) * size] = out[i * page + c * part : i * page + (c + 1) * part]
        packed = pack_stats(stats, heads)
        for c in range(chunks):
            outs[c][:, width:] = packed[c * part : (c + 1) * part]

    @pl.when(info[lb, 0] == 0)
    def _():
        for c in range(chunks):
            outs[c][:, :width] = jnp.zeros((part, width), BF16)
            outs[c][:, width:] = pack_stats(jnp.full((part, LANES), FLOOR, F32), heads)


def attend(plan, heads, lb, pages, queries):
    keys, values, info = pages
    part = plan.page // plan.chunks
    shape = jax.ShapeDtypeStruct((part, queries[0].shape[1] + LANES), BF16)
    return pl.pallas_call(
        functools.partial(attend_kernel, plan, heads, lb),
        out_shape=(shape,) * plan.chunks,
        in_specs=[in_smem()] + [in_vmem()] * (len(queries) + 2),
        out_specs=(in_vmem(),) * plan.chunks,
        compiler_params=params(32),
        cost_estimate=pl.CostEstimate(flops=2 * 10**9, bytes_accessed=4 * 2**20, transcendentals=10**6),
    )(info, *queries, keys, values)


def merged(parts, stats):
    top = functools.reduce(jnp.maximum, stats)
    shares = [jnp.exp2(s - top) for s in stats]
    total = functools.reduce(jnp.add, shares)
    shares = [s / total for s in shares]

    def head(h):
        return functools.reduce(
            jnp.add, [p(h).astype(F32) * s[:, h : h + 1] for p, s in zip(parts, shares, strict=True)]
        )

    return head, top + jnp.log2(total)


def merge_kernel(heads, *refs):
    sources, out = refs[:-1], refs[-1]
    width = out.shape[1] - LANES
    size = width // heads
    head, lse = merged([heads_of(r, size) for r in sources], [unpack_stats(r[:, width:], heads) for r in sources])
    for h in range(heads):
        out[:, h * size : (h + 1) * size] = head(h).astype(BF16)
    out[:, width:] = pack_stats(lse, heads)


def merge(heads, *sources):
    return pl.pallas_call(
        functools.partial(merge_kernel, heads),
        out_shape=jax.ShapeDtypeStruct(sources[0].shape, BF16),
        in_specs=[in_vmem()] * len(sources),
        out_specs=in_vmem(),
        compiler_params=params(8),
    )(*sources)


def heads_of(ref, size):
    return lambda h: ref[:, h * size : (h + 1) * size]


def finish_kernel(heads, near, far, out):
    width = out.shape[1]
    size = width // heads
    head, _ = merged([heads_of(r, size) for r in (near, far)], [unpack_stats(r[:, width:], heads) for r in (near, far)])
    for h in range(heads):
        out[:, h * size : (h + 1) * size] = head(h).astype(BF16)


def finish(heads, near, far):
    return pl.pallas_call(
        functools.partial(finish_kernel, heads),
        out_shape=jax.ShapeDtypeStruct((near.shape[0], near.shape[1] - LANES), BF16),
        in_specs=[in_vmem()] * 2,
        out_specs=in_vmem(),
        compiler_params=params(8),
    )(near, far)


def sources_of(plan, lb):
    return range(plan.group) if lb else reversed(range(plan.group))


def project_kernel(plan, lb, *refs):
    sources, weight, (keep, send, rows_ref) = refs[: plan.group], refs[plan.group], refs[plan.group + 1 :]
    me, column = lax.axis_index("pages"), lax.axis_index("mp")
    rows = plan.rows
    holders = plan.group // 2
    for i, k in enumerate(sources_of(plan, lb)):
        device = me ^ k ^ (lb * plan.cross)
        place = ((device // holders % 2) ^ (column % 2)) * holders + device % holders
        rows_ref[pl.ds(pl.multiple_of(place * rows, rows), rows), :] = sources[i][...]
    product = jnp.dot(rows_ref[...], weight[...], preferred_element_type=F32)
    part = holders * rows
    keep[...] = product[:part]
    send[...] = product[part:].astype(BF16)


def project(plan, lb, sources, weight):
    columns = weight.shape[1]
    part = plan.page // 2
    return pl.pallas_call(
        functools.partial(project_kernel, plan, lb),
        out_shape=(jax.ShapeDtypeStruct((part, columns), F32), jax.ShapeDtypeStruct((part, columns), BF16)),
        in_specs=[in_vmem()] * (plan.group + 1),
        out_specs=(in_vmem(), in_vmem()),
        scratch_shapes=[VMEM((plan.page, weight.shape[0]), BF16)],
        compiler_params=params(24),
    )(*(sources[k] for k in sources_of(plan, lb)), weight)


def swap(x, axis, distance):
    n = lax.axis_size(axis)
    return lax.ppermute(x, axis, [(i, i ^ distance) for i in range(n)])


def others(plan):
    return range(1, plan.group)


def spread(x, plan):
    return {0: x} | {k: swap(x, "pages", k) for k in others(plan)}


def by_halves(plan, heads, queries, weight, pages):
    far = swap(queries, "pages", plan.cross)
    near = []
    for lb, rows in enumerate((queries, far)):
        chunks = spread(rows, plan)
        outs = attend(plan, heads, lb, pages, [chunks[k] for k in range(plan.group)])
        near.append(merge(heads, *(swap(outs[k], "pages", k) for k in reversed(others(plan))), outs[0]))
    across = [swap(x, "pages", plan.cross) for x in near]
    sums = [None, None]
    for lb in (1, 0):
        rows = finish(heads, near[lb], across[1 - lb])
        keep, send = project(plan, lb, spread(rows, plan), weight)
        sums[lb] = keep + swap(send, "mp", 1).astype(F32)
    stays = plan.block(lax.axis_index("pages"), 0) == lax.axis_index("mp") // 2
    mine = jnp.where(stays, sums[0], sums[1])
    away = jnp.where(stays, sums[1], sums[0]).astype(BF16)
    return (mine + swap(away, "mp", 2).astype(F32)).astype(BF16)


def by_gathers(plan, heads, queries, weight, pages):
    width = queries.shape[1]
    size = width // heads
    gathered = lax.all_gather(queries, "pages", axis=0, tiled=True)
    rows = gathered.shape[0]
    outs = [
        attend(plan, heads, lb, pages, [gathered[lb * plan.page : (lb + 1) * plan.page]])[0]
        for lb in range(plan.blocks)
    ]
    out = jnp.concatenate(outs, axis=0)
    packed = out[:, width : width + 3 * heads].astype(F32)
    lse = packed[:, :heads] + packed[:, heads : 2 * heads] + packed[:, 2 * heads :]
    every = lax.all_gather(lse, "pages")
    top = jnp.max(every, axis=0)
    share = jnp.exp2(lse - top) / jnp.sum(jnp.exp2(every - top), axis=0)
    part = (out[:, :width].reshape(rows, heads, size).astype(F32) * share[..., None]).reshape(1, rows, width)
    received = lax.all_to_all(part.astype(BF16), "pages", split_axis=1, concat_axis=0, tiled=True)
    mixed = jnp.sum(received, axis=0, dtype=F32).astype(BF16)
    terms = jnp.dot(lax.all_gather(mixed, "pages", axis=0, tiled=True), weight, preferred_element_type=F32)
    return lax.psum_scatter(terms, "mp", scatter_dimension=0, tiled=True).astype(BF16)


def per_device(queries, cached_keys, cached_values, out_weight, select, page_table, block_page):
    n, ways = lax.axis_size("pages"), lax.axis_size("mp")
    plan = Plan(n, ways, queries.shape[0], select.shape[0], cached_keys.shape[1])
    heads = queries.shape[1] // cached_keys.shape[3]
    pages = fetch(plan, select, page_table, block_page, cached_keys, cached_values)
    way = by_halves if plan.halves else by_gathers
    return way(plan, heads, queries, out_weight, pages)


def solution(mesh):
    placed = (
        P("pages", "mp"),
        P("pages", None, "mp", None),
        P("pages", None, "mp", None),
        P("mp", "pages"),
        P(),
        P(),
        P(),
    )
    return jax.shard_map(
        per_device, mesh=mesh, in_specs=placed, out_specs=P("mp", "pages"), check_vma=False
    )
```

```python
import functools
import math

import jax
import jax.numpy as jnp
from jax import lax
from jax.experimental import pallas as pl
from jax.experimental.pallas import tpu as pltpu
from jax.sharding import PartitionSpec as P

PICKED_PAGES = 6
FLOOR = -1e30
LANES = 128
HEADS_PER_TILE = 2

VMEM = pltpu.VMEM
SMEM = pltpu.SMEM
BF16 = jnp.bfloat16
F32 = jnp.float32


def in_vmem():
    return pl.BlockSpec(memory_space=VMEM)


def in_smem():
    return pl.BlockSpec(memory_space=SMEM)


def params(mib):
    return pltpu.CompilerParams(vmem_limit_bytes=mib * 2**20)


class Plan:
    def __init__(self, n, ways, rows, blocks, page):
        self.n, self.ways, self.rows, self.blocks, self.page = n, ways, rows, blocks, page
        self.group = n // blocks
        self.halves = blocks == 2 and n == 8 and ways == 4 and rows * self.group == page
        self.cross = n * 3 // 4
        self.chunks = self.group if self.halves else 1

    def block(self, me, lb):
        return (me // self.group) ^ lb if self.halves else lb

    def offsets(self, me, lb, shape):
        row = lax.broadcasted_iota(jnp.int32, shape, 0) % self.page
        if not self.halves:
            return row
        mine = (me ^ (lb * self.cross)) % self.group
        return ((row // self.rows) ^ mine) * self.rows + row % self.rows


def fetch_kernel(plan, pages_dev, select_hbm, table_hbm, stands_hbm, keys, values, k_out, v_out, info, select, table, stands, rows, k_buf, v_buf, sems, int_sems):
    me = lax.axis_index("pages")
    blocks, picked = k_buf.shape[:2]
    span = k_buf.shape[2]
    heads = k_out.shape[1]
    page = span // heads
    low = me * pages_dev
    loads = [
        pltpu.make_async_copy(a, b, int_sems.at[i])
        for i, (a, b) in enumerate(((select_hbm, select), (table_hbm, table), (stands_hbm, stands)))
    ]
    for load in loads:
        load.start()
    row = lax.broadcasted_iota(jnp.int32, (span, span), 0)
    column = lax.broadcasted_iota(jnp.int32, (span, span), 1)
    apart = (column == (row % page) * heads + row // page).astype(F32).astype(BF16)
    for load in loads:
        load.wait()
    for lb in range(blocks):
        block = plan.block(me, lb)
        stand = stands[block]
        info[lb, 1] = plan.n * pages_dev
        info[lb, 2] = stand
        others = jnp.int32(0)
        count = jnp.int32(0)
        for i in range(select.shape[1]):
            logical = select[block, i]
            local = table[logical] - low
            mine = (local >= 0) & (local < pages_dev)
            own = logical == stand
            slot = jnp.where(own, 0, jnp.maximum(picked - 1 - others, 0))
            slot = jnp.where(mine, slot, picked)
            rows[lb, slot] = local
            rows[blocks + lb, slot] = logical
            one = mine.astype(jnp.int32)
            others = others + jnp.where(own, 0, one)
            count = count + one
        info[lb, 0] = count
        info[lb, 1] = rows[blocks + lb, 0]

        @pl.when(count > 0)
        def _(lb=lb):
            for slot in range(picked):
                local = jnp.clip(rows[lb, slot], 0, pages_dev - 1)
                pltpu.make_async_copy(keys.at[local], k_buf.at[lb, slot], sems.at[lb, slot, 0]).start()
                pltpu.make_async_copy(values.at[local], v_buf.at[lb, slot], sems.at[lb, slot, 1]).start()

    for lb in range(blocks):

        @pl.when(info[lb, 0] > 0)
        def _(lb=lb):
            for g in range(heads):
                v_out[lb, g, :, LANES:] = jnp.ones((picked * page, LANES), BF16)
            for slot in range(picked):
                pltpu.make_async_copy(keys.at[0], k_buf.at[lb, slot], sems.at[lb, slot, 0]).wait()
                pltpu.make_async_copy(values.at[0], v_buf.at[lb, slot], sems.at[lb, slot, 1]).wait()
            for slot in range(picked):
                both = jnp.concatenate([k_buf[lb, slot], v_buf[lb, slot]], axis=1)
                split = jnp.dot(apart, both, preferred_element_type=F32).astype(BF16)
                for g in range(heads):
                    here = slice(slot * page, (slot + 1) * page)
                    k_out[lb, g, here, :] = split[g * page : (g + 1) * page, :LANES]
                    v_out[lb, g, here, :LANES] = split[g * page : (g + 1) * page, LANES:]


def fetch(plan, select, table, stands, keys, values):
    pages_dev, page, heads, size = keys.shape
    blocks, picked = select.shape[0], PICKED_PAGES
    span = page * heads
    return pl.pallas_call(
        functools.partial(fetch_kernel, plan, pages_dev),
        out_shape=(
            jax.ShapeDtypeStruct((blocks, heads, picked * page, size), BF16),
            jax.ShapeDtypeStruct((blocks, heads, picked * page, size + LANES), BF16),
            jax.ShapeDtypeStruct((blocks, 3), jnp.int32),
        ),
        in_specs=[pl.BlockSpec(memory_space=pltpu.HBM)] * 5,
        out_specs=(in_vmem(), in_vmem(), in_smem()),
        scratch_shapes=[
            SMEM(select.shape, jnp.int32),
            SMEM(table.shape, jnp.int32),
            SMEM(stands.shape, jnp.int32),
            SMEM((2 * blocks, picked + 1), jnp.int32),
            VMEM((blocks, picked, span, size), BF16),
            VMEM((blocks, picked, span, size), BF16),
            pltpu.SemaphoreType.DMA((blocks, picked, 2)),
            pltpu.SemaphoreType.DMA((3,)),
        ],
        compiler_params=params(16),
        cost_estimate=pl.CostEstimate(flops=2 * 10**9, bytes_accessed=8 * 2**20, transcendentals=0),
    )(*(pltpu.with_memory_space_constraint(x, pltpu.HBM) for x in (select, table, stands, keys.reshape(pages_dev, span, size), values.reshape(pages_dev, span, size))))


def pack_stats(lse, heads):
    lane = lax.broadcasted_iota(jnp.int32, lse.shape, 1)
    high = lse.astype(BF16).astype(F32)
    rest = lse - high
    middle = rest.astype(BF16).astype(F32)
    low = rest - middle
    packed = jnp.where(lane < heads, high, 0.0)
    packed = packed + jnp.where((lane >= heads) & (lane < 2 * heads), pltpu.roll(middle, heads, 1), 0.0)
    packed = packed + jnp.where((lane >= 2 * heads) & (lane < 3 * heads), pltpu.roll(low, 2 * heads, 1), 0.0)
    return packed.astype(BF16)


def unpack_stats(packed, heads):
    wide = packed.astype(F32)
    return wide + pltpu.roll(wide, LANES - heads, 1) + pltpu.roll(wide, LANES - 2 * heads, 1)


def attend_kernel(plan, heads, lb, info, *refs):
    me = lax.axis_index("pages")
    chunks, page = plan.chunks, plan.page
    queries, (k_ref, v_ref), outs = refs[:chunks], refs[chunks : chunks + 2], refs[chunks + 2 :]
    kv_heads, size = k_ref.shape[1], k_ref.shape[3]
    repeat = heads // kv_heads
    width = heads * size
    part = page // chunks
    tile = math.gcd(repeat, HEADS_PER_TILE)
    scale = size**-0.5 * math.log2(math.e)
    lane = lax.broadcasted_iota(jnp.int32, (page, LANES), 1)

    @pl.when(info[lb, 0] > 0)
    def _():
        shape = (tile * page, page)
        key_pos = info[lb, 1] * page + lax.broadcasted_iota(jnp.int32, shape, 1)
        query_pos = info[lb, 2] * page + plan.offsets(me, lb, shape)
        allowed = key_pos <= query_pos
        stats = jnp.zeros((page, LANES), F32)
        def product(first):
            q = jnp.concatenate(
                [m[:, h * size : (h + 1) * size] for h in range(first, first + tile) for m in queries], axis=0
            )
            return lax.dot_general(q, k_ref[lb, first // repeat], (((1,), (1,)), ((), ())), preferred_element_type=F32)

        ahead = product(0)
        for first in range(0, heads, tile):
            scores = scale * ahead
            if first + tile < heads:
                ahead = product(first + tile)
            scores = jnp.concatenate([jnp.where(allowed, scores[:, :page], FLOOR), scores[:, page:]], axis=1)
            peak = jnp.max(scores, axis=1, keepdims=True)
            weights = jnp.exp2(scores - peak).astype(BF16)
            both = jnp.dot(weights, v_ref[lb, first // repeat], preferred_element_type=F32)
            total = both[:, size:]
            out = (both[:, :size] / total).astype(BF16)
            lse = peak + jnp.log2(total)
            for i in range(tile):
                h = first + i
                stats = jnp.where(lane == h, lse[i * page : (i + 1) * page], stats)
                for c in range(chunks):
                    outs[c][:, h * size : (h + 1) * size] = out[i * page + c * part : i * page + (c + 1) * part]
        packed = pack_stats(stats, heads)
        for c in range(chunks):
            outs[c][:, width:] = packed[c * part : (c + 1) * part]

    @pl.when(info[lb, 0] == 0)
    def _():
        for c in range(chunks):
            outs[c][:, :width] = jnp.zeros((part, width), BF16)
            outs[c][:, width:] = pack_stats(jnp.full((part, LANES), FLOOR, F32), heads)


def attend(plan, heads, lb, pages, queries):
    keys, values, info = pages
    part = plan.page // plan.chunks
    shape = jax.ShapeDtypeStruct((part, queries[0].shape[1] + LANES), BF16)
    return pl.pallas_call(
        functools.partial(attend_kernel, plan, heads, lb),
        out_shape=(shape,) * plan.chunks,
        in_specs=[in_smem()] + [in_vmem()] * (len(queries) + 2),
        out_specs=(in_vmem(),) * plan.chunks,
        compiler_params=params(32),
        cost_estimate=pl.CostEstimate(flops=2 * 10**9, bytes_accessed=4 * 2**20, transcendentals=10**6),
    )(info, *queries, keys, values)


def merged(parts, stats):
    top = functools.reduce(jnp.maximum, stats)
    shares = [jnp.exp2(s - top) for s in stats]
    total = functools.reduce(jnp.add, shares)
    shares = [s / total for s in shares]

    def head(h):
        return functools.reduce(
            jnp.add, [p(h).astype(F32) * s[:, h : h + 1] for p, s in zip(parts, shares, strict=True)]
        )

    return head, top + jnp.log2(total)


def merge_kernel(heads, *refs):
    sources, out = refs[:-1], refs[-1]
    width = out.shape[1] - LANES
    size = width // heads
    head, lse = merged([heads_of(r, size) for r in sources], [unpack_stats(r[:, width:], heads) for r in sources])
    for h in range(heads):
        out[:, h * size : (h + 1) * size] = head(h).astype(BF16)
    out[:, width:] = pack_stats(lse, heads)


def merge(heads, *sources):
    return pl.pallas_call(
        functools.partial(merge_kernel, heads),
        out_shape=jax.ShapeDtypeStruct(sources[0].shape, BF16),
        in_specs=[in_vmem()] * len(sources),
        out_specs=in_vmem(),
        compiler_params=params(8),
    )(*sources)


def heads_of(ref, size):
    return lambda h: ref[:, h * size : (h + 1) * size]


def finish_kernel(heads, near, far, out):
    width = out.shape[1]
    size = width // heads
    head, _ = merged([heads_of(r, size) for r in (near, far)], [unpack_stats(r[:, width:], heads) for r in (near, far)])
    for h in range(heads):
        out[:, h * size : (h + 1) * size] = head(h).astype(BF16)


def finish(heads, near, far):
    return pl.pallas_call(
        functools.partial(finish_kernel, heads),
        out_shape=jax.ShapeDtypeStruct((near.shape[0], near.shape[1] - LANES), BF16),
        in_specs=[in_vmem()] * 2,
        out_specs=in_vmem(),
        compiler_params=params(8),
    )(near, far)


def project_kernel(plan, lb, *refs):
    sources, (weight, keep, send, rows_ref) = refs[:-4], refs[-4:]
    me, column = lax.axis_index("pages"), lax.axis_index("mp")
    rows = plan.rows
    holders = plan.group // 2
    for k, source in enumerate(sources):
        device = me ^ k ^ (lb * plan.cross)
        place = ((device // holders % 2) ^ (column % 2)) * holders + device % holders
        rows_ref[pl.ds(pl.multiple_of(place * rows, rows), rows), :] = source[...]
    product = jnp.dot(rows_ref[...], weight[...], preferred_element_type=F32)
    part = holders * rows
    keep[...] = product[:part]
    send[...] = product[part:].astype(BF16)


def project_pair_kernel(plan, *refs):
    sources, (weight, keep, send, rows_ref) = refs[:-4], refs[-4:]
    me = lax.axis_index("pages")
    rows = plan.rows
    for k, source in enumerate(sources):
        rows_ref[pl.ds(pl.multiple_of((me ^ k) % 2 * rows, rows), rows), :] = source[...]
    product = jnp.dot(rows_ref[...], weight[...], preferred_element_type=F32)
    keep[...] = product
    send[...] = product.astype(BF16)


def project(plan, kernel, sources, weight):
    columns = weight.shape[1]
    part = plan.page // 2
    return pl.pallas_call(
        kernel,
        out_shape=(jax.ShapeDtypeStruct((part, columns), F32), jax.ShapeDtypeStruct((part, columns), BF16)),
        in_specs=[in_vmem()] * (len(sources) + 1),
        out_specs=(in_vmem(), in_vmem()),
        scratch_shapes=[VMEM((len(sources) * plan.rows, weight.shape[0]), BF16)],
        compiler_params=params(24),
    )(*sources, weight)


def swap(x, axis, distance):
    n = lax.axis_size(axis)
    return lax.ppermute(x, axis, [(i, i ^ distance) for i in range(n)])


def others(plan):
    return range(1, plan.group)


def swap_y(plan, x, late):
    pairs = [
        (p * plan.ways + m, p * plan.ways + (m ^ 2))
        for p in range(plan.n)
        for m in range(plan.ways)
        if (p // 2 + m) % 2 == late
    ]
    return lax.ppermute(x, ("pages", "mp"), pairs)


def spread(x, plan):
    return {0: x} | {k: swap(x, "pages", k) for k in others(plan)}


def by_halves(plan, heads, queries, weight, pages):
    far = swap(queries, "pages", plan.cross)
    near = []
    for lb, rows in enumerate((queries, far)):
        chunks = spread(rows, plan)
        outs = attend(plan, heads, lb, pages, [chunks[k] for k in range(plan.group)])
        near.append(merge(heads, outs[0], *(swap(outs[k], "pages", k) for k in others(plan))))
    across = [swap(x, "pages", plan.cross) for x in near]
    far_rows = spread(finish(heads, near[1], across[0]), plan)
    rows = spread(finish(heads, near[0], across[1]), plan)
    keep, send = project(plan, functools.partial(project_kernel, plan, 1), [far_rows[k] for k in range(plan.group)], weight)
    far_sum = keep + swap(send, "mp", 1).astype(F32)
    me, column = lax.axis_index("pages"), lax.axis_index("mp")
    stays = plan.block(me, 0) == column // 2
    halves, arrived, aways = [], [], []
    for late in range(2):
        pair = [rows[2 * late], rows[2 * late + 1]]
        keep, send = project(plan, functools.partial(project_pair_kernel, plan), pair, weight)
        if late:
            send, aways[0] = lax.optimization_barrier((send, aways[0]))
        halves.append(keep + swap(send, "mp", 1).astype(F32))
        away = jnp.where(stays, far_sum, halves[late]).astype(BF16)
        aways.append(away)
    arrived = [swap_y(plan, away, late) for late, away in enumerate(aways)]
    here = (me // 2 + column) % 2 == 0
    mine = jnp.where(stays, jnp.where(here, halves[0], halves[1]), far_sum)
    return (mine + arrived[0].astype(F32) + arrived[1].astype(F32)).astype(BF16)


def by_gathers(plan, heads, queries, weight, pages):
    width = queries.shape[1]
    size = width // heads
    gathered = lax.all_gather(queries, "pages", axis=0, tiled=True)
    rows = gathered.shape[0]
    outs = [
        attend(plan, heads, lb, pages, [gathered[lb * plan.page : (lb + 1) * plan.page]])[0]
        for lb in range(plan.blocks)
    ]
    out = jnp.concatenate(outs, axis=0)
    packed = out[:, width : width + 3 * heads].astype(F32)
    lse = packed[:, :heads] + packed[:, heads : 2 * heads] + packed[:, 2 * heads :]
    every = lax.all_gather(lse, "pages")
    top = jnp.max(every, axis=0)
    share = jnp.exp2(lse - top) / jnp.sum(jnp.exp2(every - top), axis=0)
    part = (out[:, :width].reshape(rows, heads, size).astype(F32) * share[..., None]).reshape(1, rows, width)
    received = lax.all_to_all(part.astype(BF16), "pages", split_axis=1, concat_axis=0, tiled=True)
    mixed = jnp.sum(received, axis=0, dtype=F32).astype(BF16)
    terms = jnp.dot(lax.all_gather(mixed, "pages", axis=0, tiled=True), weight, preferred_element_type=F32)
    return lax.psum_scatter(terms, "mp", scatter_dimension=0, tiled=True).astype(BF16)


def per_device(queries, cached_keys, cached_values, out_weight, select, page_table, block_page):
    n, ways = lax.axis_size("pages"), lax.axis_size("mp")
    plan = Plan(n, ways, queries.shape[0], select.shape[0], cached_keys.shape[1])
    heads = queries.shape[1] // cached_keys.shape[3]
    pages = fetch(plan, select, page_table, block_page, cached_keys, cached_values)
    way = by_halves if plan.halves else by_gathers
    return way(plan, heads, queries, out_weight, pages)


def solution(mesh):
    placed = (
        P("pages", "mp"),
        P("pages", None, "mp", None),
        P("pages", None, "mp", None),
        P("mp", "pages"),
        P(),
        P(),
        P(),
    )
    return jax.shard_map(
        per_device, mesh=mesh, in_specs=placed, out_specs=P("mp", "pages"), check_vma=False
    )
```

```python
import functools
import math

import jax
import jax.numpy as jnp
from jax import lax
from jax.experimental import pallas as pl
from jax.experimental.pallas import tpu as pltpu
from jax.sharding import PartitionSpec as P

PICKED_PAGES = 6
FLOOR = -1e30
LANES = 128
HEADS_PER_TILE = 2

VMEM = pltpu.VMEM
SMEM = pltpu.SMEM
BF16 = jnp.bfloat16
F32 = jnp.float32


def in_vmem():
    return pl.BlockSpec(memory_space=VMEM)


def in_smem():
    return pl.BlockSpec(memory_space=SMEM)


def params(mib):
    return pltpu.CompilerParams(vmem_limit_bytes=mib * 2**20)


class Plan:
    def __init__(self, n, ways, rows, blocks, page):
        self.n, self.rows, self.blocks, self.page = n, rows, blocks, page
        self.group = n // blocks
        self.halves = blocks == 2 and n == 8 and ways == 4 and rows * self.group == page
        self.cross = n // 2
        self.chunks = self.group if self.halves else 1

    def block(self, me, lb):
        return (me // self.group) ^ lb if self.halves else lb

    def offsets(self, me, lb, shape):
        row = lax.broadcasted_iota(jnp.int32, shape, 0) % self.page
        if not self.halves:
            return row
        mine = (me ^ (lb * self.cross)) % self.group
        return ((row // self.rows) ^ mine) * self.rows + row % self.rows


def fetch_kernel(plan, pages_dev, select_hbm, table_hbm, stands_hbm, keys, values, k_out, v_out, info, select, table, stands, rows, k_buf, v_buf, sems, int_sems):
    me = lax.axis_index("pages")
    blocks, heads = k_out.shape[:2]
    span = k_buf.shape[1]
    page = span // heads
    picked = k_out.shape[2] // page
    low = me * pages_dev
    loads = [
        pltpu.make_async_copy(a, b, int_sems.at[i])
        for i, (a, b) in enumerate(((select_hbm, select), (table_hbm, table), (stands_hbm, stands)))
    ]
    whole = [
        pltpu.make_async_copy(a, b, sems.at[i]) for i, (a, b) in enumerate(((keys, k_buf), (values, v_buf)))
    ]
    for load in loads + whole:
        load.start()
    row = lax.broadcasted_iota(jnp.int32, (span, span), 0)
    column = lax.broadcasted_iota(jnp.int32, (span, span), 1)
    apart = (column == (row % page) * heads + row // page).astype(F32).astype(BF16)
    for load in loads:
        load.wait()
    for lb in range(blocks):
        block = plan.block(me, lb)
        stand = stands[block]
        info[lb, 1] = plan.n * pages_dev
        info[lb, 2] = stand
        others = jnp.int32(0)
        count = jnp.int32(0)
        for i in range(select.shape[1]):
            logical = select[block, i]
            local = table[logical] - low
            mine = (local >= 0) & (local < pages_dev)
            own = logical == stand
            slot = jnp.where(own, 0, jnp.maximum(picked - 1 - others, 0))
            slot = jnp.where(mine, slot, picked)
            rows[lb, slot] = local
            rows[blocks + lb, slot] = logical
            one = mine.astype(jnp.int32)
            others = others + jnp.where(own, 0, one)
            count = count + one
        info[lb, 0] = count
        info[lb, 1] = rows[blocks + lb, 0]

    for load in whole:
        load.wait()
    for lb in range(blocks):

        @pl.when(info[lb, 0] > 0)
        def _(lb=lb):
            for g in range(heads):
                v_out[lb, g, :, LANES:] = jnp.ones((picked * page, LANES), BF16)
            for slot in range(picked):
                local = jnp.clip(rows[lb, slot], 0, pages_dev - 1)
                both = jnp.concatenate([k_buf[local], v_buf[local]], axis=1)
                split = jnp.dot(apart, both, preferred_element_type=F32).astype(BF16)
                for g in range(heads):
                    here = slice(slot * page, (slot + 1) * page)
                    k_out[lb, g, here, :] = split[g * page : (g + 1) * page, :LANES]
                    v_out[lb, g, here, :LANES] = split[g * page : (g + 1) * page, LANES:]


def fetch(plan, select, table, stands, keys, values):
    pages_dev, page, heads, size = keys.shape
    blocks, picked = select.shape[0], PICKED_PAGES
    span = page * heads
    return pl.pallas_call(
        functools.partial(fetch_kernel, plan, pages_dev),
        out_shape=(
            jax.ShapeDtypeStruct((blocks, heads, picked * page, size), BF16),
            jax.ShapeDtypeStruct((blocks, heads, picked * page, size + LANES), BF16),
            jax.ShapeDtypeStruct((blocks, 3), jnp.int32),
        ),
        in_specs=[pl.BlockSpec(memory_space=pltpu.HBM)] * 5,
        out_specs=(in_vmem(), in_vmem(), in_smem()),
        scratch_shapes=[
            SMEM(select.shape, jnp.int32),
            SMEM(table.shape, jnp.int32),
            SMEM(stands.shape, jnp.int32),
            SMEM((2 * blocks, picked + 1), jnp.int32),
            VMEM((pages_dev, span, size), BF16),
            VMEM((pages_dev, span, size), BF16),
            pltpu.SemaphoreType.DMA((2,)),
            pltpu.SemaphoreType.DMA((3,)),
        ],
        compiler_params=params(16),
        cost_estimate=pl.CostEstimate(flops=2 * 10**9, bytes_accessed=8 * 2**20, transcendentals=0),
    )(*(pltpu.with_memory_space_constraint(x, pltpu.HBM) for x in (select, table, stands, keys.reshape(pages_dev, span, size), values.reshape(pages_dev, span, size))))


def pack_stats(lse, heads):
    lane = lax.broadcasted_iota(jnp.int32, lse.shape, 1)
    high = lse.astype(BF16).astype(F32)
    rest = lse - high
    middle = rest.astype(BF16).astype(F32)
    low = rest - middle
    packed = jnp.where(lane < heads, high, 0.0)
    packed = packed + jnp.where((lane >= heads) & (lane < 2 * heads), pltpu.roll(middle, heads, 1), 0.0)
    packed = packed + jnp.where((lane >= 2 * heads) & (lane < 3 * heads), pltpu.roll(low, 2 * heads, 1), 0.0)
    return packed.astype(BF16)


def unpack_stats(packed, heads):
    wide = packed.astype(F32)
    return wide + pltpu.roll(wide, LANES - heads, 1) + pltpu.roll(wide, LANES - 2 * heads, 1)


def attend_kernel(plan, heads, lb, info, *refs):
    me = lax.axis_index("pages")
    chunks, page = plan.chunks, plan.page
    queries, (k_ref, v_ref), outs = refs[:chunks], refs[chunks : chunks + 2], refs[chunks + 2 :]
    kv_heads, size = k_ref.shape[1], k_ref.shape[3]
    repeat = heads // kv_heads
    width = heads * size
    part = page // chunks
    tile = math.gcd(repeat, HEADS_PER_TILE)
    scale = size**-0.5 * math.log2(math.e)
    lane = lax.broadcasted_iota(jnp.int32, (page, LANES), 1)

    @pl.when(info[lb, 0] > 0)
    def _():
        shape = (tile * page, page)
        key_pos = info[lb, 1] * page + lax.broadcasted_iota(jnp.int32, shape, 1)
        query_pos = info[lb, 2] * page + plan.offsets(me, lb, shape)
        allowed = key_pos <= query_pos
        stats = jnp.zeros((page, LANES), F32)
        def product(first):
            q = jnp.concatenate(
                [m[:, h * size : (h + 1) * size] for h in range(first, first + tile) for m in queries], axis=0
            )
            return lax.dot_general(q, k_ref[lb, first // repeat], (((1,), (1,)), ((), ())), preferred_element_type=F32)

        ahead = product(0)
        for first in range(0, heads, tile):
            scores = scale * ahead
            if first + tile < heads:
                ahead = product(first + tile)
            scores = jnp.concatenate([jnp.where(allowed, scores[:, :page], FLOOR), scores[:, page:]], axis=1)
            peak = jnp.max(scores, axis=1, keepdims=True)
            weights = jnp.exp2(scores - peak).astype(BF16)
            both = jnp.dot(weights, v_ref[lb, first // repeat], preferred_element_type=F32)
            total = both[:, size:]
            out = (both[:, :size] / total).astype(BF16)
            lse = peak + jnp.log2(total)
            for i in range(tile):
                h = first + i
                stats = jnp.where(lane == h, lse[i * page : (i + 1) * page], stats)
                for c in range(chunks):
                    outs[c][:, h * size : (h + 1) * size] = out[i * page + c * part : i * page + (c + 1) * part]
        packed = pack_stats(stats, heads)
        for c in range(chunks):
            outs[c][:, width:] = packed[c * part : (c + 1) * part]

    @pl.when(info[lb, 0] == 0)
    def _():
        for c in range(chunks):
            outs[c][:, :width] = jnp.zeros((part, width), BF16)
            outs[c][:, width:] = pack_stats(jnp.full((part, LANES), FLOOR, F32), heads)


def attend(plan, heads, lb, pages, queries):
    keys, values, info = pages
    part = plan.page // plan.chunks
    shape = jax.ShapeDtypeStruct((part, queries[0].shape[1] + LANES), BF16)
    return pl.pallas_call(
        functools.partial(attend_kernel, plan, heads, lb),
        out_shape=(shape,) * plan.chunks,
        in_specs=[in_smem()] + [in_vmem()] * (len(queries) + 2),
        out_specs=(in_vmem(),) * plan.chunks,
        compiler_params=params(32),
        cost_estimate=pl.CostEstimate(flops=2 * 10**9, bytes_accessed=4 * 2**20, transcendentals=10**6),
    )(info, *queries, keys, values)


def merged(parts, stats):
    top = functools.reduce(jnp.maximum, stats)
    shares = [jnp.exp2(s - top) for s in stats]
    total = functools.reduce(jnp.add, shares)
    shares = [s / total for s in shares]

    def head(h):
        return functools.reduce(
            jnp.add, [p(h).astype(F32) * s[:, h : h + 1] for p, s in zip(parts, shares, strict=True)]
        )

    return head, top + jnp.log2(total)


def merge_kernel(heads, *refs):
    sources, out = refs[:-1], refs[-1]
    width = out.shape[1] - LANES
    size = width // heads
    head, lse = merged([heads_of(r, size) for r in sources], [unpack_stats(r[:, width:], heads) for r in sources])
    for h in range(heads):
        out[:, h * size : (h + 1) * size] = head(h).astype(BF16)
    out[:, width:] = pack_stats(lse, heads)


def merge(heads, *sources):
    return pl.pallas_call(
        functools.partial(merge_kernel, heads),
        out_shape=jax.ShapeDtypeStruct(sources[0].shape, BF16),
        in_specs=[in_vmem()] * len(sources),
        out_specs=in_vmem(),
        compiler_params=params(8),
    )(*sources)


def heads_of(ref, size):
    return lambda h: ref[:, h * size : (h + 1) * size]


def finish_kernel(heads, near, far, out):
    width = out.shape[1]
    size = width // heads
    head, _ = merged([heads_of(r, size) for r in (near, far)], [unpack_stats(r[:, width:], heads) for r in (near, far)])
    for h in range(heads):
        out[:, h * size : (h + 1) * size] = head(h).astype(BF16)


def finish(heads, near, far):
    return pl.pallas_call(
        functools.partial(finish_kernel, heads),
        out_shape=jax.ShapeDtypeStruct((near.shape[0], near.shape[1] - LANES), BF16),
        in_specs=[in_vmem()] * 2,
        out_specs=in_vmem(),
        compiler_params=params(8),
    )(near, far)


def project_kernel(plan, lb, *refs):
    sources, weight, (keep, send, rows_ref) = refs[: plan.group], refs[plan.group], refs[plan.group + 1 :]
    me, column = lax.axis_index("pages"), lax.axis_index("mp")
    rows = plan.rows
    holders = plan.group // 2
    for k in range(plan.group):
        device = me ^ k ^ (lb * plan.cross)
        place = ((device // holders % 2) ^ (column % 2)) * holders + device % holders
        rows_ref[pl.ds(pl.multiple_of(place * rows, rows), rows), :] = sources[k][...]
    product = jnp.dot(rows_ref[...], weight[...], preferred_element_type=F32)
    part = holders * rows
    keep[...] = product[:part]
    send[...] = product[part:].astype(BF16)


def project(plan, lb, sources, weight):
    columns = weight.shape[1]
    part = plan.page // 2
    return pl.pallas_call(
        functools.partial(project_kernel, plan, lb),
        out_shape=(jax.ShapeDtypeStruct((part, columns), F32), jax.ShapeDtypeStruct((part, columns), BF16)),
        in_specs=[in_vmem()] * (plan.group + 1),
        out_specs=(in_vmem(), in_vmem()),
        scratch_shapes=[VMEM((plan.page, weight.shape[0]), BF16)],
        compiler_params=params(24),
    )(*(sources[k] for k in range(plan.group)), weight)


def swap(x, axis, distance):
    n = lax.axis_size(axis)
    return lax.ppermute(x, axis, [(i, i ^ distance) for i in range(n)])


def others(plan):
    return range(1, plan.group)


def spread(x, plan):
    return {0: x} | {k: swap(x, "pages", k) for k in others(plan)}


def by_halves(plan, heads, queries, weight, pages):
    far = swap(queries, "pages", plan.cross)
    near = []
    for lb, rows in enumerate((queries, far)):
        chunks = spread(rows, plan)
        outs = attend(plan, heads, lb, pages, [chunks[k] for k in range(plan.group)])
        near.append(merge(heads, outs[0], *(swap(outs[k], "pages", k) for k in others(plan))))
    across = [swap(x, "pages", plan.cross) for x in near]
    sums = [None, None]
    for lb in (1, 0):
        rows = finish(heads, near[lb], across[1 - lb])
        keep, send = project(plan, lb, spread(rows, plan), weight)
        sums[lb] = keep + swap(send, "mp", 1).astype(F32)
    stays = plan.block(lax.axis_index("pages"), 0) == lax.axis_index("mp") // 2
    mine = jnp.where(stays, sums[0], sums[1])
    away = jnp.where(stays, sums[1], sums[0]).astype(BF16)
    return (mine + swap(away, "mp", 2).astype(F32)).astype(BF16)


def by_gathers(plan, heads, queries, weight, pages):
    width = queries.shape[1]
    size = width // heads
    gathered = lax.all_gather(queries, "pages", axis=0, tiled=True)
    rows = gathered.shape[0]
    outs = [
        attend(plan, heads, lb, pages, [gathered[lb * plan.page : (lb + 1) * plan.page]])[0]
        for lb in range(plan.blocks)
    ]
    out = jnp.concatenate(outs, axis=0)
    packed = out[:, width : width + 3 * heads].astype(F32)
    lse = packed[:, :heads] + packed[:, heads : 2 * heads] + packed[:, 2 * heads :]
    every = lax.all_gather(lse, "pages")
    top = jnp.max(every, axis=0)
    share = jnp.exp2(lse - top) / jnp.sum(jnp.exp2(every - top), axis=0)
    part = (out[:, :width].reshape(rows, heads, size).astype(F32) * share[..., None]).reshape(1, rows, width)
    received = lax.all_to_all(part.astype(BF16), "pages", split_axis=1, concat_axis=0, tiled=True)
    mixed = jnp.sum(received, axis=0, dtype=F32).astype(BF16)
    terms = jnp.dot(lax.all_gather(mixed, "pages", axis=0, tiled=True), weight, preferred_element_type=F32)
    return lax.psum_scatter(terms, "mp", scatter_dimension=0, tiled=True).astype(BF16)


def per_device(queries, cached_keys, cached_values, out_weight, select, page_table, block_page):
    n, ways = lax.axis_size("pages"), lax.axis_size("mp")
    plan = Plan(n, ways, queries.shape[0], select.shape[0], cached_keys.shape[1])
    heads = queries.shape[1] // cached_keys.shape[3]
    pages = fetch(plan, select, page_table, block_page, cached_keys, cached_values)
    way = by_halves if plan.halves else by_gathers
    return way(plan, heads, queries, out_weight, pages)


def solution(mesh):
    placed = (
        P("pages", "mp"),
        P("pages", None, "mp", None),
        P("pages", None, "mp", None),
        P("mp", "pages"),
        P(),
        P(),
        P(),
    )
    return jax.shard_map(
        per_device, mesh=mesh, in_specs=placed, out_specs=P("mp", "pages"), check_vma=False
    )
```

```python
import functools
import math

import jax
import jax.numpy as jnp
from jax import lax
from jax.experimental import pallas as pl
from jax.experimental.pallas import tpu as pltpu
from jax.sharding import PartitionSpec as P

PICKED_PAGES = 6
FLOOR = -1e30
LANES = 128
HEADS_PER_TILE = 2

VMEM = pltpu.VMEM
SMEM = pltpu.SMEM
BF16 = jnp.bfloat16
F32 = jnp.float32


def in_vmem():
    return pl.BlockSpec(memory_space=VMEM)


def in_smem():
    return pl.BlockSpec(memory_space=SMEM)


def params(mib):
    return pltpu.CompilerParams(vmem_limit_bytes=mib * 2**20)


class Plan:
    def __init__(self, n, ways, rows, blocks, page):
        self.n, self.rows, self.blocks, self.page = n, rows, blocks, page
        self.group = n // blocks
        self.halves = blocks == 2 and n == 8 and ways == 4 and rows * self.group == page
        self.cross = n // 2
        self.chunks = self.group if self.halves else 1

    def block(self, me, lb):
        return (me // self.group) ^ lb if self.halves else lb

    def offsets(self, me, lb, shape):
        row = lax.broadcasted_iota(jnp.int32, shape, 0) % self.page
        if not self.halves:
            return row
        mine = (me ^ (lb * self.cross)) % self.group
        return ((row // self.rows) ^ mine) * self.rows + row % self.rows


def fetch_kernel(plan, pages_dev, select_hbm, table_hbm, stands_hbm, keys, values, k_out, v_out, info, select, table, stands, rows, k_buf, v_buf, sems, int_sems):
    me = lax.axis_index("pages")
    blocks, heads = k_out.shape[:2]
    span = k_buf.shape[1]
    page = span // heads
    picked = k_out.shape[2] // page
    low = me * pages_dev
    loads = [
        pltpu.make_async_copy(a, b, int_sems.at[i])
        for i, (a, b) in enumerate(((select_hbm, select), (table_hbm, table), (stands_hbm, stands)))
    ]
    whole = [
        pltpu.make_async_copy(a, b, sems.at[i]) for i, (a, b) in enumerate(((keys, k_buf), (values, v_buf)))
    ]
    for load in loads + whole:
        load.start()
    row = lax.broadcasted_iota(jnp.int32, (span, span), 0)
    column = lax.broadcasted_iota(jnp.int32, (span, span), 1)
    apart = (column == (row % page) * heads + row // page).astype(F32).astype(BF16)
    for load in loads:
        load.wait()
    for lb in range(blocks):
        block = plan.block(me, lb)
        stand = stands[block]
        info[lb, 1] = plan.n * pages_dev
        info[lb, 2] = stand
        others = jnp.int32(0)
        count = jnp.int32(0)
        for i in range(select.shape[1]):
            logical = select[block, i]
            local = table[logical] - low
            mine = (local >= 0) & (local < pages_dev)
            own = logical == stand
            slot = jnp.where(own, 0, jnp.maximum(picked - 1 - others, 0))
            slot = jnp.where(mine, slot, picked)
            rows[lb, slot] = local
            rows[blocks + lb, slot] = logical
            one = mine.astype(jnp.int32)
            others = others + jnp.where(own, 0, one)
            count = count + one
        info[lb, 0] = count
        info[lb, 1] = rows[blocks + lb, 0]

    for load in whole:
        load.wait()
    for lb in range(blocks):

        @pl.when(info[lb, 0] > 0)
        def _(lb=lb):
            for g in range(heads):
                v_out[lb, g, :, LANES:] = jnp.ones((picked * page, LANES), BF16)
            for slot in range(picked):
                local = jnp.clip(rows[lb, slot], 0, pages_dev - 1)
                both = jnp.concatenate([k_buf[local], v_buf[local]], axis=1)
                split = jnp.dot(apart, both, preferred_element_type=F32).astype(BF16)
                for g in range(heads):
                    here = slice(slot * page, (slot + 1) * page)
                    k_out[lb, g, here, :] = split[g * page : (g + 1) * page, :LANES]
                    v_out[lb, g, here, :LANES] = split[g * page : (g + 1) * page, LANES:]


def fetch(plan, select, table, stands, keys, values):
    pages_dev, page, heads, size = keys.shape
    blocks, picked = select.shape[0], PICKED_PAGES
    span = page * heads
    return pl.pallas_call(
        functools.partial(fetch_kernel, plan, pages_dev),
        out_shape=(
            jax.ShapeDtypeStruct((blocks, heads, picked * page, size), BF16),
            jax.ShapeDtypeStruct((blocks, heads, picked * page, size + LANES), BF16),
            jax.ShapeDtypeStruct((blocks, 3), jnp.int32),
        ),
        in_specs=[pl.BlockSpec(memory_space=pltpu.HBM)] * 5,
        out_specs=(in_vmem(), in_vmem(), in_smem()),
        scratch_shapes=[
            SMEM(select.shape, jnp.int32),
            SMEM(table.shape, jnp.int32),
            SMEM(stands.shape, jnp.int32),
            SMEM((2 * blocks, picked + 1), jnp.int32),
            VMEM((pages_dev, span, size), BF16),
            VMEM((pages_dev, span, size), BF16),
            pltpu.SemaphoreType.DMA((2,)),
            pltpu.SemaphoreType.DMA((3,)),
        ],
        compiler_params=params(16),
        cost_estimate=pl.CostEstimate(flops=2 * 10**9, bytes_accessed=8 * 2**20, transcendentals=0),
    )(*(pltpu.with_memory_space_constraint(x, pltpu.HBM) for x in (select, table, stands, keys.reshape(pages_dev, span, size), values.reshape(pages_dev, span, size))))


def pack_stats(lse, heads):
    lane = lax.broadcasted_iota(jnp.int32, lse.shape, 1)
    high = lse.astype(BF16).astype(F32)
    rest = lse - high
    middle = rest.astype(BF16).astype(F32)
    low = rest - middle
    packed = jnp.where(lane < heads, high, 0.0)
    packed = packed + jnp.where((lane >= heads) & (lane < 2 * heads), pltpu.roll(middle, heads, 1), 0.0)
    packed = packed + jnp.where((lane >= 2 * heads) & (lane < 3 * heads), pltpu.roll(low, 2 * heads, 1), 0.0)
    return packed.astype(BF16)


def unpack_stats(packed, heads):
    wide = packed.astype(F32)
    return wide + pltpu.roll(wide, LANES - heads, 1) + pltpu.roll(wide, LANES - 2 * heads, 1)


def attend_kernel(plan, heads, lb, info, *refs):
    me = lax.axis_index("pages")
    chunks, page = plan.chunks, plan.page
    queries, (k_ref, v_ref), outs = refs[:chunks], refs[chunks : chunks + 2], refs[chunks + 2 :]
    kv_heads, size = k_ref.shape[1], k_ref.shape[3]
    repeat = heads // kv_heads
    width = heads * size
    part = page // chunks
    tile = math.gcd(repeat, HEADS_PER_TILE)
    scale = size**-0.5 * math.log2(math.e)
    lane = lax.broadcasted_iota(jnp.int32, (page, LANES), 1)

    @pl.when(info[lb, 0] > 0)
    def _():
        shape = (tile * page, page)
        key_pos = info[lb, 1] * page + lax.broadcasted_iota(jnp.int32, shape, 1)
        query_pos = info[lb, 2] * page + plan.offsets(me, lb, shape)
        allowed = key_pos <= query_pos
        stats = jnp.zeros((page, LANES), F32)
        def product(first):
            q = jnp.concatenate(
                [m[:, h * size : (h + 1) * size] for h in range(first, first + tile) for m in queries], axis=0
            )
            return lax.dot_general(q, k_ref[lb, first // repeat], (((1,), (1,)), ((), ())), preferred_element_type=F32)

        ahead = product(0)
        for first in range(0, heads, tile):
            scores = scale * ahead
            if first + tile < heads:
                ahead = product(first + tile)
            scores = jnp.concatenate([jnp.where(allowed, scores[:, :page], FLOOR), scores[:, page:]], axis=1)
            peak = jnp.max(scores, axis=1, keepdims=True)
            weights = jnp.exp2(scores - peak).astype(BF16)
            both = jnp.dot(weights, v_ref[lb, first // repeat], preferred_element_type=F32)
            total = both[:, size:]
            out = (both[:, :size] / total).astype(BF16)
            lse = peak + jnp.log2(total)
            for i in range(tile):
                h = first + i
                stats = jnp.where(lane == h, lse[i * page : (i + 1) * page], stats)
                for c in range(chunks):
                    outs[c][:, h * size : (h + 1) * size] = out[i * page + c * part : i * page + (c + 1) * part]
        packed = pack_stats(stats, heads)
        for c in range(chunks):
            outs[c][:, width:] = packed[c * part : (c + 1) * part]

    @pl.when(info[lb, 0] == 0)
    def _():
        for c in range(chunks):
            outs[c][:, :width] = jnp.zeros((part, width), BF16)
            outs[c][:, width:] = pack_stats(jnp.full((part, LANES), FLOOR, F32), heads)


def attend(plan, heads, lb, pages, queries):
    keys, values, info = pages
    part = plan.page // plan.chunks
    shape = jax.ShapeDtypeStruct((part, queries[0].shape[1] + LANES), BF16)
    return pl.pallas_call(
        functools.partial(attend_kernel, plan, heads, lb),
        out_shape=(shape,) * plan.chunks,
        in_specs=[in_smem()] + [in_vmem()] * (len(queries) + 2),
        out_specs=(in_vmem(),) * plan.chunks,
        compiler_params=params(32),
        cost_estimate=pl.CostEstimate(flops=2 * 10**9, bytes_accessed=4 * 2**20, transcendentals=10**6),
    )(info, *queries, keys, values)


def merged(parts, stats):
    top = functools.reduce(jnp.maximum, stats)
    shares = [jnp.exp2(s - top) for s in stats]
    total = functools.reduce(jnp.add, shares)
    shares = [s / total for s in shares]

    def head(h):
        return functools.reduce(
            jnp.add, [p(h).astype(F32) * s[:, h : h + 1] for p, s in zip(parts, shares, strict=True)]
        )

    return head, top + jnp.log2(total)


def merge_kernel(heads, *refs):
    sources, out = refs[:-1], refs[-1]
    width = out.shape[1] - LANES
    size = width // heads
    head, lse = merged([heads_of(r, size) for r in sources], [unpack_stats(r[:, width:], heads) for r in sources])
    for h in range(heads):
        out[:, h * size : (h + 1) * size] = head(h).astype(BF16)
    out[:, width:] = pack_stats(lse, heads)


def merge(heads, *sources):
    return pl.pallas_call(
        functools.partial(merge_kernel, heads),
        out_shape=jax.ShapeDtypeStruct(sources[0].shape, BF16),
        in_specs=[in_vmem()] * len(sources),
        out_specs=in_vmem(),
        compiler_params=params(8),
    )(*sources)


def heads_of(ref, size):
    return lambda h: ref[:, h * size : (h + 1) * size]


def finish_kernel(heads, near, far, out):
    width = out.shape[1]
    size = width // heads
    head, _ = merged([heads_of(r, size) for r in (near, far)], [unpack_stats(r[:, width:], heads) for r in (near, far)])
    for h in range(heads):
        out[:, h * size : (h + 1) * size] = head(h).astype(BF16)


def finish(heads, near, far):
    return pl.pallas_call(
        functools.partial(finish_kernel, heads),
        out_shape=jax.ShapeDtypeStruct((near.shape[0], near.shape[1] - LANES), BF16),
        in_specs=[in_vmem()] * 2,
        out_specs=in_vmem(),
        compiler_params=params(8),
    )(near, far)


def project_kernel(plan, lb, *refs):
    sources, weight, (keep, send, rows_ref) = refs[: plan.group], refs[plan.group], refs[plan.group + 1 :]
    me, column = lax.axis_index("pages"), lax.axis_index("mp")
    rows = plan.rows
    holders = plan.group // 2
    for k in range(plan.group):
        device = me ^ k ^ (lb * plan.cross)
        place = ((device // holders % 2) ^ (column % 2)) * holders + device % holders
        rows_ref[pl.ds(pl.multiple_of(place * rows, rows), rows), :] = sources[k][...]
    product = jnp.dot(rows_ref[...], weight[...], preferred_element_type=F32)
    part = holders * rows
    keep[...] = product[:part]
    send[...] = product[part:].astype(BF16)


def project(plan, lb, sources, weight):
    columns = weight.shape[1]
    part = plan.page // 2
    return pl.pallas_call(
        functools.partial(project_kernel, plan, lb),
        out_shape=(jax.ShapeDtypeStruct((part, columns), F32), jax.ShapeDtypeStruct((part, columns), BF16)),
        in_specs=[in_vmem()] * (plan.group + 1),
        out_specs=(in_vmem(), in_vmem()),
        scratch_shapes=[VMEM((plan.page, weight.shape[0]), BF16)],
        compiler_params=params(24),
    )(*(sources[k] for k in range(plan.group)), weight)


def swap(x, axis, distance):
    n = lax.axis_size(axis)
    return lax.ppermute(x, axis, [(i, i ^ distance) for i in range(n)])


def others(plan):
    return range(1, plan.group)


def spread(x, plan):
    return {0: x} | {k: swap(x, "pages", k) for k in others(plan)}


def by_halves(plan, heads, queries, weight, pages):
    far = swap(queries, "pages", plan.cross)
    near = []
    for lb, rows in enumerate((queries, far)):
        chunks = spread(rows, plan)
        outs = attend(plan, heads, lb, pages, [chunks[k] for k in range(plan.group)])
        near.append(merge(heads, *(swap(outs[k], "pages", k) for k in reversed(others(plan))), outs[0]))
    across = [swap(x, "pages", plan.cross) for x in near]
    sums = [None, None]
    for lb in (1, 0):
        rows = finish(heads, near[lb], across[1 - lb])
        keep, send = project(plan, lb, spread(rows, plan), weight)
        sums[lb] = keep + swap(send, "mp", 1).astype(F32)
    stays = plan.block(lax.axis_index("pages"), 0) == lax.axis_index("mp") // 2
    mine = jnp.where(stays, sums[0], sums[1])
    away = jnp.where(stays, sums[1], sums[0]).astype(BF16)
    return (mine + swap(away, "mp", 2).astype(F32)).astype(BF16)


def by_gathers(plan, heads, queries, weight, pages):
    width = queries.shape[1]
    size = width // heads
    gathered = lax.all_gather(queries, "pages", axis=0, tiled=True)
    rows = gathered.shape[0]
    outs = [
        attend(plan, heads, lb, pages, [gathered[lb * plan.page : (lb + 1) * plan.page]])[0]
        for lb in range(plan.blocks)
    ]
    out = jnp.concatenate(outs, axis=0)
    packed = out[:, width : width + 3 * heads].astype(F32)
    lse = packed[:, :heads] + packed[:, heads : 2 * heads] + packed[:, 2 * heads :]
    every = lax.all_gather(lse, "pages")
    top = jnp.max(every, axis=0)
    share = jnp.exp2(lse - top) / jnp.sum(jnp.exp2(every - top), axis=0)
    part = (out[:, :width].reshape(rows, heads, size).astype(F32) * share[..., None]).reshape(1, rows, width)
    received = lax.all_to_all(part.astype(BF16), "pages", split_axis=1, concat_axis=0, tiled=True)
    mixed = jnp.sum(received, axis=0, dtype=F32).astype(BF16)
    terms = jnp.dot(lax.all_gather(mixed, "pages", axis=0, tiled=True), weight, preferred_element_type=F32)
    return lax.psum_scatter(terms, "mp", scatter_dimension=0, tiled=True).astype(BF16)


def per_device(queries, cached_keys, cached_values, out_weight, select, page_table, block_page):
    n, ways = lax.axis_size("pages"), lax.axis_size("mp")
    plan = Plan(n, ways, queries.shape[0], select.shape[0], cached_keys.shape[1])
    heads = queries.shape[1] // cached_keys.shape[3]
    pages = fetch(plan, select, page_table, block_page, cached_keys, cached_values)
    way = by_halves if plan.halves else by_gathers
    return way(plan, heads, queries, out_weight, pages)


def solution(mesh):
    placed = (
        P("pages", "mp"),
        P("pages", None, "mp", None),
        P("pages", None, "mp", None),
        P("mp", "pages"),
        P(),
        P(),
        P(),
    )
    return jax.shard_map(
        per_device, mesh=mesh, in_specs=placed, out_specs=P("mp", "pages"), check_vma=False
    )
```

```python
import functools
import math

import jax
import jax.numpy as jnp
from jax import lax
from jax.experimental import pallas as pl
from jax.experimental.pallas import tpu as pltpu
from jax.sharding import PartitionSpec as P

PICKED_PAGES = 6
FLOOR = -1e30
LANES = 128
HEADS_PER_TILE = 2

VMEM = pltpu.VMEM
SMEM = pltpu.SMEM
BF16 = jnp.bfloat16
F32 = jnp.float32


def in_vmem():
    return pl.BlockSpec(memory_space=VMEM)


def in_smem():
    return pl.BlockSpec(memory_space=SMEM)


def params(mib):
    return pltpu.CompilerParams(vmem_limit_bytes=mib * 2**20)


class Plan:
    def __init__(self, n, ways, rows, blocks, page):
        self.n, self.rows, self.blocks, self.page = n, rows, blocks, page
        self.group = n // blocks
        self.halves = blocks == 2 and n == 8 and ways == 4 and rows * self.group == page
        self.cross = n * 3 // 4
        self.chunks = self.group if self.halves else 1

    def block(self, me, lb):
        return (me // self.group) ^ lb if self.halves else lb

    def offsets(self, me, lb, shape):
        row = lax.broadcasted_iota(jnp.int32, shape, 0) % self.page
        if not self.halves:
            return row
        mine = (me ^ (lb * self.cross)) % self.group
        return ((row // self.rows) ^ mine) * self.rows + row % self.rows


def fetch_kernel(plan, pages_dev, select_hbm, table_hbm, stands_hbm, keys, values, k_out, v_out, info, select, table, stands, rows, k_buf, v_buf, sems, int_sems):
    me = lax.axis_index("pages")
    blocks, heads = k_out.shape[:2]
    span = k_buf.shape[1]
    page = span // heads
    picked = k_out.shape[2] // page
    low = me * pages_dev
    loads = [
        pltpu.make_async_copy(a, b, int_sems.at[i])
        for i, (a, b) in enumerate(((select_hbm, select), (table_hbm, table), (stands_hbm, stands)))
    ]
    whole = [
        pltpu.make_async_copy(a, b, sems.at[i]) for i, (a, b) in enumerate(((keys, k_buf), (values, v_buf)))
    ]
    for load in loads + whole:
        load.start()
    row = lax.broadcasted_iota(jnp.int32, (span, span), 0)
    column = lax.broadcasted_iota(jnp.int32, (span, span), 1)
    apart = (column == (row % page) * heads + row // page).astype(F32).astype(BF16)
    for load in loads:
        load.wait()
    for lb in range(blocks):
        block = plan.block(me, lb)
        stand = stands[block]
        info[lb, 1] = plan.n * pages_dev
        info[lb, 2] = stand
        others = jnp.int32(0)
        count = jnp.int32(0)
        for i in range(select.shape[1]):
            logical = select[block, i]
            local = table[logical] - low
            mine = (local >= 0) & (local < pages_dev)
            own = logical == stand
            slot = jnp.where(own, 0, jnp.maximum(picked - 1 - others, 0))
            slot = jnp.where(mine, slot, picked)
            rows[lb, slot] = local
            rows[blocks + lb, slot] = logical
            one = mine.astype(jnp.int32)
            others = others + jnp.where(own, 0, one)
            count = count + one
        info[lb, 0] = count
        info[lb, 1] = rows[blocks + lb, 0]

    for load in whole:
        load.wait()
    for lb in range(blocks):

        @pl.when(info[lb, 0] > 0)
        def _(lb=lb):
            for g in range(heads):
                v_out[lb, g, :, LANES:] = jnp.ones((picked * page, LANES), BF16)
            for slot in range(picked):
                local = jnp.clip(rows[lb, slot], 0, pages_dev - 1)
                both = jnp.concatenate([k_buf[local], v_buf[local]], axis=1)
                split = jnp.dot(apart, both, preferred_element_type=F32).astype(BF16)
                for g in range(heads):
                    here = slice(slot * page, (slot + 1) * page)
                    k_out[lb, g, here, :] = split[g * page : (g + 1) * page, :LANES]
                    v_out[lb, g, here, :LANES] = split[g * page : (g + 1) * page, LANES:]


def fetch(plan, select, table, stands, keys, values):
    pages_dev, page, heads, size = keys.shape
    blocks, picked = select.shape[0], PICKED_PAGES
    span = page * heads
    return pl.pallas_call(
        functools.partial(fetch_kernel, plan, pages_dev),
        out_shape=(
            jax.ShapeDtypeStruct((blocks, heads, picked * page, size), BF16),
            jax.ShapeDtypeStruct((blocks, heads, picked * page, size + LANES), BF16),
            jax.ShapeDtypeStruct((blocks, 3), jnp.int32),
        ),
        in_specs=[pl.BlockSpec(memory_space=pltpu.HBM)] * 5,
        out_specs=(in_vmem(), in_vmem(), in_smem()),
        scratch_shapes=[
            SMEM(select.shape, jnp.int32),
            SMEM(table.shape, jnp.int32),
            SMEM(stands.shape, jnp.int32),
            SMEM((2 * blocks, picked + 1), jnp.int32),
            VMEM((pages_dev, span, size), BF16),
            VMEM((pages_dev, span, size), BF16),
            pltpu.SemaphoreType.DMA((2,)),
            pltpu.SemaphoreType.DMA((3,)),
        ],
        compiler_params=params(16),
        cost_estimate=pl.CostEstimate(flops=2 * 10**9, bytes_accessed=8 * 2**20, transcendentals=0),
    )(*(pltpu.with_memory_space_constraint(x, pltpu.HBM) for x in (select, table, stands, keys.reshape(pages_dev, span, size), values.reshape(pages_dev, span, size))))


def pack_stats(lse, heads):
    lane = lax.broadcasted_iota(jnp.int32, lse.shape, 1)
    high = lse.astype(BF16).astype(F32)
    rest = lse - high
    middle = rest.astype(BF16).astype(F32)
    low = rest - middle
    packed = jnp.where(lane < heads, high, 0.0)
    packed = packed + jnp.where((lane >= heads) & (lane < 2 * heads), pltpu.roll(middle, heads, 1), 0.0)
    packed = packed + jnp.where((lane >= 2 * heads) & (lane < 3 * heads), pltpu.roll(low, 2 * heads, 1), 0.0)
    return packed.astype(BF16)


def unpack_stats(packed, heads):
    wide = packed.astype(F32)
    return wide + pltpu.roll(wide, LANES - heads, 1) + pltpu.roll(wide, LANES - 2 * heads, 1)


def attend_kernel(plan, heads, lb, info, *refs):
    me = lax.axis_index("pages")
    chunks, page = plan.chunks, plan.page
    queries, (k_ref, v_ref), outs = refs[:chunks][::-1], refs[chunks : chunks + 2], refs[chunks + 2 :]
    kv_heads, size = k_ref.shape[1], k_ref.shape[3]
    repeat = heads // kv_heads
    width = heads * size
    part = page // chunks
    tile = math.gcd(repeat, HEADS_PER_TILE)
    scale = size**-0.5 * math.log2(math.e)
    lane = lax.broadcasted_iota(jnp.int32, (page, LANES), 1)

    @pl.when(info[lb, 0] > 0)
    def _():
        shape = (tile * page, page)
        key_pos = info[lb, 1] * page + lax.broadcasted_iota(jnp.int32, shape, 1)
        query_pos = info[lb, 2] * page + plan.offsets(me, lb, shape)
        allowed = key_pos <= query_pos
        stats = jnp.zeros((page, LANES), F32)
        def product(first):
            q = jnp.concatenate(
                [m[:, h * size : (h + 1) * size] for h in range(first, first + tile) for m in queries], axis=0
            )
            return lax.dot_general(q, k_ref[lb, first // repeat], (((1,), (1,)), ((), ())), preferred_element_type=F32)

        ahead = product(0)
        for first in range(0, heads, tile):
            scores = scale * ahead
            if first + tile < heads:
                ahead = product(first + tile)
            scores = jnp.concatenate([jnp.where(allowed, scores[:, :page], FLOOR), scores[:, page:]], axis=1)
            peak = jnp.max(scores, axis=1, keepdims=True)
            weights = jnp.exp2(scores - peak).astype(BF16)
            both = jnp.dot(weights, v_ref[lb, first // repeat], preferred_element_type=F32)
            total = both[:, size:]
            out = (both[:, :size] / total).astype(BF16)
            lse = peak + jnp.log2(total)
            for i in range(tile):
                h = first + i
                stats = jnp.where(lane == h, lse[i * page : (i + 1) * page], stats)
                for c in range(chunks):
                    outs[c][:, h * size : (h + 1) * size] = out[i * page + c * part : i * page + (c + 1) * part]
        packed = pack_stats(stats, heads)
        for c in range(chunks):
            outs[c][:, width:] = packed[c * part : (c + 1) * part]

    @pl.when(info[lb, 0] == 0)
    def _():
        for c in range(chunks):
            outs[c][:, :width] = jnp.zeros((part, width), BF16)
            outs[c][:, width:] = pack_stats(jnp.full((part, LANES), FLOOR, F32), heads)


def attend(plan, heads, lb, pages, queries):
    keys, values, info = pages
    part = plan.page // plan.chunks
    shape = jax.ShapeDtypeStruct((part, queries[0].shape[1] + LANES), BF16)
    return pl.pallas_call(
        functools.partial(attend_kernel, plan, heads, lb),
        out_shape=(shape,) * plan.chunks,
        in_specs=[in_smem()] + [in_vmem()] * (len(queries) + 2),
        out_specs=(in_vmem(),) * plan.chunks,
        compiler_params=params(32),
        cost_estimate=pl.CostEstimate(flops=2 * 10**9, bytes_accessed=4 * 2**20, transcendentals=10**6),
    )(info, *queries[::-1], keys, values)


def merged(parts, stats):
    top = functools.reduce(jnp.maximum, stats)
    shares = [jnp.exp2(s - top) for s in stats]
    total = functools.reduce(jnp.add, shares)
    shares = [s / total for s in shares]

    def head(h):
        return functools.reduce(
            jnp.add, [p(h).astype(F32) * s[:, h : h + 1] for p, s in zip(parts, shares, strict=True)]
        )

    return head, top + jnp.log2(total)


def merge_kernel(heads, *refs):
    sources, out = refs[:-1], refs[-1]
    width = out.shape[1] - LANES
    size = width // heads
    head, lse = merged([heads_of(r, size) for r in sources], [unpack_stats(r[:, width:], heads) for r in sources])
    for h in range(heads):
        out[:, h * size : (h + 1) * size] = head(h).astype(BF16)
    out[:, width:] = pack_stats(lse, heads)


def merge(heads, *sources):
    return pl.pallas_call(
        functools.partial(merge_kernel, heads),
        out_shape=jax.ShapeDtypeStruct(sources[0].shape, BF16),
        in_specs=[in_vmem()] * len(sources),
        out_specs=in_vmem(),
        compiler_params=params(8),
    )(*sources)


def heads_of(ref, size):
    return lambda h: ref[:, h * size : (h + 1) * size]


def finish_kernel(heads, near, far, out):
    width = out.shape[1]
    size = width // heads
    head, _ = merged([heads_of(r, size) for r in (near, far)], [unpack_stats(r[:, width:], heads) for r in (near, far)])
    for h in range(heads):
        out[:, h * size : (h + 1) * size] = head(h).astype(BF16)


def finish(heads, near, far):
    return pl.pallas_call(
        functools.partial(finish_kernel, heads),
        out_shape=jax.ShapeDtypeStruct((near.shape[0], near.shape[1] - LANES), BF16),
        in_specs=[in_vmem()] * 2,
        out_specs=in_vmem(),
        compiler_params=params(8),
    )(near, far)


def project_kernel(plan, lb, *refs):
    sources, weight, (keep, send, rows_ref) = refs[: plan.group], refs[plan.group], refs[plan.group + 1 :]
    me, column = lax.axis_index("pages"), lax.axis_index("mp")
    rows = plan.rows
    holders = plan.group // 2
    for k in range(plan.group):
        device = me ^ k ^ (lb * plan.cross)
        place = ((device // holders % 2) ^ (column % 2)) * holders + device % holders
        rows_ref[pl.ds(pl.multiple_of(place * rows, rows), rows), :] = sources[k][...]
    product = jnp.dot(rows_ref[...], weight[...], preferred_element_type=F32)
    part = holders * rows
    keep[...] = product[:part]
    send[...] = product[part:].astype(BF16)


def project(plan, lb, sources, weight):
    columns = weight.shape[1]
    part = plan.page // 2
    return pl.pallas_call(
        functools.partial(project_kernel, plan, lb),
        out_shape=(jax.ShapeDtypeStruct((part, columns), F32), jax.ShapeDtypeStruct((part, columns), BF16)),
        in_specs=[in_vmem()] * (plan.group + 1),
        out_specs=(in_vmem(), in_vmem()),
        scratch_shapes=[VMEM((plan.page, weight.shape[0]), BF16)],
        compiler_params=params(24),
    )(*(sources[k] for k in range(plan.group)), weight)


def swap(x, axis, distance):
    n = lax.axis_size(axis)
    return lax.ppermute(x, axis, [(i, i ^ distance) for i in range(n)])


def others(plan):
    return range(1, plan.group)


def spread(x, plan):
    return {0: x} | {k: swap(x, "pages", k) for k in others(plan)}


def by_halves(plan, heads, queries, weight, pages):
    far = swap(queries, "pages", plan.cross)
    near = []
    for lb, rows in enumerate((queries, far)):
        chunks = spread(rows, plan)
        outs = attend(plan, heads, lb, pages, [chunks[k] for k in range(plan.group)])
        near.append(merge(heads, outs[0], *(swap(outs[k], "pages", k) for k in others(plan))))
    across = [swap(x, "pages", plan.cross) for x in near]
    sums = [None, None]
    for lb in (1, 0):
        rows = finish(heads, near[lb], across[1 - lb])
        keep, send = project(plan, lb, spread(rows, plan), weight)
        sums[lb] = keep + swap(send, "mp", 1).astype(F32)
    stays = plan.block(lax.axis_index("pages"), 0) == lax.axis_index("mp") // 2
    mine = jnp.where(stays, sums[0], sums[1])
    away = jnp.where(stays, sums[1], sums[0]).astype(BF16)
    return (mine + swap(away, "mp", 2).astype(F32)).astype(BF16)


def by_gathers(plan, heads, queries, weight, pages):
    width = queries.shape[1]
    size = width // heads
    gathered = lax.all_gather(queries, "pages", axis=0, tiled=True)
    rows = gathered.shape[0]
    outs = [
        attend(plan, heads, lb, pages, [gathered[lb * plan.page : (lb + 1) * plan.page]])[0]
        for lb in range(plan.blocks)
    ]
    out = jnp.concatenate(outs, axis=0)
    packed = out[:, width : width + 3 * heads].astype(F32)
    lse = packed[:, :heads] + packed[:, heads : 2 * heads] + packed[:, 2 * heads :]
    every = lax.all_gather(lse, "pages")
    top = jnp.max(every, axis=0)
    share = jnp.exp2(lse - top) / jnp.sum(jnp.exp2(every - top), axis=0)
    part = (out[:, :width].reshape(rows, heads, size).astype(F32) * share[..., None]).reshape(1, rows, width)
    received = lax.all_to_all(part.astype(BF16), "pages", split_axis=1, concat_axis=0, tiled=True)
    mixed = jnp.sum(received, axis=0, dtype=F32).astype(BF16)
    terms = jnp.dot(lax.all_gather(mixed, "pages", axis=0, tiled=True), weight, preferred_element_type=F32)
    return lax.psum_scatter(terms, "mp", scatter_dimension=0, tiled=True).astype(BF16)


def per_device(queries, cached_keys, cached_values, out_weight, select, page_table, block_page):
    n, ways = lax.axis_size("pages"), lax.axis_size("mp")
    plan = Plan(n, ways, queries.shape[0], select.shape[0], cached_keys.shape[1])
    heads = queries.shape[1] // cached_keys.shape[3]
    pages = fetch(plan, select, page_table, block_page, cached_keys, cached_values)
    way = by_halves if plan.halves else by_gathers
    return way(plan, heads, queries, out_weight, pages)


def solution(mesh):
    placed = (
        P("pages", "mp"),
        P("pages", None, "mp", None),
        P("pages", None, "mp", None),
        P("mp", "pages"),
        P(),
        P(),
        P(),
    )
    return jax.shard_map(
        per_device, mesh=mesh, in_specs=placed, out_specs=P("mp", "pages"), check_vma=False
    )
```

```python
import functools
import math

import jax
import jax.numpy as jnp
from jax import lax
from jax.experimental import pallas as pl
from jax.experimental.pallas import tpu as pltpu
from jax.sharding import PartitionSpec as P

PICKED_PAGES = 6
FLOOR = -1e30
LANES = 128
HEADS_PER_TILE = 2

VMEM = pltpu.VMEM
SMEM = pltpu.SMEM
BF16 = jnp.bfloat16
F32 = jnp.float32


def in_vmem():
    return pl.BlockSpec(memory_space=VMEM)


def in_smem():
    return pl.BlockSpec(memory_space=SMEM)


def params(mib):
    return pltpu.CompilerParams(vmem_limit_bytes=mib * 2**20)


class Plan:
    def __init__(self, n, ways, rows, blocks, page):
        self.n, self.rows, self.blocks, self.page = n, rows, blocks, page
        self.group = n // blocks
        self.halves = blocks == 2 and n == 8 and ways == 4 and rows * self.group == page
        self.cross = n * 3 // 4
        self.chunks = self.group if self.halves else 1

    def block(self, me, lb):
        return (me // self.group) ^ lb if self.halves else lb

    def offsets(self, me, lb, shape):
        row = lax.broadcasted_iota(jnp.int32, shape, 0) % self.page
        if not self.halves:
            return row
        mine = (me ^ (lb * self.cross)) % self.group
        return ((row // self.rows) ^ mine) * self.rows + row % self.rows


def fetch_kernel(plan, pages_dev, select_hbm, table_hbm, stands_hbm, keys, values, k_out, v_out, info, select, table, stands, rows, k_buf, v_buf, sems, int_sems):
    me = lax.axis_index("pages")
    blocks, heads = k_out.shape[:2]
    span = k_buf.shape[1]
    page = span // heads
    picked = k_out.shape[2] // page
    low = me * pages_dev
    loads = [
        pltpu.make_async_copy(a, b, int_sems.at[i])
        for i, (a, b) in enumerate(((select_hbm, select), (table_hbm, table), (stands_hbm, stands)))
    ]
    whole = [
        pltpu.make_async_copy(a, b, sems.at[i]) for i, (a, b) in enumerate(((keys, k_buf), (values, v_buf)))
    ]
    for load in loads + whole:
        load.start()
    row = lax.broadcasted_iota(jnp.int32, (span, span), 0)
    column = lax.broadcasted_iota(jnp.int32, (span, span), 1)
    apart = (column == (row % page) * heads + row // page).astype(F32).astype(BF16)
    for load in loads:
        load.wait()
    for lb in range(blocks):
        block = plan.block(me, lb)
        stand = stands[block]
        info[lb, 1] = plan.n * pages_dev
        info[lb, 2] = stand
        others = jnp.int32(0)
        count = jnp.int32(0)
        for i in range(select.shape[1]):
            logical = select[block, i]
            local = table[logical] - low
            mine = (local >= 0) & (local < pages_dev)
            own = logical == stand
            slot = jnp.where(own, 0, jnp.maximum(picked - 1 - others, 0))
            slot = jnp.where(mine, slot, picked)
            rows[lb, slot] = local
            rows[blocks + lb, slot] = logical
            one = mine.astype(jnp.int32)
            others = others + jnp.where(own, 0, one)
            count = count + one
        info[lb, 0] = count
        info[lb, 1] = rows[blocks + lb, 0]

    for load in whole:
        load.wait()
    for lb in range(blocks):

        @pl.when(info[lb, 0] > 0)
        def _(lb=lb):
            for g in range(heads):
                v_out[lb, g, :, LANES:] = jnp.ones((picked * page, LANES), BF16)
            for slot in range(picked):
                local = jnp.clip(rows[lb, slot], 0, pages_dev - 1)
                both = jnp.concatenate([k_buf[local], v_buf[local]], axis=1)
                split = jnp.dot(apart, both, preferred_element_type=F32).astype(BF16)
                for g in range(heads):
                    here = slice(slot * page, (slot + 1) * page)
                    k_out[lb, g, here, :] = split[g * page : (g + 1) * page, :LANES]
                    v_out[lb, g, here, :LANES] = split[g * page : (g + 1) * page, LANES:]


def fetch(plan, select, table, stands, keys, values):
    pages_dev, page, heads, size = keys.shape
    blocks, picked = select.shape[0], PICKED_PAGES
    span = page * heads
    return pl.pallas_call(
        functools.partial(fetch_kernel, plan, pages_dev),
        out_shape=(
            jax.ShapeDtypeStruct((blocks, heads, picked * page, size), BF16),
            jax.ShapeDtypeStruct((blocks, heads, picked * page, size + LANES), BF16),
            jax.ShapeDtypeStruct((blocks, 3), jnp.int32),
        ),
        in_specs=[pl.BlockSpec(memory_space=pltpu.HBM)] * 5,
        out_specs=(in_vmem(), in_vmem(), in_smem()),
        scratch_shapes=[
            SMEM(select.shape, jnp.int32),
            SMEM(table.shape, jnp.int32),
            SMEM(stands.shape, jnp.int32),
            SMEM((2 * blocks, picked + 1), jnp.int32),
            VMEM((pages_dev, span, size), BF16),
            VMEM((pages_dev, span, size), BF16),
            pltpu.SemaphoreType.DMA((2,)),
            pltpu.SemaphoreType.DMA((3,)),
        ],
        compiler_params=params(16),
        cost_estimate=pl.CostEstimate(flops=2 * 10**9, bytes_accessed=8 * 2**20, transcendentals=0),
    )(*(pltpu.with_memory_space_constraint(x, pltpu.HBM) for x in (select, table, stands, keys.reshape(pages_dev, span, size), values.reshape(pages_dev, span, size))))


def pack_stats(lse, heads):
    lane = lax.broadcasted_iota(jnp.int32, lse.shape, 1)
    high = lse.astype(BF16).astype(F32)
    rest = lse - high
    middle = rest.astype(BF16).astype(F32)
    low = rest - middle
    packed = jnp.where(lane < heads, high, 0.0)
    packed = packed + jnp.where((lane >= heads) & (lane < 2 * heads), pltpu.roll(middle, heads, 1), 0.0)
    packed = packed + jnp.where((lane >= 2 * heads) & (lane < 3 * heads), pltpu.roll(low, 2 * heads, 1), 0.0)
    return packed.astype(BF16)


def unpack_stats(packed, heads):
    wide = packed.astype(F32)
    return wide + pltpu.roll(wide, LANES - heads, 1) + pltpu.roll(wide, LANES - 2 * heads, 1)


def attend_kernel(plan, heads, lb, info, *refs):
    me = lax.axis_index("pages")
    chunks, page = plan.chunks, plan.page
    queries, (k_ref, v_ref), outs = refs[:chunks][::-1], refs[chunks : chunks + 2], refs[chunks + 2 :]
    kv_heads, size = k_ref.shape[1], k_ref.shape[3]
    repeat = heads // kv_heads
    width = heads * size
    part = page // chunks
    tile = math.gcd(repeat, HEADS_PER_TILE)
    scale = size**-0.5 * math.log2(math.e)
    lane = lax.broadcasted_iota(jnp.int32, (page, LANES), 1)

    @pl.when(info[lb, 0] > 0)
    def _():
        shape = (tile * page, page)
        key_pos = info[lb, 1] * page + lax.broadcasted_iota(jnp.int32, shape, 1)
        query_pos = info[lb, 2] * page + plan.offsets(me, lb, shape)
        allowed = key_pos <= query_pos
        stats = jnp.zeros((page, LANES), F32)
        def product(first):
            q = jnp.concatenate(
                [m[:, h * size : (h + 1) * size] for h in range(first, first + tile) for m in queries], axis=0
            )
            return lax.dot_general(q, k_ref[lb, first // repeat], (((1,), (1,)), ((), ())), preferred_element_type=F32)

        ahead = product(0)
        for first in range(0, heads, tile):
            scores = scale * ahead
            if first + tile < heads:
                ahead = product(first + tile)
            scores = jnp.concatenate([jnp.where(allowed, scores[:, :page], FLOOR), scores[:, page:]], axis=1)
            peak = jnp.max(scores, axis=1, keepdims=True)
            weights = jnp.exp2(scores - peak).astype(BF16)
            both = jnp.dot(weights, v_ref[lb, first // repeat], preferred_element_type=F32)
            total = both[:, size:]
            out = (both[:, :size] / total).astype(BF16)
            lse = peak + jnp.log2(total)
            for i in range(tile):
                h = first + i
                stats = jnp.where(lane == h, lse[i * page : (i + 1) * page], stats)
                for c in range(chunks):
                    outs[c][:, h * size : (h + 1) * size] = out[i * page + c * part : i * page + (c + 1) * part]
        packed = pack_stats(stats, heads)
        for c in range(chunks):
            outs[c][:, width:] = packed[c * part : (c + 1) * part]

    @pl.when(info[lb, 0] == 0)
    def _():
        for c in range(chunks):
            outs[c][:, :width] = jnp.zeros((part, width), BF16)
            outs[c][:, width:] = pack_stats(jnp.full((part, LANES), FLOOR, F32), heads)


def attend(plan, heads, lb, pages, queries):
    keys, values, info = pages
    part = plan.page // plan.chunks
    shape = jax.ShapeDtypeStruct((part, queries[0].shape[1] + LANES), BF16)
    return pl.pallas_call(
        functools.partial(attend_kernel, plan, heads, lb),
        out_shape=(shape,) * plan.chunks,
        in_specs=[in_smem()] + [in_vmem()] * (len(queries) + 2),
        out_specs=(in_vmem(),) * plan.chunks,
        compiler_params=params(32),
        cost_estimate=pl.CostEstimate(flops=2 * 10**9, bytes_accessed=4 * 2**20, transcendentals=10**6),
    )(info, *queries[::-1], keys, values)


def merged(parts, stats):
    top = functools.reduce(jnp.maximum, stats)
    shares = [jnp.exp2(s - top) for s in stats]
    total = functools.reduce(jnp.add, shares)
    shares = [s / total for s in shares]

    def head(h):
        return functools.reduce(
            jnp.add, [p(h).astype(F32) * s[:, h : h + 1] for p, s in zip(parts, shares, strict=True)]
        )

    return head, top + jnp.log2(total)


def merge_kernel(heads, *refs):
    sources, out = refs[:-1], refs[-1]
    width = out.shape[1] - LANES
    size = width // heads
    head, lse = merged([heads_of(r, size) for r in sources], [unpack_stats(r[:, width:], heads) for r in sources])
    for h in range(heads):
        out[:, h * size : (h + 1) * size] = head(h).astype(BF16)
    out[:, width:] = pack_stats(lse, heads)


def merge(heads, *sources):
    return pl.pallas_call(
        functools.partial(merge_kernel, heads),
        out_shape=jax.ShapeDtypeStruct(sources[0].shape, BF16),
        in_specs=[in_vmem()] * len(sources),
        out_specs=in_vmem(),
        compiler_params=params(8),
    )(*sources)


def heads_of(ref, size):
    return lambda h: ref[:, h * size : (h + 1) * size]


def finish_kernel(heads, near, far, out):
    width = out.shape[1]
    size = width // heads
    head, _ = merged([heads_of(r, size) for r in (near, far)], [unpack_stats(r[:, width:], heads) for r in (near, far)])
    for h in range(heads):
        out[:, h * size : (h + 1) * size] = head(h).astype(BF16)


def finish(heads, near, far):
    return pl.pallas_call(
        functools.partial(finish_kernel, heads),
        out_shape=jax.ShapeDtypeStruct((near.shape[0], near.shape[1] - LANES), BF16),
        in_specs=[in_vmem()] * 2,
        out_specs=in_vmem(),
        compiler_params=params(8),
    )(near, far)


def project_kernel(plan, lb, *refs):
    sources, weight, (keep, send, rows_ref) = refs[: plan.group], refs[plan.group], refs[plan.group + 1 :]
    me, column = lax.axis_index("pages"), lax.axis_index("mp")
    rows = plan.rows
    holders = plan.group // 2
    for k in range(plan.group):
        device = me ^ k ^ (lb * plan.cross)
        place = ((device // holders % 2) ^ (column % 2)) * holders + device % holders
        rows_ref[pl.ds(pl.multiple_of(place * rows, rows), rows), :] = sources[k][...]
    product = jnp.dot(rows_ref[...], weight[...], preferred_element_type=F32)
    part = holders * rows
    keep[...] = product[:part]
    send[...] = product[part:].astype(BF16)


def project(plan, lb, sources, weight):
    columns = weight.shape[1]
    part = plan.page // 2
    return pl.pallas_call(
        functools.partial(project_kernel, plan, lb),
        out_shape=(jax.ShapeDtypeStruct((part, columns), F32), jax.ShapeDtypeStruct((part, columns), BF16)),
        in_specs=[in_vmem()] * (plan.group + 1),
        out_specs=(in_vmem(), in_vmem()),
        scratch_shapes=[VMEM((plan.page, weight.shape[0]), BF16)],
        compiler_params=params(24),
    )(*(sources[k] for k in range(plan.group)), weight)


def swap(x, axis, distance):
    n = lax.axis_size(axis)
    return lax.ppermute(x, axis, [(i, i ^ distance) for i in range(n)])


def others(plan):
    return range(1, plan.group)


def spread(x, plan):
    return {0: x} | {k: swap(x, "pages", k) for k in others(plan)}


def by_halves(plan, heads, queries, weight, pages):
    far = swap(queries, "pages", plan.cross)
    near = []
    for lb, rows in enumerate((queries, far)):
        chunks = spread(rows, plan)
        outs = attend(plan, heads, lb, pages, [chunks[k] for k in range(plan.group)])
        order = reversed(others(plan)) if lb else others(plan)
        near.append(merge(heads, outs[0], *(swap(outs[k], "pages", k) for k in order)))
    across = [swap(x, "pages", plan.cross) for x in near]
    sums = [None, None]
    for lb in (1, 0):
        rows = finish(heads, near[lb], across[1 - lb])
        keep, send = project(plan, lb, spread(rows, plan), weight)
        sums[lb] = keep + swap(send, "mp", 1).astype(F32)
    stays = plan.block(lax.axis_index("pages"), 0) == lax.axis_index("mp") // 2
    mine = jnp.where(stays, sums[0], sums[1])
    away = jnp.where(stays, sums[1], sums[0]).astype(BF16)
    return (mine + swap(away, "mp", 2).astype(F32)).astype(BF16)


def by_gathers(plan, heads, queries, weight, pages):
    width = queries.shape[1]
    size = width // heads
    gathered = lax.all_gather(queries, "pages", axis=0, tiled=True)
    rows = gathered.shape[0]
    outs = [
        attend(plan, heads, lb, pages, [gathered[lb * plan.page : (lb + 1) * plan.page]])[0]
        for lb in range(plan.blocks)
    ]
    out = jnp.concatenate(outs, axis=0)
    packed = out[:, width : width + 3 * heads].astype(F32)
    lse = packed[:, :heads] + packed[:, heads : 2 * heads] + packed[:, 2 * heads :]
    every = lax.all_gather(lse, "pages")
    top = jnp.max(every, axis=0)
    share = jnp.exp2(lse - top) / jnp.sum(jnp.exp2(every - top), axis=0)
    part = (out[:, :width].reshape(rows, heads, size).astype(F32) * share[..., None]).reshape(1, rows, width)
    received = lax.all_to_all(part.astype(BF16), "pages", split_axis=1, concat_axis=0, tiled=True)
    mixed = jnp.sum(received, axis=0, dtype=F32).astype(BF16)
    terms = jnp.dot(lax.all_gather(mixed, "pages", axis=0, tiled=True), weight, preferred_element_type=F32)
    return lax.psum_scatter(terms, "mp", scatter_dimension=0, tiled=True).astype(BF16)


def per_device(queries, cached_keys, cached_values, out_weight, select, page_table, block_page):
    n, ways = lax.axis_size("pages"), lax.axis_size("mp")
    plan = Plan(n, ways, queries.shape[0], select.shape[0], cached_keys.shape[1])
    heads = queries.shape[1] // cached_keys.shape[3]
    pages = fetch(plan, select, page_table, block_page, cached_keys, cached_values)
    way = by_halves if plan.halves else by_gathers
    return way(plan, heads, queries, out_weight, pages)


def solution(mesh):
    placed = (
        P("pages", "mp"),
        P("pages", None, "mp", None),
        P("pages", None, "mp", None),
        P("mp", "pages"),
        P(),
        P(),
        P(),
    )
    return jax.shard_map(
        per_device, mesh=mesh, in_specs=placed, out_specs=P("mp", "pages"), check_vma=False
    )
```

```python
import functools
import math

import jax
import jax.numpy as jnp
from jax import lax
from jax.experimental import pallas as pl
from jax.experimental.pallas import tpu as pltpu
from jax.sharding import PartitionSpec as P

PICKED_PAGES = 6
FLOOR = -1e30
LANES = 128
HEADS_PER_TILE = 2

VMEM = pltpu.VMEM
SMEM = pltpu.SMEM
BF16 = jnp.bfloat16
F32 = jnp.float32


def in_vmem():
    return pl.BlockSpec(memory_space=VMEM)


def in_smem():
    return pl.BlockSpec(memory_space=SMEM)


def params(mib):
    return pltpu.CompilerParams(vmem_limit_bytes=mib * 2**20)


class Plan:
    def __init__(self, n, ways, rows, blocks, page):
        self.n, self.rows, self.blocks, self.page = n, rows, blocks, page
        self.group = n // blocks
        self.halves = blocks == 2 and n == 8 and ways == 4 and rows * self.group == page
        self.cross = n * 3 // 4
        self.chunks = self.group if self.halves else 1

    def block(self, me, lb):
        return (me // self.group) ^ lb if self.halves else lb

    def offsets(self, me, lb, shape):
        row = lax.broadcasted_iota(jnp.int32, shape, 0) % self.page
        if not self.halves:
            return row
        mine = (me ^ (lb * self.cross)) % self.group
        return ((row // self.rows) ^ mine) * self.rows + row % self.rows


def fetch_kernel(plan, pages_dev, select_hbm, table_hbm, stands_hbm, keys, values, k_out, v_out, info, select, table, stands, rows, k_buf, v_buf, sems, int_sems):
    me = lax.axis_index("pages")
    blocks, heads = k_out.shape[:2]
    span = k_buf.shape[1]
    page = span // heads
    picked = k_out.shape[2] // page
    low = me * pages_dev
    loads = [
        pltpu.make_async_copy(a, b, int_sems.at[i])
        for i, (a, b) in enumerate(((select_hbm, select), (table_hbm, table), (stands_hbm, stands)))
    ]
    whole = [
        pltpu.make_async_copy(a, b, sems.at[i]) for i, (a, b) in enumerate(((keys, k_buf), (values, v_buf)))
    ]
    for load in loads + whole:
        load.start()
    row = lax.broadcasted_iota(jnp.int32, (span, span), 0)
    column = lax.broadcasted_iota(jnp.int32, (span, span), 1)
    apart = (column == (row % page) * heads + row // page).astype(F32).astype(BF16)
    for load in loads:
        load.wait()
    for lb in range(blocks):
        block = plan.block(me, lb)
        stand = stands[block]
        info[lb, 1] = plan.n * pages_dev
        info[lb, 2] = stand
        others = jnp.int32(0)
        count = jnp.int32(0)
        for i in range(select.shape[1]):
            logical = select[block, i]
            local = table[logical] - low
            mine = (local >= 0) & (local < pages_dev)
            own = logical == stand
            slot = jnp.where(own, 0, jnp.maximum(picked - 1 - others, 0))
            slot = jnp.where(mine, slot, picked)
            rows[lb, slot] = local
            rows[blocks + lb, slot] = logical
            one = mine.astype(jnp.int32)
            others = others + jnp.where(own, 0, one)
            count = count + one
        info[lb, 0] = count
        info[lb, 1] = rows[blocks + lb, 0]

    for load in whole:
        load.wait()
    for lb in range(blocks):

        @pl.when(info[lb, 0] > 0)
        def _(lb=lb):
            for g in range(heads):
                v_out[lb, g, :, LANES:] = jnp.ones((picked * page, LANES), BF16)
            for slot in range(picked):
                local = jnp.clip(rows[lb, slot], 0, pages_dev - 1)
                both = jnp.concatenate([k_buf[local], v_buf[local]], axis=1)
                split = jnp.dot(apart, both, preferred_element_type=F32).astype(BF16)
                for g in range(heads):
                    here = slice(slot * page, (slot + 1) * page)
                    k_out[lb, g, here, :] = split[g * page : (g + 1) * page, :LANES]
                    v_out[lb, g, here, :LANES] = split[g * page : (g + 1) * page, LANES:]


def fetch(plan, select, table, stands, keys, values):
    pages_dev, page, heads, size = keys.shape
    blocks, picked = select.shape[0], PICKED_PAGES
    span = page * heads
    return pl.pallas_call(
        functools.partial(fetch_kernel, plan, pages_dev),
        out_shape=(
            jax.ShapeDtypeStruct((blocks, heads, picked * page, size), BF16),
            jax.ShapeDtypeStruct((blocks, heads, picked * page, size + LANES), BF16),
            jax.ShapeDtypeStruct((blocks, 3), jnp.int32),
        ),
        in_specs=[pl.BlockSpec(memory_space=pltpu.HBM)] * 5,
        out_specs=(in_vmem(), in_vmem(), in_smem()),
        scratch_shapes=[
            SMEM(select.shape, jnp.int32),
            SMEM(table.shape, jnp.int32),
            SMEM(stands.shape, jnp.int32),
            SMEM((2 * blocks, picked + 1), jnp.int32),
            VMEM((pages_dev, span, size), BF16),
            VMEM((pages_dev, span, size), BF16),
            pltpu.SemaphoreType.DMA((2,)),
            pltpu.SemaphoreType.DMA((3,)),
        ],
        compiler_params=params(16),
        cost_estimate=pl.CostEstimate(flops=2 * 10**9, bytes_accessed=8 * 2**20, transcendentals=0),
    )(*(pltpu.with_memory_space_constraint(x, pltpu.HBM) for x in (select, table, stands, keys.reshape(pages_dev, span, size), values.reshape(pages_dev, span, size))))


def pack_stats(lse, heads):
    lane = lax.broadcasted_iota(jnp.int32, lse.shape, 1)
    high = lse.astype(BF16).astype(F32)
    rest = lse - high
    middle = rest.astype(BF16).astype(F32)
    low = rest - middle
    packed = jnp.where(lane < heads, high, 0.0)
    packed = packed + jnp.where((lane >= heads) & (lane < 2 * heads), pltpu.roll(middle, heads, 1), 0.0)
    packed = packed + jnp.where((lane >= 2 * heads) & (lane < 3 * heads), pltpu.roll(low, 2 * heads, 1), 0.0)
    return packed.astype(BF16)


def unpack_stats(packed, heads):
    wide = packed.astype(F32)
    return wide + pltpu.roll(wide, LANES - heads, 1) + pltpu.roll(wide, LANES - 2 * heads, 1)


def attend_kernel(plan, heads, lb, info, *refs):
    me = lax.axis_index("pages")
    chunks, page = plan.chunks, plan.page
    queries, (k_ref, v_ref), outs = refs[:chunks][::-1], refs[chunks : chunks + 2], refs[chunks + 2 :]
    kv_heads, size = k_ref.shape[1], k_ref.shape[3]
    repeat = heads // kv_heads
    width = heads * size
    part = page // chunks
    tile = math.gcd(repeat, HEADS_PER_TILE)
    scale = size**-0.5 * math.log2(math.e)
    lane = lax.broadcasted_iota(jnp.int32, (page, LANES), 1)

    @pl.when(info[lb, 0] > 0)
    def _():
        shape = (tile * page, page)
        key_pos = info[lb, 1] * page + lax.broadcasted_iota(jnp.int32, shape, 1)
        query_pos = info[lb, 2] * page + plan.offsets(me, lb, shape)
        allowed = key_pos <= query_pos
        stats = jnp.zeros((page, LANES), F32)
        def product(first):
            q = jnp.concatenate(
                [m[:, h * size : (h + 1) * size] for h in range(first, first + tile) for m in queries], axis=0
            )
            return lax.dot_general(q, k_ref[lb, first // repeat], (((1,), (1,)), ((), ())), preferred_element_type=F32)

        ahead = product(0)
        for first in range(0, heads, tile):
            scores = scale * ahead
            if first + tile < heads:
                ahead = product(first + tile)
            scores = jnp.concatenate([jnp.where(allowed, scores[:, :page], FLOOR), scores[:, page:]], axis=1)
            peak = jnp.max(scores, axis=1, keepdims=True)
            weights = jnp.exp2(scores - peak).astype(BF16)
            both = jnp.dot(weights, v_ref[lb, first // repeat], preferred_element_type=F32)
            total = both[:, size:]
            out = (both[:, :size] / total).astype(BF16)
            lse = peak + jnp.log2(total)
            for i in range(tile):
                h = first + i
                stats = jnp.where(lane == h, lse[i * page : (i + 1) * page], stats)
                for c in range(chunks):
                    outs[c][:, h * size : (h + 1) * size] = out[i * page + c * part : i * page + (c + 1) * part]
        packed = pack_stats(stats, heads)
        for c in range(chunks):
            outs[c][:, width:] = packed[c * part : (c + 1) * part]

    @pl.when(info[lb, 0] == 0)
    def _():
        for c in range(chunks):
            outs[c][:, :width] = jnp.zeros((part, width), BF16)
            outs[c][:, width:] = pack_stats(jnp.full((part, LANES), FLOOR, F32), heads)


def attend(plan, heads, lb, pages, queries):
    keys, values, info = pages
    part = plan.page // plan.chunks
    shape = jax.ShapeDtypeStruct((part, queries[0].shape[1] + LANES), BF16)
    return pl.pallas_call(
        functools.partial(attend_kernel, plan, heads, lb),
        out_shape=(shape,) * plan.chunks,
        in_specs=[in_smem()] + [in_vmem()] * (len(queries) + 2),
        out_specs=(in_vmem(),) * plan.chunks,
        compiler_params=params(32),
        cost_estimate=pl.CostEstimate(flops=2 * 10**9, bytes_accessed=4 * 2**20, transcendentals=10**6),
    )(info, *queries[::-1], keys, values)


def merged(parts, stats):
    top = functools.reduce(jnp.maximum, stats)
    shares = [jnp.exp2(s - top) for s in stats]
    total = functools.reduce(jnp.add, shares)
    shares = [s / total for s in shares]

    def head(h):
        return functools.reduce(
            jnp.add, [p(h).astype(F32) * s[:, h : h + 1] for p, s in zip(parts, shares, strict=True)]
        )

    return head, top + jnp.log2(total)


def merge_kernel(heads, *refs):
    sources, out = refs[:-1], refs[-1]
    width = out.shape[1] - LANES
    size = width // heads
    head, lse = merged([heads_of(r, size) for r in sources], [unpack_stats(r[:, width:], heads) for r in sources])
    for h in range(heads):
        out[:, h * size : (h + 1) * size] = head(h).astype(BF16)
    out[:, width:] = pack_stats(lse, heads)


def merge(heads, *sources):
    return pl.pallas_call(
        functools.partial(merge_kernel, heads),
        out_shape=jax.ShapeDtypeStruct(sources[0].shape, BF16),
        in_specs=[in_vmem()] * len(sources),
        out_specs=in_vmem(),
        compiler_params=params(8),
    )(*sources)


def heads_of(ref, size):
    return lambda h: ref[:, h * size : (h + 1) * size]


def finish_kernel(heads, near, far, out):
    width = out.shape[1]
    size = width // heads
    head, _ = merged([heads_of(r, size) for r in (near, far)], [unpack_stats(r[:, width:], heads) for r in (near, far)])
    for h in range(heads):
        out[:, h * size : (h + 1) * size] = head(h).astype(BF16)


def finish(heads, near, far):
    return pl.pallas_call(
        functools.partial(finish_kernel, heads),
        out_shape=jax.ShapeDtypeStruct((near.shape[0], near.shape[1] - LANES), BF16),
        in_specs=[in_vmem()] * 2,
        out_specs=in_vmem(),
        compiler_params=params(8),
    )(near, far)


def sources_of(plan, lb):
    return range(plan.group) if lb else [0, *middle_first(plan)]


def project_kernel(plan, lb, *refs):
    sources, weight, (keep, send, rows_ref) = refs[: plan.group], refs[plan.group], refs[plan.group + 1 :]
    me, column = lax.axis_index("pages"), lax.axis_index("mp")
    rows = plan.rows
    holders = plan.group // 2
    for i, k in enumerate(sources_of(plan, lb)):
        device = me ^ k ^ (lb * plan.cross)
        place = ((device // holders % 2) ^ (column % 2)) * holders + device % holders
        rows_ref[pl.ds(pl.multiple_of(place * rows, rows), rows), :] = sources[i][...]
    product = jnp.dot(rows_ref[...], weight[...], preferred_element_type=F32)
    part = holders * rows
    keep[...] = product[:part]
    send[...] = product[part:].astype(BF16)


def project(plan, lb, sources, weight):
    columns = weight.shape[1]
    part = plan.page // 2
    return pl.pallas_call(
        functools.partial(project_kernel, plan, lb),
        out_shape=(jax.ShapeDtypeStruct((part, columns), F32), jax.ShapeDtypeStruct((part, columns), BF16)),
        in_specs=[in_vmem()] * (plan.group + 1),
        out_specs=(in_vmem(), in_vmem()),
        scratch_shapes=[VMEM((plan.page, weight.shape[0]), BF16)],
        compiler_params=params(24),
    )(*(sources[k] for k in sources_of(plan, lb)), weight)


def swap(x, axis, distance):
    n = lax.axis_size(axis)
    return lax.ppermute(x, axis, [(i, i ^ distance) for i in range(n)])


def others(plan):
    return range(1, plan.group)


def middle_first(plan):
    return [*range(plan.group // 2, plan.group), *range(1, plan.group // 2)]


def spread(x, plan):
    return {0: x} | {k: swap(x, "pages", k) for k in others(plan)}


def by_halves(plan, heads, queries, weight, pages):
    far = swap(queries, "pages", plan.cross)
    near = []
    for lb, rows in enumerate((queries, far)):
        chunks = spread(rows, plan)
        outs = attend(plan, heads, lb, pages, [chunks[k] for k in range(plan.group)])
        near.append(merge(heads, outs[0], *(swap(outs[k], "pages", k) for k in middle_first(plan))))
    across = [swap(x, "pages", plan.cross) for x in near]
    sums = [None, None]
    for lb in (1, 0):
        rows = finish(heads, near[lb], across[1 - lb])
        keep, send = project(plan, lb, spread(rows, plan), weight)
        sums[lb] = keep + swap(send, "mp", 1).astype(F32)
    stays = plan.block(lax.axis_index("pages"), 0) == lax.axis_index("mp") // 2
    mine = jnp.where(stays, sums[0], sums[1])
    away = jnp.where(stays, sums[1], sums[0]).astype(BF16)
    return (mine + swap(away, "mp", 2).astype(F32)).astype(BF16)


def by_gathers(plan, heads, queries, weight, pages):
    width = queries.shape[1]
    size = width // heads
    gathered = lax.all_gather(queries, "pages", axis=0, tiled=True)
    rows = gathered.shape[0]
    outs = [
        attend(plan, heads, lb, pages, [gathered[lb * plan.page : (lb + 1) * plan.page]])[0]
        for lb in range(plan.blocks)
    ]
    out = jnp.concatenate(outs, axis=0)
    packed = out[:, width : width + 3 * heads].astype(F32)
    lse = packed[:, :heads] + packed[:, heads : 2 * heads] + packed[:, 2 * heads :]
    every = lax.all_gather(lse, "pages")
    top = jnp.max(every, axis=0)
    share = jnp.exp2(lse - top) / jnp.sum(jnp.exp2(every - top), axis=0)
    part = (out[:, :width].reshape(rows, heads, size).astype(F32) * share[..., None]).reshape(1, rows, width)
    received = lax.all_to_all(part.astype(BF16), "pages", split_axis=1, concat_axis=0, tiled=True)
    mixed = jnp.sum(received, axis=0, dtype=F32).astype(BF16)
    terms = jnp.dot(lax.all_gather(mixed, "pages", axis=0, tiled=True), weight, preferred_element_type=F32)
    return lax.psum_scatter(terms, "mp", scatter_dimension=0, tiled=True).astype(BF16)


def per_device(queries, cached_keys, cached_values, out_weight, select, page_table, block_page):
    n, ways = lax.axis_size("pages"), lax.axis_size("mp")
    plan = Plan(n, ways, queries.shape[0], select.shape[0], cached_keys.shape[1])
    heads = queries.shape[1] // cached_keys.shape[3]
    pages = fetch(plan, select, page_table, block_page, cached_keys, cached_values)
    way = by_halves if plan.halves else by_gathers
    return way(plan, heads, queries, out_weight, pages)


def solution(mesh):
    placed = (
        P("pages", "mp"),
        P("pages", None, "mp", None),
        P("pages", None, "mp", None),
        P("mp", "pages"),
        P(),
        P(),
        P(),
    )
    return jax.shard_map(
        per_device, mesh=mesh, in_specs=placed, out_specs=P("mp", "pages"), check_vma=False
    )
```

```python
import functools
import math

import jax
import jax.numpy as jnp
from jax import lax
from jax.experimental import pallas as pl
from jax.experimental.pallas import tpu as pltpu
from jax.sharding import PartitionSpec as P

PICKED_PAGES = 6
FLOOR = -1e30
LANES = 128
HEADS_PER_TILE = 2

VMEM = pltpu.VMEM
SMEM = pltpu.SMEM
BF16 = jnp.bfloat16
F32 = jnp.float32


def in_vmem():
    return pl.BlockSpec(memory_space=VMEM)


def in_smem():
    return pl.BlockSpec(memory_space=SMEM)


def params(mib):
    return pltpu.CompilerParams(vmem_limit_bytes=mib * 2**20)


class Plan:
    def __init__(self, n, ways, rows, blocks, page):
        self.n, self.rows, self.blocks, self.page = n, rows, blocks, page
        self.group = n // blocks
        self.halves = blocks == 2 and n == 8 and ways == 4 and rows * self.group == page
        self.cross = n * 3 // 4
        self.chunks = self.group if self.halves else 1

    def block(self, me, lb):
        return (me // self.group) ^ lb if self.halves else lb

    def offsets(self, me, lb, shape):
        row = lax.broadcasted_iota(jnp.int32, shape, 0) % self.page
        if not self.halves:
            return row
        mine = (me ^ (lb * self.cross)) % self.group
        return ((row // self.rows) ^ mine) * self.rows + row % self.rows


def fetch_kernel(plan, pages_dev, select_hbm, table_hbm, stands_hbm, keys, values, k_out, v_out, info, select, table, stands, rows, k_buf, v_buf, sems, int_sems):
    me = lax.axis_index("pages")
    blocks, heads = k_out.shape[:2]
    span = k_buf.shape[1]
    page = span // heads
    picked = k_out.shape[2] // page
    low = me * pages_dev
    loads = [
        pltpu.make_async_copy(a, b, int_sems.at[i])
        for i, (a, b) in enumerate(((select_hbm, select), (table_hbm, table), (stands_hbm, stands)))
    ]
    whole = [
        pltpu.make_async_copy(a, b, sems.at[i]) for i, (a, b) in enumerate(((keys, k_buf), (values, v_buf)))
    ]
    for load in loads + whole:
        load.start()
    row = lax.broadcasted_iota(jnp.int32, (span, span), 0)
    column = lax.broadcasted_iota(jnp.int32, (span, span), 1)
    apart = (column == (row % page) * heads + row // page).astype(F32).astype(BF16)
    for load in loads:
        load.wait()
    for lb in range(blocks):
        block = plan.block(me, lb)
        stand = stands[block]
        info[lb, 1] = plan.n * pages_dev
        info[lb, 2] = stand
        others = jnp.int32(0)
        count = jnp.int32(0)
        for i in range(select.shape[1]):
            logical = select[block, i]
            local = table[logical] - low
            mine = (local >= 0) & (local < pages_dev)
            own = logical == stand
            slot = jnp.where(own, 0, jnp.maximum(picked - 1 - others, 0))
            slot = jnp.where(mine, slot, picked)
            rows[lb, slot] = local
            rows[blocks + lb, slot] = logical
            one = mine.astype(jnp.int32)
            others = others + jnp.where(own, 0, one)
            count = count + one
        info[lb, 0] = count
        info[lb, 1] = rows[blocks + lb, 0]

    for load in whole:
        load.wait()
    for lb in range(blocks):

        @pl.when(info[lb, 0] > 0)
        def _(lb=lb):
            for g in range(heads):
                v_out[lb, g, :, LANES:] = jnp.ones((picked * page, LANES), BF16)
            for slot in range(picked):
                local = jnp.clip(rows[lb, slot], 0, pages_dev - 1)
                both = jnp.concatenate([k_buf[local], v_buf[local]], axis=1)
                split = jnp.dot(apart, both, preferred_element_type=F32).astype(BF16)
                for g in range(heads):
                    here = slice(slot * page, (slot + 1) * page)
                    k_out[lb, g, here, :] = split[g * page : (g + 1) * page, :LANES]
                    v_out[lb, g, here, :LANES] = split[g * page : (g + 1) * page, LANES:]


def fetch(plan, select, table, stands, keys, values):
    pages_dev, page, heads, size = keys.shape
    blocks, picked = select.shape[0], PICKED_PAGES
    span = page * heads
    return pl.pallas_call(
        functools.partial(fetch_kernel, plan, pages_dev),
        out_shape=(
            jax.ShapeDtypeStruct((blocks, heads, picked * page, size), BF16),
            jax.ShapeDtypeStruct((blocks, heads, picked * page, size + LANES), BF16),
            jax.ShapeDtypeStruct((blocks, 3), jnp.int32),
        ),
        in_specs=[pl.BlockSpec(memory_space=pltpu.HBM)] * 5,
        out_specs=(in_vmem(), in_vmem(), in_smem()),
        scratch_shapes=[
            SMEM(select.shape, jnp.int32),
            SMEM(table.shape, jnp.int32),
            SMEM(stands.shape, jnp.int32),
            SMEM((2 * blocks, picked + 1), jnp.int32),
            VMEM((pages_dev, span, size), BF16),
            VMEM((pages_dev, span, size), BF16),
            pltpu.SemaphoreType.DMA((2,)),
            pltpu.SemaphoreType.DMA((3,)),
        ],
        compiler_params=params(16),
        cost_estimate=pl.CostEstimate(flops=2 * 10**9, bytes_accessed=8 * 2**20, transcendentals=0),
    )(*(pltpu.with_memory_space_constraint(x, pltpu.HBM) for x in (select, table, stands, keys.reshape(pages_dev, span, size), values.reshape(pages_dev, span, size))))


def pack_stats(lse, heads):
    lane = lax.broadcasted_iota(jnp.int32, lse.shape, 1)
    high = lse.astype(BF16).astype(F32)
    rest = lse - high
    middle = rest.astype(BF16).astype(F32)
    low = rest - middle
    packed = jnp.where(lane < heads, high, 0.0)
    packed = packed + jnp.where((lane >= heads) & (lane < 2 * heads), pltpu.roll(middle, heads, 1), 0.0)
    packed = packed + jnp.where((lane >= 2 * heads) & (lane < 3 * heads), pltpu.roll(low, 2 * heads, 1), 0.0)
    return packed.astype(BF16)


def unpack_stats(packed, heads):
    wide = packed.astype(F32)
    return wide + pltpu.roll(wide, LANES - heads, 1) + pltpu.roll(wide, LANES - 2 * heads, 1)


def attend_kernel(plan, heads, lb, info, *refs):
    me = lax.axis_index("pages")
    chunks, page = plan.chunks, plan.page
    queries, (k_ref, v_ref), outs = refs[:chunks][::-1], refs[chunks : chunks + 2], refs[chunks + 2 :]
    kv_heads, size = k_ref.shape[1], k_ref.shape[3]
    repeat = heads // kv_heads
    width = heads * size
    part = page // chunks
    tile = math.gcd(repeat, HEADS_PER_TILE)
    scale = size**-0.5 * math.log2(math.e)
    lane = lax.broadcasted_iota(jnp.int32, (page, LANES), 1)

    @pl.when(info[lb, 0] > 0)
    def _():
        shape = (tile * page, page)
        key_pos = info[lb, 1] * page + lax.broadcasted_iota(jnp.int32, shape, 1)
        query_pos = info[lb, 2] * page + plan.offsets(me, lb, shape)
        allowed = key_pos <= query_pos
        stats = jnp.zeros((page, LANES), F32)
        def product(first):
            q = jnp.concatenate(
                [m[:, h * size : (h + 1) * size] for h in range(first, first + tile) for m in queries], axis=0
            )
            return lax.dot_general(q, k_ref[lb, first // repeat], (((1,), (1,)), ((), ())), preferred_element_type=F32)

        ahead = product(0)
        for first in range(0, heads, tile):
            scores = scale * ahead
            if first + tile < heads:
                ahead = product(first + tile)
            scores = jnp.concatenate([jnp.where(allowed, scores[:, :page], FLOOR), scores[:, page:]], axis=1)
            peak = jnp.max(scores, axis=1, keepdims=True)
            weights = jnp.exp2(scores - peak).astype(BF16)
            both = jnp.dot(weights, v_ref[lb, first // repeat], preferred_element_type=F32)
            total = both[:, size:]
            out = (both[:, :size] / total).astype(BF16)
            lse = peak + jnp.log2(total)
            for i in range(tile):
                h = first + i
                stats = jnp.where(lane == h, lse[i * page : (i + 1) * page], stats)
                for c in range(chunks):
                    outs[c][:, h * size : (h + 1) * size] = out[i * page + c * part : i * page + (c + 1) * part]
        packed = pack_stats(stats, heads)
        for c in range(chunks):
            outs[c][:, width:] = packed[c * part : (c + 1) * part]

    @pl.when(info[lb, 0] == 0)
    def _():
        for c in range(chunks):
            outs[c][:, :width] = jnp.zeros((part, width), BF16)
            outs[c][:, width:] = pack_stats(jnp.full((part, LANES), FLOOR, F32), heads)


def attend(plan, heads, lb, pages, queries):
    keys, values, info = pages
    part = plan.page // plan.chunks
    shape = jax.ShapeDtypeStruct((part, queries[0].shape[1] + LANES), BF16)
    return pl.pallas_call(
        functools.partial(attend_kernel, plan, heads, lb),
        out_shape=(shape,) * plan.chunks,
        in_specs=[in_smem()] + [in_vmem()] * (len(queries) + 2),
        out_specs=(in_vmem(),) * plan.chunks,
        compiler_params=params(32),
        cost_estimate=pl.CostEstimate(flops=2 * 10**9, bytes_accessed=4 * 2**20, transcendentals=10**6),
    )(info, *queries[::-1], keys, values)


def merged(parts, stats):
    top = functools.reduce(jnp.maximum, stats)
    shares = [jnp.exp2(s - top) for s in stats]
    total = functools.reduce(jnp.add, shares)
    shares = [s / total for s in shares]

    def head(h):
        return functools.reduce(
            jnp.add, [p(h).astype(F32) * s[:, h : h + 1] for p, s in zip(parts, shares, strict=True)]
        )

    return head, top + jnp.log2(total)


def merge_kernel(heads, *refs):
    sources, out = refs[:-1], refs[-1]
    width = out.shape[1] - LANES
    size = width // heads
    head, lse = merged([heads_of(r, size) for r in sources], [unpack_stats(r[:, width:], heads) for r in sources])
    for h in range(heads):
        out[:, h * size : (h + 1) * size] = head(h).astype(BF16)
    out[:, width:] = pack_stats(lse, heads)


def merge(heads, *sources):
    return pl.pallas_call(
        functools.partial(merge_kernel, heads),
        out_shape=jax.ShapeDtypeStruct(sources[0].shape, BF16),
        in_specs=[in_vmem()] * len(sources),
        out_specs=in_vmem(),
        compiler_params=params(8),
    )(*sources)


def heads_of(ref, size):
    return lambda h: ref[:, h * size : (h + 1) * size]


def finish_kernel(heads, near, far, out):
    width = out.shape[1]
    size = width // heads
    head, _ = merged([heads_of(r, size) for r in (near, far)], [unpack_stats(r[:, width:], heads) for r in (near, far)])
    for h in range(heads):
        out[:, h * size : (h + 1) * size] = head(h).astype(BF16)


def finish(heads, near, far):
    return pl.pallas_call(
        functools.partial(finish_kernel, heads),
        out_shape=jax.ShapeDtypeStruct((near.shape[0], near.shape[1] - LANES), BF16),
        in_specs=[in_vmem()] * 2,
        out_specs=in_vmem(),
        compiler_params=params(8),
    )(near, far)


def sources_of(plan, lb):
    return range(plan.group) if lb else [0, *middle_first(plan)]


def project_kernel(plan, lb, *refs):
    sources, weight, (keep, send, rows_ref) = refs[: plan.group], refs[plan.group], refs[plan.group + 1 :]
    me, column = lax.axis_index("pages"), lax.axis_index("mp")
    rows = plan.rows
    holders = plan.group // 2
    for i, k in enumerate(sources_of(plan, lb)):
        device = me ^ k ^ (lb * plan.cross)
        place = ((device // holders % 2) ^ (column % 2)) * holders + device % holders
        rows_ref[pl.ds(pl.multiple_of(place * rows, rows), rows), :] = sources[i][...]
    product = jnp.dot(rows_ref[...], weight[...], preferred_element_type=F32)
    part = holders * rows
    keep[...] = product[:part]
    send[...] = product[part:].astype(BF16)


def project(plan, lb, sources, weight):
    columns = weight.shape[1]
    part = plan.page // 2
    return pl.pallas_call(
        functools.partial(project_kernel, plan, lb),
        out_shape=(jax.ShapeDtypeStruct((part, columns), F32), jax.ShapeDtypeStruct((part, columns), BF16)),
        in_specs=[in_vmem()] * (plan.group + 1),
        out_specs=(in_vmem(), in_vmem()),
        scratch_shapes=[VMEM((plan.page, weight.shape[0]), BF16)],
        compiler_params=params(24),
    )(*(sources[k] for k in sources_of(plan, lb)), weight)


def swap(x, axis, distance):
    n = lax.axis_size(axis)
    return lax.ppermute(x, axis, [(i, i ^ distance) for i in range(n)])


def others(plan):
    return range(1, plan.group)


def middle_first(plan):
    return [*range(plan.group // 2, plan.group), *range(1, plan.group // 2)]


def spread(x, plan):
    return {0: x} | {k: swap(x, "pages", k) for k in others(plan)}


def by_halves(plan, heads, queries, weight, pages):
    far = swap(queries, "pages", plan.cross)
    near = []
    for lb, rows in enumerate((queries, far)):
        chunks = spread(rows, plan)
        outs = attend(plan, heads, lb, pages, [chunks[k] for k in range(plan.group)])
        order = reversed(others(plan)) if lb else others(plan)
        near.append(merge(heads, outs[0], *(swap(outs[k], "pages", k) for k in order)))
    across = [swap(x, "pages", plan.cross) for x in near]
    sums = [None, None]
    for lb in (1, 0):
        rows = finish(heads, near[lb], across[1 - lb])
        keep, send = project(plan, lb, spread(rows, plan), weight)
        sums[lb] = keep + swap(send, "mp", 1).astype(F32)
    stays = plan.block(lax.axis_index("pages"), 0) == lax.axis_index("mp") // 2
    mine = jnp.where(stays, sums[0], sums[1])
    away = jnp.where(stays, sums[1], sums[0]).astype(BF16)
    return (mine + swap(away, "mp", 2).astype(F32)).astype(BF16)


def by_gathers(plan, heads, queries, weight, pages):
    width = queries.shape[1]
    size = width // heads
    gathered = lax.all_gather(queries, "pages", axis=0, tiled=True)
    rows = gathered.shape[0]
    outs = [
        attend(plan, heads, lb, pages, [gathered[lb * plan.page : (lb + 1) * plan.page]])[0]
        for lb in range(plan.blocks)
    ]
    out = jnp.concatenate(outs, axis=0)
    packed = out[:, width : width + 3 * heads].astype(F32)
    lse = packed[:, :heads] + packed[:, heads : 2 * heads] + packed[:, 2 * heads :]
    every = lax.all_gather(lse, "pages")
    top = jnp.max(every, axis=0)
    share = jnp.exp2(lse - top) / jnp.sum(jnp.exp2(every - top), axis=0)
    part = (out[:, :width].reshape(rows, heads, size).astype(F32) * share[..., None]).reshape(1, rows, width)
    received = lax.all_to_all(part.astype(BF16), "pages", split_axis=1, concat_axis=0, tiled=True)
    mixed = jnp.sum(received, axis=0, dtype=F32).astype(BF16)
    terms = jnp.dot(lax.all_gather(mixed, "pages", axis=0, tiled=True), weight, preferred_element_type=F32)
    return lax.psum_scatter(terms, "mp", scatter_dimension=0, tiled=True).astype(BF16)


def per_device(queries, cached_keys, cached_values, out_weight, select, page_table, block_page):
    n, ways = lax.axis_size("pages"), lax.axis_size("mp")
    plan = Plan(n, ways, queries.shape[0], select.shape[0], cached_keys.shape[1])
    heads = queries.shape[1] // cached_keys.shape[3]
    pages = fetch(plan, select, page_table, block_page, cached_keys, cached_values)
    way = by_halves if plan.halves else by_gathers
    return way(plan, heads, queries, out_weight, pages)


def solution(mesh):
    placed = (
        P("pages", "mp"),
        P("pages", None, "mp", None),
        P("pages", None, "mp", None),
        P("mp", "pages"),
        P(),
        P(),
        P(),
    )
    return jax.shard_map(
        per_device, mesh=mesh, in_specs=placed, out_specs=P("mp", "pages"), check_vma=False
    )
```

```python
import functools
import math

import jax
import jax.numpy as jnp
from jax import lax
from jax.experimental import pallas as pl
from jax.experimental.pallas import tpu as pltpu
from jax.sharding import PartitionSpec as P

PICKED_PAGES = 6
FLOOR = -1e30
LANES = 128
HEADS_PER_TILE = 2

VMEM = pltpu.VMEM
SMEM = pltpu.SMEM
BF16 = jnp.bfloat16
F32 = jnp.float32


def in_vmem():
    return pl.BlockSpec(memory_space=VMEM)


def in_smem():
    return pl.BlockSpec(memory_space=SMEM)


def params(mib):
    return pltpu.CompilerParams(vmem_limit_bytes=mib * 2**20)


class Plan:
    def __init__(self, n, ways, rows, blocks, page):
        self.n, self.rows, self.blocks, self.page = n, rows, blocks, page
        self.group = n // blocks
        self.halves = blocks == 2 and n == 8 and ways == 4 and rows * self.group == page
        self.cross = n * 3 // 4
        self.chunks = self.group if self.halves else 1

    def block(self, me, lb):
        return (me // self.group) ^ lb if self.halves else lb

    def offsets(self, me, lb, shape):
        row = lax.broadcasted_iota(jnp.int32, shape, 0) % self.page
        if not self.halves:
            return row
        mine = (me ^ (lb * self.cross)) % self.group
        return ((row // self.rows) ^ mine) * self.rows + row % self.rows


def fetch_kernel(plan, pages_dev, select_hbm, table_hbm, stands_hbm, keys, values, k_out, v_out, info, select, table, stands, rows, k_buf, v_buf, sems, int_sems):
    me = lax.axis_index("pages")
    blocks, heads = k_out.shape[:2]
    span = k_buf.shape[1]
    page = span // heads
    picked = k_out.shape[2] // page
    low = me * pages_dev
    loads = [
        pltpu.make_async_copy(a, b, int_sems.at[i])
        for i, (a, b) in enumerate(((select_hbm, select), (table_hbm, table), (stands_hbm, stands)))
    ]
    whole = [
        pltpu.make_async_copy(a, b, sems.at[i]) for i, (a, b) in enumerate(((keys, k_buf), (values, v_buf)))
    ]
    for load in loads + whole:
        load.start()
    row = lax.broadcasted_iota(jnp.int32, (span, span), 0)
    column = lax.broadcasted_iota(jnp.int32, (span, span), 1)
    apart = (column == (row % page) * heads + row // page).astype(F32).astype(BF16)
    for load in loads:
        load.wait()
    for lb in range(blocks):
        block = plan.block(me, lb)
        stand = stands[block]
        info[lb, 1] = plan.n * pages_dev
        info[lb, 2] = stand
        others = jnp.int32(0)
        count = jnp.int32(0)
        for i in range(select.shape[1]):
            logical = select[block, i]
            local = table[logical] - low
            mine = (local >= 0) & (local < pages_dev)
            own = logical == stand
            slot = jnp.where(own, 0, jnp.maximum(picked - 1 - others, 0))
            slot = jnp.where(mine, slot, picked)
            rows[lb, slot] = local
            rows[blocks + lb, slot] = logical
            one = mine.astype(jnp.int32)
            others = others + jnp.where(own, 0, one)
            count = count + one
        info[lb, 0] = count
        info[lb, 1] = rows[blocks + lb, 0]

    for load in whole:
        load.wait()
    for lb in range(blocks):

        @pl.when(info[lb, 0] > 0)
        def _(lb=lb):
            for g in range(heads):
                v_out[lb, g, :, LANES:] = jnp.ones((picked * page, LANES), BF16)
            for slot in range(picked):
                local = jnp.clip(rows[lb, slot], 0, pages_dev - 1)
                both = jnp.concatenate([k_buf[local], v_buf[local]], axis=1)
                split = jnp.dot(apart, both, preferred_element_type=F32).astype(BF16)
                for g in range(heads):
                    here = slice(slot * page, (slot + 1) * page)
                    k_out[lb, g, here, :] = split[g * page : (g + 1) * page, :LANES]
                    v_out[lb, g, here, :LANES] = split[g * page : (g + 1) * page, LANES:]


def fetch(plan, select, table, stands, keys, values):
    pages_dev, page, heads, size = keys.shape
    blocks, picked = select.shape[0], PICKED_PAGES
    span = page * heads
    return pl.pallas_call(
        functools.partial(fetch_kernel, plan, pages_dev),
        out_shape=(
            jax.ShapeDtypeStruct((blocks, heads, picked * page, size), BF16),
            jax.ShapeDtypeStruct((blocks, heads, picked * page, size + LANES), BF16),
            jax.ShapeDtypeStruct((blocks, 3), jnp.int32),
        ),
        in_specs=[pl.BlockSpec(memory_space=pltpu.HBM)] * 5,
        out_specs=(in_vmem(), in_vmem(), in_smem()),
        scratch_shapes=[
            SMEM(select.shape, jnp.int32),
            SMEM(table.shape, jnp.int32),
            SMEM(stands.shape, jnp.int32),
            SMEM((2 * blocks, picked + 1), jnp.int32),
            VMEM((pages_dev, span, size), BF16),
            VMEM((pages_dev, span, size), BF16),
            pltpu.SemaphoreType.DMA((2,)),
            pltpu.SemaphoreType.DMA((3,)),
        ],
        compiler_params=params(16),
        cost_estimate=pl.CostEstimate(flops=2 * 10**9, bytes_accessed=8 * 2**20, transcendentals=0),
    )(*(pltpu.with_memory_space_constraint(x, pltpu.HBM) for x in (select, table, stands, keys.reshape(pages_dev, span, size), values.reshape(pages_dev, span, size))))


def pack_stats(lse, heads):
    lane = lax.broadcasted_iota(jnp.int32, lse.shape, 1)
    high = lse.astype(BF16).astype(F32)
    rest = lse - high
    middle = rest.astype(BF16).astype(F32)
    low = rest - middle
    packed = jnp.where(lane < heads, high, 0.0)
    packed = packed + jnp.where((lane >= heads) & (lane < 2 * heads), pltpu.roll(middle, heads, 1), 0.0)
    packed = packed + jnp.where((lane >= 2 * heads) & (lane < 3 * heads), pltpu.roll(low, 2 * heads, 1), 0.0)
    return packed.astype(BF16)


def unpack_stats(packed, heads):
    wide = packed.astype(F32)
    return wide + pltpu.roll(wide, LANES - heads, 1) + pltpu.roll(wide, LANES - 2 * heads, 1)


def attend_kernel(plan, heads, lb, info, *refs):
    me = lax.axis_index("pages")
    chunks, page = plan.chunks, plan.page
    queries, (k_ref, v_ref), outs = refs[:chunks][::-1], refs[chunks : chunks + 2], refs[chunks + 2 :]
    kv_heads, size = k_ref.shape[1], k_ref.shape[3]
    repeat = heads // kv_heads
    width = heads * size
    part = page // chunks
    tile = math.gcd(repeat, HEADS_PER_TILE)
    scale = size**-0.5 * math.log2(math.e)
    lane = lax.broadcasted_iota(jnp.int32, (page, LANES), 1)

    @pl.when(info[lb, 0] > 0)
    def _():
        shape = (tile * page, page)
        key_pos = info[lb, 1] * page + lax.broadcasted_iota(jnp.int32, shape, 1)
        query_pos = info[lb, 2] * page + plan.offsets(me, lb, shape)
        allowed = key_pos <= query_pos
        stats = jnp.zeros((page, LANES), F32)
        def product(first):
            q = jnp.concatenate(
                [m[:, h * size : (h + 1) * size] for h in range(first, first + tile) for m in queries], axis=0
            )
            return lax.dot_general(q, k_ref[lb, first // repeat], (((1,), (1,)), ((), ())), preferred_element_type=F32)

        ahead = product(0)
        for first in range(0, heads, tile):
            scores = scale * ahead
            if first + tile < heads:
                ahead = product(first + tile)
            scores = jnp.concatenate([jnp.where(allowed, scores[:, :page], FLOOR), scores[:, page:]], axis=1)
            peak = jnp.max(scores, axis=1, keepdims=True)
            weights = jnp.exp2(scores - peak).astype(BF16)
            both = jnp.dot(weights, v_ref[lb, first // repeat], preferred_element_type=F32)
            total = both[:, size:]
            out = (both[:, :size] / total).astype(BF16)
            lse = peak + jnp.log2(total)
            for i in range(tile):
                h = first + i
                stats = jnp.where(lane == h, lse[i * page : (i + 1) * page], stats)
                for c in range(chunks):
                    outs[c][:, h * size : (h + 1) * size] = out[i * page + c * part : i * page + (c + 1) * part]
        packed = pack_stats(stats, heads)
        for c in range(chunks):
            outs[c][:, width:] = packed[c * part : (c + 1) * part]

    @pl.when(info[lb, 0] == 0)
    def _():
        for c in range(chunks):
            outs[c][:, :width] = jnp.zeros((part, width), BF16)
            outs[c][:, width:] = pack_stats(jnp.full((part, LANES), FLOOR, F32), heads)


def attend(plan, heads, lb, pages, queries):
    keys, values, info = pages
    part = plan.page // plan.chunks
    shape = jax.ShapeDtypeStruct((part, queries[0].shape[1] + LANES), BF16)
    return pl.pallas_call(
        functools.partial(attend_kernel, plan, heads, lb),
        out_shape=(shape,) * plan.chunks,
        in_specs=[in_smem()] + [in_vmem()] * (len(queries) + 2),
        out_specs=(in_vmem(),) * plan.chunks,
        compiler_params=params(32),
        cost_estimate=pl.CostEstimate(flops=2 * 10**9, bytes_accessed=4 * 2**20, transcendentals=10**6),
    )(info, *queries[::-1], keys, values)


def merged(parts, stats):
    top = functools.reduce(jnp.maximum, stats)
    shares = [jnp.exp2(s - top) for s in stats]
    total = functools.reduce(jnp.add, shares)
    shares = [s / total for s in shares]

    def head(h):
        return functools.reduce(
            jnp.add, [p(h).astype(F32) * s[:, h : h + 1] for p, s in zip(parts, shares, strict=True)]
        )

    return head, top + jnp.log2(total)


def merge_kernel(heads, *refs):
    sources, out = refs[:-1], refs[-1]
    width = out.shape[1] - LANES
    size = width // heads
    head, lse = merged([heads_of(r, size) for r in sources], [unpack_stats(r[:, width:], heads) for r in sources])
    for h in range(heads):
        out[:, h * size : (h + 1) * size] = head(h).astype(BF16)
    out[:, width:] = pack_stats(lse, heads)


def merge(heads, *sources):
    return pl.pallas_call(
        functools.partial(merge_kernel, heads),
        out_shape=jax.ShapeDtypeStruct(sources[0].shape, BF16),
        in_specs=[in_vmem()] * len(sources),
        out_specs=in_vmem(),
        compiler_params=params(8),
    )(*sources)


def heads_of(ref, size):
    return lambda h: ref[:, h * size : (h + 1) * size]


def finish_kernel(heads, near, far, out):
    width = out.shape[1]
    size = width // heads
    head, _ = merged([heads_of(r, size) for r in (near, far)], [unpack_stats(r[:, width:], heads) for r in (near, far)])
    for h in range(heads):
        out[:, h * size : (h + 1) * size] = head(h).astype(BF16)


def finish(heads, near, far):
    return pl.pallas_call(
        functools.partial(finish_kernel, heads),
        out_shape=jax.ShapeDtypeStruct((near.shape[0], near.shape[1] - LANES), BF16),
        in_specs=[in_vmem()] * 2,
        out_specs=in_vmem(),
        compiler_params=params(8),
    )(near, far)


def sources_of(plan, lb):
    return range(plan.group) if lb else [0, *middle_first(plan)]


def project_kernel(plan, lb, *refs):
    sources, weight, (keep, send, rows_ref) = refs[: plan.group], refs[plan.group], refs[plan.group + 1 :]
    me, column = lax.axis_index("pages"), lax.axis_index("mp")
    rows = plan.rows
    holders = plan.group // 2
    for i, k in enumerate(sources_of(plan, lb)):
        device = me ^ k ^ (lb * plan.cross)
        place = ((device // holders % 2) ^ (column % 2)) * holders + device % holders
        rows_ref[pl.ds(pl.multiple_of(place * rows, rows), rows), :] = sources[i][...]
    product = jnp.dot(rows_ref[...], weight[...], preferred_element_type=F32)
    part = holders * rows
    keep[...] = product[:part]
    send[...] = product[part:].astype(BF16)


def project(plan, lb, sources, weight):
    columns = weight.shape[1]
    part = plan.page // 2
    return pl.pallas_call(
        functools.partial(project_kernel, plan, lb),
        out_shape=(jax.ShapeDtypeStruct((part, columns), F32), jax.ShapeDtypeStruct((part, columns), BF16)),
        in_specs=[in_vmem()] * (plan.group + 1),
        out_specs=(in_vmem(), in_vmem()),
        scratch_shapes=[VMEM((plan.page, weight.shape[0]), BF16)],
        compiler_params=params(24),
    )(*(sources[k] for k in sources_of(plan, lb)), weight)


def swap(x, axis, distance):
    n = lax.axis_size(axis)
    return lax.ppermute(x, axis, [(i, i ^ distance) for i in range(n)])


def others(plan):
    return range(1, plan.group)


def middle_first(plan):
    return [*range(plan.group // 2, plan.group), *range(1, plan.group // 2)]


def spread(x, plan):
    return {0: x} | {k: swap(x, "pages", k) for k in others(plan)}


def by_halves(plan, heads, queries, weight, pages):
    far = swap(queries, "pages", plan.cross)
    near = []
    for lb, rows in enumerate((queries, far)):
        chunks = spread(rows, plan)
        outs = attend(plan, heads, lb, pages, [chunks[k] for k in range(plan.group)])
        near.append(merge(heads, outs[0], *(swap(outs[k], "pages", k) for k in others(plan))))
    across = [swap(x, "pages", plan.cross) for x in near]
    sums = [None, None]
    for lb in (1, 0):
        rows = finish(heads, near[lb], across[1 - lb])
        keep, send = project(plan, lb, spread(rows, plan), weight)
        sums[lb] = keep + swap(send, "mp", 1).astype(F32)
    stays = plan.block(lax.axis_index("pages"), 0) == lax.axis_index("mp") // 2
    mine = jnp.where(stays, sums[0], sums[1])
    away = jnp.where(stays, sums[1], sums[0]).astype(BF16)
    return (mine + swap(away, "mp", 2).astype(F32)).astype(BF16)


def by_gathers(plan, heads, queries, weight, pages):
    width = queries.shape[1]
    size = width // heads
    gathered = lax.all_gather(queries, "pages", axis=0, tiled=True)
    rows = gathered.shape[0]
    outs = [
        attend(plan, heads, lb, pages, [gathered[lb * plan.page : (lb + 1) * plan.page]])[0]
        for lb in range(plan.blocks)
    ]
    out = jnp.concatenate(outs, axis=0)
    packed = out[:, width : width + 3 * heads].astype(F32)
    lse = packed[:, :heads] + packed[:, heads : 2 * heads] + packed[:, 2 * heads :]
    every = lax.all_gather(lse, "pages")
    top = jnp.max(every, axis=0)
    share = jnp.exp2(lse - top) / jnp.sum(jnp.exp2(every - top), axis=0)
    part = (out[:, :width].reshape(rows, heads, size).astype(F32) * share[..., None]).reshape(1, rows, width)
    received = lax.all_to_all(part.astype(BF16), "pages", split_axis=1, concat_axis=0, tiled=True)
    mixed = jnp.sum(received, axis=0, dtype=F32).astype(BF16)
    terms = jnp.dot(lax.all_gather(mixed, "pages", axis=0, tiled=True), weight, preferred_element_type=F32)
    return lax.psum_scatter(terms, "mp", scatter_dimension=0, tiled=True).astype(BF16)


def per_device(queries, cached_keys, cached_values, out_weight, select, page_table, block_page):
    n, ways = lax.axis_size("pages"), lax.axis_size("mp")
    plan = Plan(n, ways, queries.shape[0], select.shape[0], cached_keys.shape[1])
    heads = queries.shape[1] // cached_keys.shape[3]
    pages = fetch(plan, select, page_table, block_page, cached_keys, cached_values)
    way = by_halves if plan.halves else by_gathers
    return way(plan, heads, queries, out_weight, pages)


def solution(mesh):
    placed = (
        P("pages", "mp"),
        P("pages", None, "mp", None),
        P("pages", None, "mp", None),
        P("mp", "pages"),
        P(),
        P(),
        P(),
    )
    return jax.shard_map(
        per_device, mesh=mesh, in_specs=placed, out_specs=P("mp", "pages"), check_vma=False
    )
```

```python
import functools
import math

import jax
import jax.numpy as jnp
from jax import lax
from jax.experimental import pallas as pl
from jax.experimental.pallas import tpu as pltpu
from jax.sharding import PartitionSpec as P

PICKED_PAGES = 6
FLOOR = -1e30
LANES = 128
HEADS_PER_TILE = 2

VMEM = pltpu.VMEM
SMEM = pltpu.SMEM
BF16 = jnp.bfloat16
F32 = jnp.float32


def in_vmem():
    return pl.BlockSpec(memory_space=VMEM)


def in_smem():
    return pl.BlockSpec(memory_space=SMEM)


def params(mib):
    return pltpu.CompilerParams(vmem_limit_bytes=mib * 2**20)


class Plan:
    def __init__(self, n, ways, rows, blocks, page):
        self.n, self.rows, self.blocks, self.page = n, rows, blocks, page
        self.group = n // blocks
        self.halves = blocks == 2 and n == 8 and ways == 4 and rows * self.group == page
        self.cross = n * 3 // 4
        self.chunks = self.group if self.halves else 1

    def block(self, me, lb):
        return (me // self.group) ^ lb if self.halves else lb

    def offsets(self, me, lb, shape):
        row = lax.broadcasted_iota(jnp.int32, shape, 0) % self.page
        if not self.halves:
            return row
        mine = (me ^ (lb * self.cross)) % self.group
        return ((row // self.rows) ^ mine) * self.rows + row % self.rows


def fetch_kernel(plan, pages_dev, select_hbm, table_hbm, stands_hbm, keys, values, k_out, v_out, info, select, table, stands, rows, k_buf, v_buf, sems, int_sems):
    me = lax.axis_index("pages")
    blocks, heads = k_out.shape[:2]
    span = k_buf.shape[1]
    page = span // heads
    picked = k_out.shape[2] // page
    low = me * pages_dev
    loads = [
        pltpu.make_async_copy(a, b, int_sems.at[i])
        for i, (a, b) in enumerate(((select_hbm, select), (table_hbm, table), (stands_hbm, stands)))
    ]
    whole = [
        pltpu.make_async_copy(a, b, sems.at[i]) for i, (a, b) in enumerate(((keys, k_buf), (values, v_buf)))
    ]
    for load in loads + whole:
        load.start()
    row = lax.broadcasted_iota(jnp.int32, (span, span), 0)
    column = lax.broadcasted_iota(jnp.int32, (span, span), 1)
    apart = (column == (row % page) * heads + row // page).astype(F32).astype(BF16)
    for load in loads:
        load.wait()
    for lb in range(blocks):
        block = plan.block(me, lb)
        stand = stands[block]
        info[lb, 1] = plan.n * pages_dev
        info[lb, 2] = stand
        others = jnp.int32(0)
        count = jnp.int32(0)
        for i in range(select.shape[1]):
            logical = select[block, i]
            local = table[logical] - low
            mine = (local >= 0) & (local < pages_dev)
            own = logical == stand
            slot = jnp.where(own, 0, jnp.maximum(picked - 1 - others, 0))
            slot = jnp.where(mine, slot, picked)
            rows[lb, slot] = local
            rows[blocks + lb, slot] = logical
            one = mine.astype(jnp.int32)
            others = others + jnp.where(own, 0, one)
            count = count + one
        info[lb, 0] = count
        info[lb, 1] = rows[blocks + lb, 0]

    for load in whole:
        load.wait()
    for lb in range(blocks):

        @pl.when(info[lb, 0] > 0)
        def _(lb=lb):
            for g in range(heads):
                v_out[lb, g, :, LANES:] = jnp.ones((picked * page, LANES), BF16)
            for slot in range(picked):
                local = jnp.clip(rows[lb, slot], 0, pages_dev - 1)
                both = jnp.concatenate([k_buf[local], v_buf[local]], axis=1)
                split = jnp.dot(apart, both, preferred_element_type=F32).astype(BF16)
                for g in range(heads):
                    here = slice(slot * page, (slot + 1) * page)
                    k_out[lb, g, here, :] = split[g * page : (g + 1) * page, :LANES]
                    v_out[lb, g, here, :LANES] = split[g * page : (g + 1) * page, LANES:]


def fetch(plan, select, table, stands, keys, values):
    pages_dev, page, heads, size = keys.shape
    blocks, picked = select.shape[0], PICKED_PAGES
    span = page * heads
    return pl.pallas_call(
        functools.partial(fetch_kernel, plan, pages_dev),
        out_shape=(
            jax.ShapeDtypeStruct((blocks, heads, picked * page, size), BF16),
            jax.ShapeDtypeStruct((blocks, heads, picked * page, size + LANES), BF16),
            jax.ShapeDtypeStruct((blocks, 3), jnp.int32),
        ),
        in_specs=[pl.BlockSpec(memory_space=pltpu.HBM)] * 5,
        out_specs=(in_vmem(), in_vmem(), in_smem()),
        scratch_shapes=[
            SMEM(select.shape, jnp.int32),
            SMEM(table.shape, jnp.int32),
            SMEM(stands.shape, jnp.int32),
            SMEM((2 * blocks, picked + 1), jnp.int32),
            VMEM((pages_dev, span, size), BF16),
            VMEM((pages_dev, span, size), BF16),
            pltpu.SemaphoreType.DMA((2,)),
            pltpu.SemaphoreType.DMA((3,)),
        ],
        compiler_params=params(16),
        cost_estimate=pl.CostEstimate(flops=2 * 10**9, bytes_accessed=8 * 2**20, transcendentals=0),
    )(*(pltpu.with_memory_space_constraint(x, pltpu.HBM) for x in (select, table, stands, keys.reshape(pages_dev, span, size), values.reshape(pages_dev, span, size))))


def pack_stats(lse, heads):
    lane = lax.broadcasted_iota(jnp.int32, lse.shape, 1)
    high = lse.astype(BF16).astype(F32)
    rest = lse - high
    middle = rest.astype(BF16).astype(F32)
    low = rest - middle
    packed = jnp.where(lane < heads, high, 0.0)
    packed = packed + jnp.where((lane >= heads) & (lane < 2 * heads), pltpu.roll(middle, heads, 1), 0.0)
    packed = packed + jnp.where((lane >= 2 * heads) & (lane < 3 * heads), pltpu.roll(low, 2 * heads, 1), 0.0)
    return packed.astype(BF16)


def unpack_stats(packed, heads):
    wide = packed.astype(F32)
    return wide + pltpu.roll(wide, LANES - heads, 1) + pltpu.roll(wide, LANES - 2 * heads, 1)


def as_sent(chunks):
    return [*range(chunks // 2, chunks), *range(1, chunks // 2), 0] if chunks > 1 else [0]


def attend_kernel(plan, heads, lb, info, *refs):
    me = lax.axis_index("pages")
    chunks, page = plan.chunks, plan.page
    sent, (k_ref, v_ref), outs = refs[:chunks], refs[chunks : chunks + 2], refs[chunks + 2 :]
    queries = [sent[i] for i in sorted(range(chunks), key=as_sent(chunks).__getitem__)]
    kv_heads, size = k_ref.shape[1], k_ref.shape[3]
    repeat = heads // kv_heads
    width = heads * size
    part = page // chunks
    tile = math.gcd(repeat, HEADS_PER_TILE)
    scale = size**-0.5 * math.log2(math.e)
    lane = lax.broadcasted_iota(jnp.int32, (page, LANES), 1)

    @pl.when(info[lb, 0] > 0)
    def _():
        shape = (tile * page, page)
        key_pos = info[lb, 1] * page + lax.broadcasted_iota(jnp.int32, shape, 1)
        query_pos = info[lb, 2] * page + plan.offsets(me, lb, shape)
        allowed = key_pos <= query_pos
        stats = jnp.zeros((page, LANES), F32)
        def product(first):
            q = jnp.concatenate(
                [m[:, h * size : (h + 1) * size] for h in range(first, first + tile) for m in queries], axis=0
            )
            return lax.dot_general(q, k_ref[lb, first // repeat], (((1,), (1,)), ((), ())), preferred_element_type=F32)

        ahead = product(0)
        for first in range(0, heads, tile):
            scores = scale * ahead
            if first + tile < heads:
                ahead = product(first + tile)
            scores = jnp.concatenate([jnp.where(allowed, scores[:, :page], FLOOR), scores[:, page:]], axis=1)
            peak = jnp.max(scores, axis=1, keepdims=True)
            weights = jnp.exp2(scores - peak).astype(BF16)
            both = jnp.dot(weights, v_ref[lb, first // repeat], preferred_element_type=F32)
            total = both[:, size:]
            out = (both[:, :size] / total).astype(BF16)
            lse = peak + jnp.log2(total)
            for i in range(tile):
                h = first + i
                stats = jnp.where(lane == h, lse[i * page : (i + 1) * page], stats)
                for c in range(chunks):
                    outs[c][:, h * size : (h + 1) * size] = out[i * page + c * part : i * page + (c + 1) * part]
        packed = pack_stats(stats, heads)
        for c in range(chunks):
            outs[c][:, width:] = packed[c * part : (c + 1) * part]

    @pl.when(info[lb, 0] == 0)
    def _():
        for c in range(chunks):
            outs[c][:, :width] = jnp.zeros((part, width), BF16)
            outs[c][:, width:] = pack_stats(jnp.full((part, LANES), FLOOR, F32), heads)


def attend(plan, heads, lb, pages, queries):
    keys, values, info = pages
    part = plan.page // plan.chunks
    shape = jax.ShapeDtypeStruct((part, queries[0].shape[1] + LANES), BF16)
    return pl.pallas_call(
        functools.partial(attend_kernel, plan, heads, lb),
        out_shape=(shape,) * plan.chunks,
        in_specs=[in_smem()] + [in_vmem()] * (len(queries) + 2),
        out_specs=(in_vmem(),) * plan.chunks,
        compiler_params=params(32),
        cost_estimate=pl.CostEstimate(flops=2 * 10**9, bytes_accessed=4 * 2**20, transcendentals=10**6),
    )(info, *(queries[k] for k in as_sent(len(queries))), keys, values)


def merged(parts, stats):
    top = functools.reduce(jnp.maximum, stats)
    shares = [jnp.exp2(s - top) for s in stats]
    total = functools.reduce(jnp.add, shares)
    shares = [s / total for s in shares]

    def head(h):
        return functools.reduce(
            jnp.add, [p(h).astype(F32) * s[:, h : h + 1] for p, s in zip(parts, shares, strict=True)]
        )

    return head, top + jnp.log2(total)


def merge_kernel(heads, *refs):
    sources, out = refs[:-1], refs[-1]
    width = out.shape[1] - LANES
    size = width // heads
    head, lse = merged([heads_of(r, size) for r in sources], [unpack_stats(r[:, width:], heads) for r in sources])
    for h in range(heads):
        out[:, h * size : (h + 1) * size] = head(h).astype(BF16)
    out[:, width:] = pack_stats(lse, heads)


def merge(heads, *sources):
    return pl.pallas_call(
        functools.partial(merge_kernel, heads),
        out_shape=jax.ShapeDtypeStruct(sources[0].shape, BF16),
        in_specs=[in_vmem()] * len(sources),
        out_specs=in_vmem(),
        compiler_params=params(8),
    )(*sources)


def heads_of(ref, size):
    return lambda h: ref[:, h * size : (h + 1) * size]


def finish_kernel(heads, near, far, out):
    width = out.shape[1]
    size = width // heads
    head, _ = merged([heads_of(r, size) for r in (near, far)], [unpack_stats(r[:, width:], heads) for r in (near, far)])
    for h in range(heads):
        out[:, h * size : (h + 1) * size] = head(h).astype(BF16)


def finish(heads, near, far):
    return pl.pallas_call(
        functools.partial(finish_kernel, heads),
        out_shape=jax.ShapeDtypeStruct((near.shape[0], near.shape[1] - LANES), BF16),
        in_specs=[in_vmem()] * 2,
        out_specs=in_vmem(),
        compiler_params=params(8),
    )(near, far)


def project_kernel(plan, lb, *refs):
    sources, weight, (keep, send, rows_ref) = refs[: plan.group], refs[plan.group], refs[plan.group + 1 :]
    me, column = lax.axis_index("pages"), lax.axis_index("mp")
    rows = plan.rows
    holders = plan.group // 2
    for k in range(plan.group):
        device = me ^ k ^ (lb * plan.cross)
        place = ((device // holders % 2) ^ (column % 2)) * holders + device % holders
        rows_ref[pl.ds(pl.multiple_of(place * rows, rows), rows), :] = sources[k][...]
    product = jnp.dot(rows_ref[...], weight[...], preferred_element_type=F32)
    part = holders * rows
    keep[...] = product[:part]
    send[...] = product[part:].astype(BF16)


def project(plan, lb, sources, weight):
    columns = weight.shape[1]
    part = plan.page // 2
    return pl.pallas_call(
        functools.partial(project_kernel, plan, lb),
        out_shape=(jax.ShapeDtypeStruct((part, columns), F32), jax.ShapeDtypeStruct((part, columns), BF16)),
        in_specs=[in_vmem()] * (plan.group + 1),
        out_specs=(in_vmem(), in_vmem()),
        scratch_shapes=[VMEM((plan.page, weight.shape[0]), BF16)],
        compiler_params=params(24),
    )(*(sources[k] for k in range(plan.group)), weight)


def swap(x, axis, distance):
    n = lax.axis_size(axis)
    return lax.ppermute(x, axis, [(i, i ^ distance) for i in range(n)])


def others(plan):
    return range(1, plan.group)


def spread(x, plan):
    return {0: x} | {k: swap(x, "pages", k) for k in others(plan)}


def by_halves(plan, heads, queries, weight, pages):
    far = swap(queries, "pages", plan.cross)
    near = []
    for lb, rows in enumerate((queries, far)):
        chunks = spread(rows, plan)
        outs = attend(plan, heads, lb, pages, [chunks[k] for k in range(plan.group)])
        near.append(merge(heads, outs[0], *(swap(outs[k], "pages", k) for k in others(plan))))
    across = [swap(x, "pages", plan.cross) for x in near]
    sums = [None, None]
    for lb in (1, 0):
        rows = finish(heads, near[lb], across[1 - lb])
        keep, send = project(plan, lb, spread(rows, plan), weight)
        sums[lb] = keep + swap(send, "mp", 1).astype(F32)
    stays = plan.block(lax.axis_index("pages"), 0) == lax.axis_index("mp") // 2
    mine = jnp.where(stays, sums[0], sums[1])
    away = jnp.where(stays, sums[1], sums[0]).astype(BF16)
    return (mine + swap(away, "mp", 2).astype(F32)).astype(BF16)


def by_gathers(plan, heads, queries, weight, pages):
    width = queries.shape[1]
    size = width // heads
    gathered = lax.all_gather(queries, "pages", axis=0, tiled=True)
    rows = gathered.shape[0]
    outs = [
        attend(plan, heads, lb, pages, [gathered[lb * plan.page : (lb + 1) * plan.page]])[0]
        for lb in range(plan.blocks)
    ]
    out = jnp.concatenate(outs, axis=0)
    packed = out[:, width : width + 3 * heads].astype(F32)
    lse = packed[:, :heads] + packed[:, heads : 2 * heads] + packed[:, 2 * heads :]
    every = lax.all_gather(lse, "pages")
    top = jnp.max(every, axis=0)
    share = jnp.exp2(lse - top) / jnp.sum(jnp.exp2(every - top), axis=0)
    part = (out[:, :width].reshape(rows, heads, size).astype(F32) * share[..., None]).reshape(1, rows, width)
    received = lax.all_to_all(part.astype(BF16), "pages", split_axis=1, concat_axis=0, tiled=True)
    mixed = jnp.sum(received, axis=0, dtype=F32).astype(BF16)
    terms = jnp.dot(lax.all_gather(mixed, "pages", axis=0, tiled=True), weight, preferred_element_type=F32)
    return lax.psum_scatter(terms, "mp", scatter_dimension=0, tiled=True).astype(BF16)


def per_device(queries, cached_keys, cached_values, out_weight, select, page_table, block_page):
    n, ways = lax.axis_size("pages"), lax.axis_size("mp")
    plan = Plan(n, ways, queries.shape[0], select.shape[0], cached_keys.shape[1])
    heads = queries.shape[1] // cached_keys.shape[3]
    pages = fetch(plan, select, page_table, block_page, cached_keys, cached_values)
    way = by_halves if plan.halves else by_gathers
    return way(plan, heads, queries, out_weight, pages)


def solution(mesh):
    placed = (
        P("pages", "mp"),
        P("pages", None, "mp", None),
        P("pages", None, "mp", None),
        P("mp", "pages"),
        P(),
        P(),
        P(),
    )
    return jax.shard_map(
        per_device, mesh=mesh, in_specs=placed, out_specs=P("mp", "pages"), check_vma=False
    )
```

```python
import functools
import math

import jax
import jax.numpy as jnp
from jax import lax
from jax.experimental import pallas as pl
from jax.experimental.pallas import tpu as pltpu
from jax.sharding import PartitionSpec as P

PICKED_PAGES = 6
FLOOR = -1e30
LANES = 128
HEADS_PER_TILE = 2

VMEM = pltpu.VMEM
SMEM = pltpu.SMEM
BF16 = jnp.bfloat16
F32 = jnp.float32


def in_vmem():
    return pl.BlockSpec(memory_space=VMEM)


def in_smem():
    return pl.BlockSpec(memory_space=SMEM)


def params(mib):
    return pltpu.CompilerParams(vmem_limit_bytes=mib * 2**20)


class Plan:
    def __init__(self, n, ways, rows, blocks, page):
        self.n, self.rows, self.blocks, self.page = n, rows, blocks, page
        self.group = n // blocks
        self.halves = blocks == 2 and n == 8 and ways == 4 and rows * self.group == page
        self.cross = n * 3 // 4
        self.chunks = self.group if self.halves else 1

    def block(self, me, lb):
        return (me // self.group) ^ lb if self.halves else lb

    def offsets(self, me, lb, shape):
        row = lax.broadcasted_iota(jnp.int32, shape, 0) % self.page
        if not self.halves:
            return row
        mine = (me ^ (lb * self.cross)) % self.group
        return ((row // self.rows) ^ mine) * self.rows + row % self.rows


def fetch_kernel(plan, pages_dev, select_hbm, table_hbm, stands_hbm, keys, values, k_out, v_out, info, select, table, stands, rows, k_buf, v_buf, sems, int_sems):
    me = lax.axis_index("pages")
    blocks, heads = k_out.shape[:2]
    span = k_buf.shape[1]
    page = span // heads
    picked = k_out.shape[2] // page
    low = me * pages_dev
    loads = [
        pltpu.make_async_copy(a, b, int_sems.at[i])
        for i, (a, b) in enumerate(((select_hbm, select), (table_hbm, table), (stands_hbm, stands)))
    ]
    whole = [
        pltpu.make_async_copy(a, b, sems.at[i]) for i, (a, b) in enumerate(((keys, k_buf), (values, v_buf)))
    ]
    for load in loads + whole:
        load.start()
    row = lax.broadcasted_iota(jnp.int32, (span, span), 0)
    column = lax.broadcasted_iota(jnp.int32, (span, span), 1)
    apart = (column == (row % page) * heads + row // page).astype(F32).astype(BF16)
    for load in loads:
        load.wait()
    for lb in range(blocks):
        block = plan.block(me, lb)
        stand = stands[block]
        info[lb, 1] = plan.n * pages_dev
        info[lb, 2] = stand
        others = jnp.int32(0)
        count = jnp.int32(0)
        for i in range(select.shape[1]):
            logical = select[block, i]
            local = table[logical] - low
            mine = (local >= 0) & (local < pages_dev)
            own = logical == stand
            slot = jnp.where(own, 0, jnp.maximum(picked - 1 - others, 0))
            slot = jnp.where(mine, slot, picked)
            rows[lb, slot] = local
            rows[blocks + lb, slot] = logical
            one = mine.astype(jnp.int32)
            others = others + jnp.where(own, 0, one)
            count = count + one
        info[lb, 0] = count
        info[lb, 1] = rows[blocks + lb, 0]

    for load in whole:
        load.wait()
    for lb in range(blocks):

        @pl.when(info[lb, 0] > 0)
        def _(lb=lb):
            for g in range(heads):
                v_out[lb, g, :, LANES:] = jnp.ones((picked * page, LANES), BF16)
            for slot in range(picked):
                local = jnp.clip(rows[lb, slot], 0, pages_dev - 1)
                both = jnp.concatenate([k_buf[local], v_buf[local]], axis=1)
                split = jnp.dot(apart, both, preferred_element_type=F32).astype(BF16)
                for g in range(heads):
                    here = slice(slot * page, (slot + 1) * page)
                    k_out[lb, g, here, :] = split[g * page : (g + 1) * page, :LANES]
                    v_out[lb, g, here, :LANES] = split[g * page : (g + 1) * page, LANES:]


def fetch(plan, select, table, stands, keys, values):
    pages_dev, page, heads, size = keys.shape
    blocks, picked = select.shape[0], PICKED_PAGES
    span = page * heads
    return pl.pallas_call(
        functools.partial(fetch_kernel, plan, pages_dev),
        out_shape=(
            jax.ShapeDtypeStruct((blocks, heads, picked * page, size), BF16),
            jax.ShapeDtypeStruct((blocks, heads, picked * page, size + LANES), BF16),
            jax.ShapeDtypeStruct((blocks, 3), jnp.int32),
        ),
        in_specs=[pl.BlockSpec(memory_space=pltpu.HBM)] * 5,
        out_specs=(in_vmem(), in_vmem(), in_smem()),
        scratch_shapes=[
            SMEM(select.shape, jnp.int32),
            SMEM(table.shape, jnp.int32),
            SMEM(stands.shape, jnp.int32),
            SMEM((2 * blocks, picked + 1), jnp.int32),
            VMEM((pages_dev, span, size), BF16),
            VMEM((pages_dev, span, size), BF16),
            pltpu.SemaphoreType.DMA((2,)),
            pltpu.SemaphoreType.DMA((3,)),
        ],
        compiler_params=params(16),
        cost_estimate=pl.CostEstimate(flops=2 * 10**9, bytes_accessed=8 * 2**20, transcendentals=0),
    )(*(pltpu.with_memory_space_constraint(x, pltpu.HBM) for x in (select, table, stands, keys.reshape(pages_dev, span, size), values.reshape(pages_dev, span, size))))


def pack_stats(lse, heads):
    lane = lax.broadcasted_iota(jnp.int32, lse.shape, 1)
    high = lse.astype(BF16).astype(F32)
    rest = lse - high
    middle = rest.astype(BF16).astype(F32)
    low = rest - middle
    packed = jnp.where(lane < heads, high, 0.0)
    packed = packed + jnp.where((lane >= heads) & (lane < 2 * heads), pltpu.roll(middle, heads, 1), 0.0)
    packed = packed + jnp.where((lane >= 2 * heads) & (lane < 3 * heads), pltpu.roll(low, 2 * heads, 1), 0.0)
    return packed.astype(BF16)


def unpack_stats(packed, heads):
    wide = packed.astype(F32)
    return wide + pltpu.roll(wide, LANES - heads, 1) + pltpu.roll(wide, LANES - 2 * heads, 1)


def attend_kernel(plan, heads, lb, info, *refs):
    me = lax.axis_index("pages")
    chunks, page = plan.chunks, plan.page
    queries, (k_ref, v_ref), outs = refs[:chunks][::-1], refs[chunks : chunks + 2], refs[chunks + 2 :]
    kv_heads, size = k_ref.shape[1], k_ref.shape[3]
    repeat = heads // kv_heads
    width = heads * size
    part = page // chunks
    tile = math.gcd(repeat, HEADS_PER_TILE)
    scale = size**-0.5 * math.log2(math.e)
    lane = lax.broadcasted_iota(jnp.int32, (page, LANES), 1)

    @pl.when(info[lb, 0] > 0)
    def _():
        shape = (tile * page, page)
        key_pos = info[lb, 1] * page + lax.broadcasted_iota(jnp.int32, shape, 1)
        query_pos = info[lb, 2] * page + plan.offsets(me, lb, shape)
        allowed = key_pos <= query_pos
        stats = jnp.zeros((page, LANES), F32)
        def product(first):
            q = jnp.concatenate(
                [m[:, h * size : (h + 1) * size] for h in range(first, first + tile) for m in queries], axis=0
            )
            return lax.dot_general(q, k_ref[lb, first // repeat], (((1,), (1,)), ((), ())), preferred_element_type=F32)

        ahead = product(0)
        for first in range(0, heads, tile):
            scores = scale * ahead
            if first + tile < heads:
                ahead = product(first + tile)
            scores = jnp.concatenate([jnp.where(allowed, scores[:, :page], FLOOR), scores[:, page:]], axis=1)
            peak = jnp.max(scores, axis=1, keepdims=True)
            weights = jnp.exp2(scores - peak).astype(BF16)
            both = jnp.dot(weights, v_ref[lb, first // repeat], preferred_element_type=F32)
            total = both[:, size:]
            out = (both[:, :size] / total).astype(BF16)
            lse = peak + jnp.log2(total)
            for i in range(tile):
                h = first + i
                stats = jnp.where(lane == h, lse[i * page : (i + 1) * page], stats)
                for c in range(chunks):
                    outs[c][:, h * size : (h + 1) * size] = out[i * page + c * part : i * page + (c + 1) * part]
        packed = pack_stats(stats, heads)
        for c in range(chunks):
            outs[c][:, width:] = packed[c * part : (c + 1) * part]

    @pl.when(info[lb, 0] == 0)
    def _():
        for c in range(chunks):
            outs[c][:, :width] = jnp.zeros((part, width), BF16)
            outs[c][:, width:] = pack_stats(jnp.full((part, LANES), FLOOR, F32), heads)


def attend(plan, heads, lb, pages, queries):
    keys, values, info = pages
    part = plan.page // plan.chunks
    shape = jax.ShapeDtypeStruct((part, queries[0].shape[1] + LANES), BF16)
    return pl.pallas_call(
        functools.partial(attend_kernel, plan, heads, lb),
        out_shape=(shape,) * plan.chunks,
        in_specs=[in_smem()] + [in_vmem()] * (len(queries) + 2),
        out_specs=(in_vmem(),) * plan.chunks,
        compiler_params=params(32),
        cost_estimate=pl.CostEstimate(flops=2 * 10**9, bytes_accessed=4 * 2**20, transcendentals=10**6),
    )(info, *queries[::-1], keys, values)


def merged(parts, stats):
    top = functools.reduce(jnp.maximum, stats)
    shares = [jnp.exp2(s - top) for s in stats]
    total = functools.reduce(jnp.add, shares)
    shares = [s / total for s in shares]

    def head(h):
        return functools.reduce(
            jnp.add, [p(h).astype(F32) * s[:, h : h + 1] for p, s in zip(parts, shares, strict=True)]
        )

    return head, top + jnp.log2(total)


def merge_kernel(heads, *refs):
    sources, out = refs[:-1], refs[-1]
    width = out.shape[1] - LANES
    size = width // heads
    head, lse = merged([heads_of(r, size) for r in sources], [unpack_stats(r[:, width:], heads) for r in sources])
    for h in range(heads):
        out[:, h * size : (h + 1) * size] = head(h).astype(BF16)
    out[:, width:] = pack_stats(lse, heads)


def merge(heads, *sources):
    return pl.pallas_call(
        functools.partial(merge_kernel, heads),
        out_shape=jax.ShapeDtypeStruct(sources[0].shape, BF16),
        in_specs=[in_vmem()] * len(sources),
        out_specs=in_vmem(),
        compiler_params=params(8),
    )(*sources)


def heads_of(ref, size):
    return lambda h: ref[:, h * size : (h + 1) * size]


def finish_kernel(heads, near, far, out):
    width = out.shape[1]
    size = width // heads
    head, _ = merged([heads_of(r, size) for r in (near, far)], [unpack_stats(r[:, width:], heads) for r in (near, far)])
    for h in range(heads):
        out[:, h * size : (h + 1) * size] = head(h).astype(BF16)


def finish(heads, near, far):
    return pl.pallas_call(
        functools.partial(finish_kernel, heads),
        out_shape=jax.ShapeDtypeStruct((near.shape[0], near.shape[1] - LANES), BF16),
        in_specs=[in_vmem()] * 2,
        out_specs=in_vmem(),
        compiler_params=params(8),
    )(near, far)


def project_kernel(plan, lb, *refs):
    sources, weight, (keep, send, rows_ref) = refs[: plan.group], refs[plan.group], refs[plan.group + 1 :]
    me, column = lax.axis_index("pages"), lax.axis_index("mp")
    rows = plan.rows
    holders = plan.group // 2
    for k in range(plan.group):
        device = me ^ k ^ (lb * plan.cross)
        place = ((device // holders % 2) ^ (column % 2)) * holders + device % holders
        rows_ref[pl.ds(pl.multiple_of(place * rows, rows), rows), :] = sources[k][...]
    product = jnp.dot(rows_ref[...], weight[...], preferred_element_type=F32)
    part = holders * rows
    keep[...] = product[:part]
    send[...] = product[part:].astype(BF16)


def project(plan, lb, sources, weight):
    columns = weight.shape[1]
    part = plan.page // 2
    return pl.pallas_call(
        functools.partial(project_kernel, plan, lb),
        out_shape=(jax.ShapeDtypeStruct((part, columns), F32), jax.ShapeDtypeStruct((part, columns), BF16)),
        in_specs=[in_vmem()] * (plan.group + 1),
        out_specs=(in_vmem(), in_vmem()),
        scratch_shapes=[VMEM((plan.page, weight.shape[0]), BF16)],
        compiler_params=params(24),
    )(*(sources[k] for k in range(plan.group)), weight)


def swap(x, axis, distance):
    n = lax.axis_size(axis)
    return lax.ppermute(x, axis, [(i, i ^ distance) for i in range(n)])


def others(plan):
    return range(1, plan.group)


def spread(x, plan):
    return {0: x} | {k: swap(x, "pages", k) for k in others(plan)}


def by_halves(plan, heads, queries, weight, pages):
    far = swap(queries, "pages", plan.cross)
    near = []
    for lb, rows in enumerate((queries, far)):
        chunks = spread(rows, plan)
        outs = attend(plan, heads, lb, pages, [chunks[k] for k in range(plan.group)])
        order = [*range(plan.group // 2, plan.group), *range(1, plan.group // 2)] if lb else others(plan)
        near.append(merge(heads, outs[0], *(swap(outs[k], "pages", k) for k in order)))
    across = [swap(x, "pages", plan.cross) for x in near]
    sums = [None, None]
    for lb in (1, 0):
        rows = finish(heads, near[lb], across[1 - lb])
        keep, send = project(plan, lb, spread(rows, plan), weight)
        sums[lb] = keep + swap(send, "mp", 1).astype(F32)
    stays = plan.block(lax.axis_index("pages"), 0) == lax.axis_index("mp") // 2
    mine = jnp.where(stays, sums[0], sums[1])
    away = jnp.where(stays, sums[1], sums[0]).astype(BF16)
    return (mine + swap(away, "mp", 2).astype(F32)).astype(BF16)


def by_gathers(plan, heads, queries, weight, pages):
    width = queries.shape[1]
    size = width // heads
    gathered = lax.all_gather(queries, "pages", axis=0, tiled=True)
    rows = gathered.shape[0]
    outs = [
        attend(plan, heads, lb, pages, [gathered[lb * plan.page : (lb + 1) * plan.page]])[0]
        for lb in range(plan.blocks)
    ]
    out = jnp.concatenate(outs, axis=0)
    packed = out[:, width : width + 3 * heads].astype(F32)
    lse = packed[:, :heads] + packed[:, heads : 2 * heads] + packed[:, 2 * heads :]
    every = lax.all_gather(lse, "pages")
    top = jnp.max(every, axis=0)
    share = jnp.exp2(lse - top) / jnp.sum(jnp.exp2(every - top), axis=0)
    part = (out[:, :width].reshape(rows, heads, size).astype(F32) * share[..., None]).reshape(1, rows, width)
    received = lax.all_to_all(part.astype(BF16), "pages", split_axis=1, concat_axis=0, tiled=True)
    mixed = jnp.sum(received, axis=0, dtype=F32).astype(BF16)
    terms = jnp.dot(lax.all_gather(mixed, "pages", axis=0, tiled=True), weight, preferred_element_type=F32)
    return lax.psum_scatter(terms, "mp", scatter_dimension=0, tiled=True).astype(BF16)


def per_device(queries, cached_keys, cached_values, out_weight, select, page_table, block_page):
    n, ways = lax.axis_size("pages"), lax.axis_size("mp")
    plan = Plan(n, ways, queries.shape[0], select.shape[0], cached_keys.shape[1])
    heads = queries.shape[1] // cached_keys.shape[3]
    pages = fetch(plan, select, page_table, block_page, cached_keys, cached_values)
    way = by_halves if plan.halves else by_gathers
    return way(plan, heads, queries, out_weight, pages)


def solution(mesh):
    placed = (
        P("pages", "mp"),
        P("pages", None, "mp", None),
        P("pages", None, "mp", None),
        P("mp", "pages"),
        P(),
        P(),
        P(),
    )
    return jax.shard_map(
        per_device, mesh=mesh, in_specs=placed, out_specs=P("mp", "pages"), check_vma=False
    )
```
